32 devices in a mesh: grp: 2 (over core), dp: 16 (over z, y, x).
Axes of the slice: x: 2, y: 2, z: 4, core: 2. Of those that a mesh axis runs over, the one named last changes fastest.
Arguments:
- pixels: bfloat16 [512, 49, 768], P(('grp', 'dp')), may hold values from -20 to 20
- visible: int32 [512, 49], P(('grp', 'dp')), may hold values from 0 to 195, as said below
- scale_index: int32 [512], P(('grp', 'dp')), may hold values from 0 to 3
- cotangent: bfloat16 [2, 64, 16, 49, 512], P('grp', 'dp'), may hold values from -6 to 6
- pe_weight: float32 [768, 1024], P(None, ('grp', 'dp')), may hold values from -2 to 2
- pe_first: float32 [768, 1024], P(None, ('grp', 'dp')), may hold values from -0.00061035156 to 0.00061035156
- pe_second: float32 [768, 1024], P(None, ('grp', 'dp')), may hold values from 8.573906e-09 to 3.3972082e-08
- qkv_weight: float32 [1024, 3072], P(('grp', 'dp')), may hold values from -0.1875 to 0.1875
- qkv_first: float32 [1024, 3072], P(('grp', 'dp')), may hold values from -0.00036621094 to 0.00036621094
- qkv_second: float32 [1024, 3072], P(('grp', 'dp')), may hold values from 2.4387998e-09 to 9.66317e-09
- out_weight: float32 [1024, 1024], P(None, ('grp', 'dp')), may hold values from -0.5 to 0.5
- out_first: float32 [1024, 1024], P(None, ('grp', 'dp')), may hold values from -0.00036621094 to 0.00036621094
- out_second: float32 [1024, 1024], P(None, ('grp', 'dp')), may hold values from 2.4387998e-09 to 9.66317e-09
- up_weight: float32 [1024, 4096], P(('grp', 'dp')), may hold values from -0.1875 to 0.1875
- up_first: float32 [1024, 4096], P(('grp', 'dp')), may hold values from -0.00036621094 to 0.00036621094
- up_second: float32 [1024, 4096], P(('grp', 'dp')), may hold values from 2.4387998e-09 to 9.66317e-09
- down_weight: float32 [4096, 1024], P(None, ('grp', 'dp')), may hold values from -0.09375 to 0.09375
- down_first: float32 [4096, 1024], P(None, ('grp', 'dp')), may hold values from -0.00036621094 to 0.00036621094
- down_second: float32 [4096, 1024], P(None, ('grp', 'dp')), may hold values from 2.4387998e-09 to 9.66317e-09
- dec_weight: float32 [1024, 512], P(('grp', 'dp')), may hold values from -2 to 2
- dec_first: float32 [1024, 512], P(('grp', 'dp')), may hold values from -0.0008544922 to 0.0008544922
- dec_second: float32 [1024, 512], P(('grp', 'dp')), may hold values from 1.5242499e-08 to 6.039481e-08
- vectors: float32 [14848], P(('grp', 'dp')), may hold values from -4 to 4
- vec_first: float32 [14848], P(('grp', 'dp')), may hold values from -0.0012207031 to 0.0012207031
- vec_second: float32 [14848], P(('grp', 'dp')), may hold values from 3.4295624e-08 to 1.3588833e-07
Outputs:
- decoded: bfloat16 [2, 64, 16, 49, 512], P('grp', 'dp')
- pixel_grad: float32 [512, 49, 768], P(('grp', 'dp'))
- pe_first_new: float32 [768, 1024], P(None, ('grp', 'dp'))
- pe_second_new: float32 [768, 1024], P(None, ('grp', 'dp'))
- pe_new: float32 [768, 1024], P(None, ('grp', 'dp'))
- qkv_first_new: float32 [1024, 3072], P(('grp', 'dp'))
- qkv_second_new: float32 [1024, 3072], P(('grp', 'dp'))
- qkv_new: float32 [1024, 3072], P(('grp', 'dp'))
- out_first_new: float32 [1024, 1024], P(None, ('grp', 'dp'))
- out_second_new: float32 [1024, 1024], P(None, ('grp', 'dp'))
- out_new: float32 [1024, 1024], P(None, ('grp', 'dp'))
- up_first_new: float32 [1024, 4096], P(('grp', 'dp'))
- up_second_new: float32 [1024, 4096], P(('grp', 'dp'))
- up_new: float32 [1024, 4096], P(('grp', 'dp'))
- down_first_new: float32 [4096, 1024], P(None, ('grp', 'dp'))
- down_second_new: float32 [4096, 1024], P(None, ('grp', 'dp'))
- down_new: float32 [4096, 1024], P(None, ('grp', 'dp'))
- dec_first_new: float32 [1024, 512], P(('grp', 'dp'))
- dec_second_new: float32 [1024, 512], P(('grp', 'dp'))
- dec_new: float32 [1024, 512], P(('grp', 'dp'))
- vec_first_new: float32 [14848], P(('grp', 'dp'))
- vec_second_new: float32 [14848], P(('grp', 'dp'))
- vec_new: float32 [14848], P(('grp', 'dp'))
- grad_norm: float32 [], replicated
The draws below stay inside these ranges and needn't reach their ends.
Inputs may be any that keep to these rules, and one draw needn't show every extreme that they name: `visible`: each image names 49 distinct grid positions in increasing order.
All inputs are finite; a program needn't handle non-finite values.
Results may differ from the reference program's by a relative error of at most 0.013.
The reference program's roundings to bfloat16 on the way count: a program that leaves them out, or rounds other values in their place, can miss the bound.
Values may be sent and summed in bfloat16 or wider, within the bound.
No kernel may reach another device: no remote copies, remote signals or barrier semaphores. Data moves between devices by JAX's collectives and lax.ppermute only.
A program may use at most 320 MiB of HBM per device.

```python
import math
import jax
import jax.numpy as jnp
from jax import lax

D = 1024
FF = 4096
HEADS = 16
HDIM = 64
DDEC = 512
PATCH = 16
SIDE = 14
BANDS = 3
NSCALE = 4
STEP = 10
IMG_DEV = 16
PIX = 768
GRID = 196
VIS = 49
QUART = 49
VEC = 14848
PARAMS = 13908480
IMAGES = 512
N_GRP = 2
N_DP = 16


def ramp_up(length, start_value, end_value):
    return start_value + (end_value - start_value) * jnp.arange(length).astype(jnp.float32) / max(length - 1, 1)


def draw_pixels(key, part):
    key = jax.random.fold_in(key, 11)
    first_key = jax.random.fold_in(key, 0)
    third_key = jax.random.fold_in(key, 2)
    shape = (IMAGES, VIS, BANDS, PATCH * PATCH)
    band_scale = jax.random.uniform(third_key, (1, 1, BANDS, 1), minval=0.6, maxval=1.5)
    basic_draw = jnp.clip(jax.random.normal(first_key, shape), -5.5, 5.5)
    scales = ramp_up(IMAGES, 0.6, 1.8)
    values = basic_draw * band_scale * scales[:, None, None, None]
    return values.reshape(IMAGES, VIS, PIX).astype(jnp.bfloat16)


def draw_visible(key, part):
    key = jax.random.fold_in(key, 12)
    image_keys = jax.random.split(key, IMAGES)

    def choose_visible(single):
        return jnp.sort(jax.random.permutation(single, GRID)[:VIS]).astype(jnp.int32)
    return jax.vmap(choose_visible)(image_keys)


def draw_pe_weight(key, part):
    key = jax.random.fold_in(key, 13)
    basic_draw = jnp.clip(jax.random.normal(key, (PIX, D)), -5.0, 5.0)
    scales = ramp_up(D, 0.6, 1.4)
    return basic_draw * scales[None, :] / PIX ** 0.5


def draw_dec_weight(key, part):
    key = jax.random.fold_in(key, 14)
    basic_draw = jnp.clip(jax.random.normal(key, (D, DDEC)), -5.0, 5.0)
    scales = ramp_up(D, 0.6, 1.4)
    return basic_draw * scales[:, None] / D ** 0.5


def draw_vectors(key, part):
    key = jax.random.fold_in(key, 15)
    gain_key, bias_key, mask_key, up_key, dec_key = jax.random.split(key, 5)
    gain_ramp = ramp_up(D, 0.6, 1.4)
    jitter = jnp.clip(0.1 * jax.random.normal(gain_key, (2, D)), -0.3, 0.3)
    gains = gain_ramp[None, :] * (1.0 + jitter)
    biases = jnp.clip(0.3 * jax.random.normal(bias_key, (7, D)), -1.5, 1.5)
    mask_token = jnp.clip(jax.random.normal(mask_key, (D,)), -4.0, 4.0)
    up_bias = jnp.clip(0.3 * jax.random.normal(up_key, (FF,)), -1.5, 1.5)
    dec_bias = jnp.clip(0.3 * jax.random.normal(dec_key, (DDEC,)), -1.5, 1.5)
    return jnp.concatenate([gains[0], biases[0], gains[1], biases[1], biases[2], biases[3], biases[4], biases[5], biases[6], mask_token, up_bias, dec_bias])


def with_ends(values, key, least, largest):
    dims = values.shape
    index_at = [jax.random.randint(jax.random.fold_in(key, axis), (), 0, dims[axis]) for axis in range(len(dims))]
    values = values.at[tuple(index_at)].set(least)
    longest = dims.index(max(dims))
    index_at[longest] = (index_at[longest] + 1) % dims[longest]
    return values.at[tuple(index_at)].set(largest)


def shard_levels(key, dims, shards, smallest, largest):
    gain = 1.0
    for dim, shards_of in shards:
        draws = jax.random.uniform(jax.random.fold_in(jax.random.fold_in(key, 6), dim), (shards_of,), jnp.float32, smallest / len(shards), largest / len(shards))
        gain = gain * jnp.repeat(jnp.exp(draws), dims[dim] // shards_of).reshape((-1,) + (1,) * (len(dims) - 1 - dim))
    return gain


def bell_draw(key, extent, width, most, cuts=(), held_as=jnp.bfloat16):
    gain = shard_levels(key, extent, cuts, -0.22, 0.18) if cuts else 1.0
    values = jax.random.normal(key, extent, jnp.float32) * width * gain
    return jnp.minimum(jnp.maximum(values, -most), most).astype(held_as)


def setup_inputs(seed: int = 0) -> dict:
    key_of = jax.random.split(jax.random.key(seed), 26)
    return {
        "pixels": draw_pixels(jax.random.fold_in(key_of[25], 71), 0),
        "visible": draw_visible(jax.random.fold_in(key_of[25], 71), 0),
        "scale_index": with_ends(jax.random.randint(key_of[2], (IMAGES,), 0, NSCALE), jax.random.fold_in(key_of[2], 1), 0, NSCALE - 1).astype(jnp.int32),
        "cotangent": bell_draw(key_of[3], (N_GRP, 4 * IMG_DEV, N_DP, QUART, DDEC), 1.0, 6.0, ((0, 2), (1, 16))),
        "pe_weight": draw_pe_weight(jax.random.fold_in(key_of[25], 71), 0),
        "pe_first": bell_draw(key_of[5], (PIX, D), (0.11 * 1.5 / PARAMS ** 0.5), 0.00061035156, ((1, 32),), jnp.float32),
        "pe_second": jnp.clip(jnp.exp(math.log(3.397208203637092e-08) - 1.3768157 * jax.random.uniform(key_of[6], (PIX, D), jnp.float32) ** shard_levels(key_of[6], (PIX, D), ((1, 32),), -0.2, 0.2)), 8.573906029596401e-09, 3.397208203637092e-08),
        "qkv_weight": bell_draw(key_of[7], (D, 3 * D), D ** -0.5, 0.1875, ((0, 32),), jnp.float32),
        "qkv_first": bell_draw(key_of[8], (D, 3 * D), (0.11 * 0.8 / PARAMS ** 0.5), 0.00036621094, ((0, 32),), jnp.float32),
        "qkv_second": jnp.clip(jnp.exp(math.log(9.663169819873474e-09) - 1.3768157 * jax.random.uniform(key_of[9], (D, 3 * D), jnp.float32) ** shard_levels(key_of[9], (D, 3 * D), ((0, 32),), -0.2, 0.2)), 2.4387998287522805e-09, 9.663169819873474e-09),
        "out_weight": bell_draw(key_of[10], (D, D), (2 * D // SIDE) ** -0.5, 0.5, ((1, 32),), jnp.float32),
        "out_first": bell_draw(key_of[11], (D, D), (0.11 * 0.8 / PARAMS ** 0.5), 0.00036621094, ((1, 32),), jnp.float32),
        "out_second": jnp.clip(jnp.exp(math.log(9.663169819873474e-09) - 1.3768157 * jax.random.uniform(key_of[12], (D, D), jnp.float32) ** shard_levels(key_of[12], (D, D), ((1, 32),), -0.2, 0.2)), 2.4387998287522805e-09, 9.663169819873474e-09),
        "up_weight": bell_draw(key_of[13], (D, FF), D ** -0.5, 0.1875, ((0, 32),), jnp.float32),
        "up_first": bell_draw(key_of[14], (D, FF), (0.11 * 0.8 / PARAMS ** 0.5), 0.00036621094, ((0, 32),), jnp.float32),
        "up_second": jnp.clip(jnp.exp(math.log(9.663169819873474e-09) - 1.3768157 * jax.random.uniform(key_of[15], (D, FF), jnp.float32) ** shard_levels(key_of[15], (D, FF), ((0, 32),), -0.2, 0.2)), 2.4387998287522805e-09, 9.663169819873474e-09),
        "down_weight": bell_draw(key_of[16], (FF, D), FF ** -0.5, 0.09375, ((1, 32),), jnp.float32),
        "down_first": bell_draw(key_of[17], (FF, D), (0.11 * 0.8 / PARAMS ** 0.5), 0.00036621094, ((1, 32),), jnp.float32),
        "down_second": jnp.clip(jnp.exp(math.log(9.663169819873474e-09) - 1.3768157 * jax.random.uniform(key_of[18], (FF, D), jnp.float32) ** shard_levels(key_of[18], (FF, D), ((1, 32),), -0.2, 0.2)), 2.4387998287522805e-09, 9.663169819873474e-09),
        "dec_weight": draw_dec_weight(jax.random.fold_in(key_of[25], 71), 0),
        "dec_first": bell_draw(key_of[20], (D, DDEC), (0.11 * 2.0 / PARAMS ** 0.5), 0.0008544922, ((0, 32),), jnp.float32),
        "dec_second": jnp.clip(jnp.exp(math.log(6.039481093012e-08) - 1.3768157 * jax.random.uniform(key_of[21], (D, DDEC), jnp.float32) ** shard_levels(key_of[21], (D, DDEC), ((0, 32),), -0.2, 0.2)), 1.524249881867945e-08, 6.039481093012e-08),
        "vectors": draw_vectors(jax.random.fold_in(key_of[25], 71), 0),
        "vec_first": bell_draw(key_of[23], (VEC,), (0.11 * 3.0 / PARAMS ** 0.5), 0.0012207031, ((0, 32),), jnp.float32),
        "vec_second": jnp.clip(jnp.exp(math.log(1.3588832814548368e-07) - 1.3768157 * jax.random.uniform(key_of[24], (VEC,), jnp.float32) ** shard_levels(key_of[24], (VEC,), ((0, 32),), -0.2, 0.2)), 3.4295624118385604e-08, 1.3588832814548368e-07),
    }


EPS_NORM = 1e-05
BETA_ONE = 0.9
BETA_TWO = 0.95
ADAM_EPS = 1e-08
LR_MATRIX = 0.08
LR_VECTOR = 0.3
DECAY_MATRIX = 0.05
CLIP_LEVEL = 1.0

@jax.custom_vjp
def low(v):
    return lax.optimization_barrier(v.astype(jnp.bfloat16)).astype(jnp.float32)

@jax.custom_vjp
def low_back(v):
    return v

def low_keep(v):
    return (low(v), None)

def low_pass(kept, grad):
    return (grad,)

def back_keep(v):
    return (v, None)

def back_low(kept, grad):
    return (low(grad),)
low.defvjp(low_keep, low_pass)
low_back.defvjp(back_keep, back_low)

def matmul_high(left, right):
    return jnp.dot(left, right, precision=lax.Precision.HIGHEST, preferred_element_type=jnp.float32)

def angle_table(grid_rows, grid_cols, ratios, channels):
    quarter = channels // 4
    frequency = jnp.exp(jnp.arange(quarter).astype(jnp.float32) * (-jnp.log(10000.0) / quarter))
    row_angle = (grid_rows * ratios)[..., None] * frequency
    col_angle = (grid_cols * ratios)[..., None] * frequency
    return jnp.concatenate([jnp.sin(row_angle), jnp.cos(row_angle), jnp.sin(col_angle), jnp.cos(col_angle)], axis=-1)

def split_vectors(vector_all):
    pieces = tuple((vector_all[number * D:(number + 1) * D] for number in range(10)))
    return (pieces, vector_all[10 * D:10 * D + FF], vector_all[10 * D + FF:])

def layer_norm(hidden_in, norm_gain, norm_shift):
    center = hidden_in - lax.optimization_barrier(jnp.mean(hidden_in, axis=-1, keepdims=True))
    variance = lax.optimization_barrier(jnp.mean(center * center, axis=-1, keepdims=True))
    return center * lax.rsqrt(variance + EPS_NORM) * norm_gain + norm_shift

def group_forward(lowered, pixel_norm, visible_group, ratio_group):
    pe_w, qkv_w, out_w, up_w, down_w, dec_w, vector_all = lowered
    pieces, up_bias, dec_bias = split_vectors(vector_all)
    gain_one, shift_one, gain_two, shift_two, pe_bias, query_bias, value_bias, out_bias, down_bias, mask_token = pieces
    image_count = pixel_norm.shape[0]
    grid_rows = (visible_group // SIDE).astype(jnp.float32)
    grid_cols = (visible_group % SIDE).astype(jnp.float32)
    stream_in = low_back(matmul_high(low(pixel_norm), pe_w)) + pe_bias
    stream_in = stream_in + angle_table(grid_rows, grid_cols, ratio_group[:, None], D)
    norm_one = low(layer_norm(stream_in, gain_one, shift_one))
    projected = low_back(matmul_high(norm_one, qkv_w)) + jnp.concatenate([query_bias, jnp.zeros_like(query_bias), value_bias])
    projected = low(projected).reshape(image_count, VIS, 3, HEADS, HDIM)
    queries = projected[:, :, 0]
    keys_head = projected[:, :, 1]
    values_head = projected[:, :, 2]
    raw_scores = jnp.einsum('nqhd,nkhd->nhqk', queries, keys_head, precision=lax.Precision.HIGHEST)
    probs = jax.nn.softmax(low_back(raw_scores) * HDIM ** (-0.5), axis=-1)
    mixture = jnp.einsum('nhqk,nkhd->nqhd', low(probs), values_head, precision=lax.Precision.HIGHEST)
    mixture = low(low_back(mixture.reshape(image_count, VIS, D)))
    stream_mid = stream_in + low_back(matmul_high(mixture, out_w)) + out_bias
    norm_two = low(layer_norm(stream_mid, gain_two, shift_two))
    activated = jax.nn.gelu(low_back(matmul_high(norm_two, up_w)) + up_bias, approximate=False)
    stream_out = stream_mid + low_back(matmul_high(low(activated), down_w)) + down_bias
    placement = (visible_group[:, :, None] == jnp.arange(GRID)[None, None, :]).astype(jnp.float32)
    vacant = 1.0 - lax.optimization_barrier(jnp.sum(placement, axis=1))
    full_grid = jnp.einsum('nvg,nvd->ngd', placement, stream_out, precision=lax.Precision.HIGHEST)
    full_grid = full_grid + vacant[:, :, None] * mask_token
    decoded = matmul_high(low(low_back(full_grid)), dec_w) + dec_bias
    positions = jnp.arange(GRID)
    pos_rows = (positions // SIDE).astype(jnp.float32)[None, :]
    pos_cols = (positions % SIDE).astype(jnp.float32)[None, :]
    return decoded + angle_table(pos_rows, pos_cols, ratio_group[:, None], DDEC)

def adamw_update(weight, moment_one, moment_two, gradient, step_rate, decay_rate):
    new_one = BETA_ONE * moment_one + (1.0 - BETA_ONE) * gradient
    new_two = BETA_TWO * moment_two + (1.0 - BETA_TWO) * gradient * gradient
    fixed_one = new_one / (1.0 - BETA_ONE ** STEP)
    fixed_two = new_two / (1.0 - BETA_TWO ** STEP)
    new_weight = weight - step_rate * (fixed_one / (jnp.sqrt(fixed_two) + ADAM_EPS) + decay_rate * weight)
    return (new_one, new_two, new_weight)

def reference(pixels, visible, scale_index, cotangent, pe_weight, pe_first, pe_second, qkv_weight, qkv_first, qkv_second, out_weight, out_first, out_second, up_weight, up_first, up_second, down_weight, down_first, down_second, dec_weight, dec_first, dec_second, vectors, vec_first, vec_second):
    groups = IMAGES // IMG_DEV
    visible_groups = visible.reshape(groups, IMG_DEV, VIS)
    ratio_groups = jnp.power(2.0, scale_index.astype(jnp.float32) - 1.0).reshape(groups, IMG_DEV)
    params = (pe_weight, qkv_weight, out_weight, up_weight, down_weight, dec_weight, vectors)
    pixel_rows = pixels.astype(jnp.float32).reshape(IMAGES * VIS, BANDS, PATCH * PATCH)
    entry_count = IMAGES * VIS * PATCH * PATCH
    band_mean = lax.optimization_barrier(jnp.sum(pixel_rows, axis=(0, 2))) / entry_count
    variance = lax.optimization_barrier(jnp.sum(pixel_rows * pixel_rows, axis=(0, 2))) / entry_count - band_mean * band_mean
    band_scale = lax.rsqrt(variance + EPS_NORM)
    pixel_norm = (pixel_rows - band_mean[None, :, None]) * band_scale[None, :, None]
    pixel_norm = pixel_norm.reshape(groups, IMG_DEV, VIS, PIX)

    def forward(weights, pixel_in):
        lowered = tuple((low(member) for member in weights))
        checked = jax.checkpoint(group_forward)

        def scan_step(loop_carry, scan_item):
            return (loop_carry, checked(lowered, scan_item[0], scan_item[1], scan_item[2]))
        _, outputs = lax.scan(scan_step, jnp.zeros((), jnp.float32), (pixel_in, visible_groups, ratio_groups))
        return outputs
    outputs, pullback = jax.vjp(forward, params, pixel_norm)
    decoded = outputs.reshape(N_GRP, N_DP, IMG_DEV, 4, QUART, DDEC).transpose(0, 2, 3, 1, 4, 5)
    decoded = decoded.reshape(N_GRP, 4 * IMG_DEV, N_DP, QUART, DDEC).astype(jnp.bfloat16)
    incoming = cotangent.astype(jnp.float32).reshape(N_GRP, IMG_DEV, 4, N_DP, QUART, DDEC).transpose(0, 3, 1, 2, 4, 5)
    incoming = incoming.reshape(groups, IMG_DEV, GRID, DDEC)
    gradients, norm_grad = pullback(incoming)
    pixel_grad = norm_grad.reshape(IMAGES * VIS, BANDS, PATCH * PATCH) * band_scale[None, :, None]
    pixel_grad = pixel_grad.reshape(IMAGES, VIS, PIX)
    squares = sum((jnp.sum(gradient * gradient) for gradient in gradients))
    grad_norm = jnp.sqrt(squares)
    clip_factor = jnp.minimum(1.0, CLIP_LEVEL / grad_norm)
    firsts = (pe_first, qkv_first, out_first, up_first, down_first, dec_first, vec_first)
    seconds = (pe_second, qkv_second, out_second, up_second, down_second, dec_second, vec_second)
    results = []
    for number in range(7):
        step_rate = LR_VECTOR if number == 6 else LR_MATRIX
        decay_rate = 0.0 if number == 6 else DECAY_MATRIX
        results.append(adamw_update(params[number], firsts[number], seconds[number], gradients[number] * clip_factor, step_rate, decay_rate))
    return (decoded, pixel_grad, results[0][0], results[0][1], results[0][2], results[1][0], results[1][1], results[1][2], results[2][0], results[2][1], results[2][2], results[3][0], results[3][1], results[3][2], results[4][0], results[4][1], results[4][2], results[5][0], results[5][1], results[5][2], results[6][0], results[6][1], results[6][2], grad_norm)
```

```python
import jax
import jax.numpy as jnp
import ml_dtypes
import numpy as np
from jax import lax
from jax.experimental import pallas as pl
from jax.experimental.pallas import tpu as pltpu
from jax.sharding import PartitionSpec as P

D = 1024
FF = 4096
HEADS = 16
HDIM = 64
DDEC = 512
PATCH = 16
SIDE = 14
BANDS = 3
STEP = 10
PIX = 768
GRID = 196
VIS = 49
QUART = 49
NSCALE = 4
AXES = ("grp", "dp")
BF = jnp.bfloat16
F32 = jnp.float32

EPS_NORM = 1e-05
BETA_ONE = 0.9
BETA_TWO = 0.95
ADAM_EPS = 1e-08
LR_MATRIX = 0.08
LR_VECTOR = 0.3
DECAY_MATRIX = 0.05
CLIP_LEVEL = 1.0


def forward_product(left, right):
    return jnp.dot(left, right, preferred_element_type=F32)


def back_product(left, right):
    return lax.dot_general(left, right, (((1,), (1,)), ((), ())), preferred_element_type=F32)


def weight_product(left, right):
    return lax.dot_general(left, right, (((0,), (0,)), ((), ())), preferred_element_type=F32)


def angle_pieces(channels, pieces):
    quarter = channels // 4
    step = np.float32(-np.log(np.float32(10000.0))) / np.float32(quarter)
    frequency = np.exp(np.arange(quarter, dtype=np.float32) * step)
    ratio = np.float32(2.0) ** (np.arange(NSCALE, dtype=np.float32) - 1)
    spot = np.arange(SIDE, dtype=np.float32)
    angle = (ratio[:, None] * spot[None, :]).reshape(-1, 1) * frequency[None, :]
    half = np.concatenate([np.sin(angle.astype(np.float64)), np.cos(angle.astype(np.float64))], 1)
    zeros = np.zeros_like(half)
    rest = np.concatenate(
        [np.concatenate([half, zeros], 1), np.concatenate([zeros, half], 1)], 0
    ).astype(np.float32)
    cut = []
    for _ in range(pieces):
        part = rest.astype(ml_dtypes.bfloat16)
        cut.append(part)
        rest = rest - part.astype(np.float32)
    return jnp.asarray(np.concatenate(cut, 0))


def angle_hot(spots, scale_rows, pieces):
    row_at = scale_rows * SIDE + spots // SIDE
    col_at = (NSCALE + scale_rows) * SIDE + spots % SIDE
    slot = jnp.arange(2 * NSCALE * SIDE)[None, :]
    hot = ((slot == row_at[:, None]) | (slot == col_at[:, None])).astype(BF)
    return jnp.concatenate([hot] * pieces, axis=1)


def split_vectors(vector_all):
    pieces = tuple((vector_all[number * D : (number + 1) * D] for number in range(10)))
    return (pieces, vector_all[10 * D : 10 * D + FF], vector_all[10 * D + FF :])


def norm_forward(hidden_in, norm_gain, norm_shift):
    center = hidden_in - jnp.mean(hidden_in, axis=-1, keepdims=True)
    inv_std = lax.rsqrt(jnp.mean(center * center, axis=-1, keepdims=True) + EPS_NORM)
    normed = center * inv_std
    return (normed * norm_gain + norm_shift, normed, inv_std)


def norm_backward(grad_out, normed, inv_std, norm_gain):
    scaled = grad_out * norm_gain
    inner = (
        scaled
        - jnp.mean(scaled, axis=-1, keepdims=True)
        - normed * jnp.mean(scaled * normed, axis=-1, keepdims=True)
    )
    return (inner * inv_std, jnp.sum(grad_out * normed, axis=0), jnp.sum(grad_out, axis=0))


def gelu_slope(preact):
    return (
        0.5 * (1.0 + lax.erf(preact * 0.7071067811865476))
        + preact * jnp.exp(-0.5 * preact * preact) * 0.3989422804014327
    )


def adamw_update(weight, moment_one, moment_two, gradient, step_rate, decay_rate):
    new_one = BETA_ONE * moment_one + (1.0 - BETA_ONE) * gradient
    new_two = BETA_TWO * moment_two + (1.0 - BETA_TWO) * gradient * gradient
    fixed_one = new_one / (1.0 - BETA_ONE**STEP)
    fixed_two = new_two / (1.0 - BETA_TWO**STEP)
    new_weight = weight - step_rate * (
        fixed_one / (jnp.sqrt(fixed_two) + ADAM_EPS) + decay_rate * weight
    )
    return (new_one, new_two, new_weight)


def core_pairs():
    return [(0, 1), (1, 0)]


def dp_pairs(bits):
    return [(i, i ^ bits) for i in range(16)]


def turn_pairs(core_zero, core_one):
    return [(g * 16 + i, g * 16 + (i ^ (core_one if g else core_zero))) for g in range(2) for i in range(16)]


def tiny_sum(value, routed):
    if not routed:
        return lax.psum(value, AXES)
    for bits in (1, 2, 4, 8):
        value = value + lax.ppermute(value, "dp", dp_pairs(bits))
    return value + lax.ppermute(value, "grp", core_pairs())


def take(array, index):
    return lax.dynamic_slice_in_dim(array, index, 1, axis=array.ndim - 3)


def summed_shard(left, right, extra, routed):
    columns = right.shape[1]
    if not routed:
        full = weight_product(left, right)
        if extra is not None:
            full = full + extra(0, D)
        half = lax.psum_scatter(full.astype(BF), "grp", scatter_dimension=0, tiled=True)
        return lax.psum_scatter(half, "dp", scatter_dimension=0, tiled=True).astype(F32)
    core = lax.axis_index("grp")
    chip = lax.axis_index("dp")
    x, y, z = chip % 2, (chip // 2) % 2, chip // 4
    half = D // 2

    def product(at):
        part = weight_product(lax.dynamic_slice_in_dim(left, at, half, axis=1), right)
        return part if extra is None else part + extra(at, half)

    away = product((1 - core) * half).astype(BF)
    came = lax.ppermute(away, "grp", core_pairs())
    held = (product(core * half) + came.astype(F32)).astype(BF)
    held = held.reshape(4, 4, 32, columns)
    first = core == 0
    mine, other = jnp.where(first, x, y), jnp.where(first, 1 - x, 1 - y)
    stride, span = jnp.where(first, 1, 2), jnp.where(first, 2, 1)
    away = jnp.concatenate([take(held, other * stride), take(held, other * stride + span)], axis=1)
    kept = jnp.concatenate([take(held, mine * stride), take(held, mine * stride + span)], axis=1)
    came = lax.ppermute(away, AXES, turn_pairs(1, 2))
    held = (kept.astype(F32) + came.astype(F32)).astype(BF)
    mine = jnp.where(first, y, x)
    came = lax.ppermute(take(held, 1 - mine), AXES, turn_pairs(2, 1))
    held = (take(held, mine).astype(F32) + came.astype(F32)).astype(BF).reshape(4, 32, columns)

    def row(index):
        return lax.dynamic_index_in_dim(held, index, axis=0, keepdims=False)

    came = [lax.ppermute(row(z ^ k), "dp", dp_pairs(4 * k)) for k in (1, 2, 3)]
    total = row(z).astype(F32)
    for part in came:
        total = total + part.astype(F32)
    return total


def local(
    pixels,
    visible,
    scale_index,
    cotangent,
    pe_weight,
    pe_first,
    pe_second,
    qkv_weight,
    qkv_first,
    qkv_second,
    out_weight,
    out_first,
    out_second,
    up_weight,
    up_first,
    up_second,
    down_weight,
    down_first,
    down_second,
    dec_weight,
    dec_first,
    dec_second,
    vectors,
    vec_first,
    vec_second,
):
    image_count = pixels.shape[0]
    row_count = image_count * VIS
    device_count = lax.axis_size(AXES)
    dp_count = lax.axis_size("dp")
    shard_rows = D // device_count
    routed = dp_count == 16 and device_count == 32
    item_count = 4 * image_count // dp_count
    whole_images = item_count % 4 == 0

    early = jnp.concatenate([pe_weight.T, qkv_weight], axis=1).astype(BF)
    late = jnp.concatenate([out_weight.T, up_weight, down_weight.T, dec_weight], axis=1).astype(BF)
    early_full = lax.all_gather(early, AXES, axis=0, tiled=True)
    late_full = lax.all_gather(late, AXES, axis=0, tiled=True)
    pe_full, qkv_full = early_full[:, :PIX], early_full[:, PIX:]
    out_full = late_full[:, :D]
    up_full = late_full[:, D : D + FF]
    down_full = late_full[:, D + FF : D + 2 * FF]
    dec_full = late_full[:, D + 2 * FF :]

    pixel_rows = pixels.astype(F32).reshape(row_count, BANDS, PATCH * PATCH)
    band_sum = jnp.sum(pixel_rows, axis=(0, 2))
    band_square = jnp.sum(pixel_rows * pixel_rows, axis=(0, 2))
    stats = tiny_sum(jnp.concatenate([band_sum, band_square]), routed)
    vector_all = lax.all_gather(vectors.astype(BF), AXES, axis=0, tiled=True)
    entry_count = row_count * device_count * PATCH * PATCH
    band_mean = stats[:BANDS] / entry_count
    band_scale = lax.rsqrt(stats[BANDS:] / entry_count - band_mean * band_mean + EPS_NORM)
    pixel_norm = (pixel_rows - band_mean[None, :, None]) * band_scale[None, :, None]
    pixel_low = pixel_norm.reshape(row_count, PIX).astype(BF)
    pieces, up_bias, dec_bias = split_vectors(vector_all.astype(F32))
    (
        gain_one,
        shift_one,
        gain_two,
        shift_two,
        pe_bias,
        query_bias,
        value_bias,
        out_bias,
        down_bias,
        mask_token,
    ) = pieces

    dp_index = lax.axis_index("dp")
    marks = jnp.concatenate([visible, scale_index[:, None]], axis=1)
    if whole_images:
        marks_in = lax.all_to_all(marks, "dp", split_axis=0, concat_axis=0, tiled=True)
        sent_images = image_count // dp_count
        image_order = marks_in.reshape(dp_count, sent_images, VIS + 1)
        visible_in, scale_in = image_order[:, :, :VIS], image_order[:, :, VIS]
        grids = cotangent[0].reshape(sent_images, 4, dp_count, QUART, DDEC)
        hot_in = (
            visible_in[..., None] == jnp.arange(GRID).reshape(1, 1, 1, GRID)
        ).astype(BF)
        hot_quarter = hot_in.reshape(dp_count, sent_images, VIS, 4, QUART)
        dy_sent = jnp.einsum(
            "skvqr,kqsrc->skvc", hot_quarter, grids, preferred_element_type=F32
        ).astype(BF)
        dy_rows = lax.all_to_all(
            dy_sent.reshape(image_count, VIS, DDEC), "dp", split_axis=0, concat_axis=0, tiled=True
        ).reshape(dp_count, sent_images, VIS, DDEC)
        dy_rows = dy_rows.reshape(row_count, DDEC)
        vacant_in = 1.0 - jnp.sum(hot_quarter.astype(F32), axis=2)
        dy_all = jnp.sum(cotangent[0].astype(F32), axis=(0, 1, 2))
        dy_vacant = jnp.einsum(
            "skqr,kqsrc->c", vacant_in.astype(BF), grids, preferred_element_type=F32
        )

    spots = visible.reshape(row_count)
    scale_rows = jnp.repeat(scale_index, VIS)
    enc_table = forward_product(angle_hot(spots, scale_rows, 3), angle_pieces(D, 3))
    stream_in = back_product(pixel_low, pe_full) + pe_bias + enc_table
    norm_out_one, normed_one, inv_std_one = norm_forward(stream_in, gain_one, shift_one)
    norm_one = norm_out_one.astype(BF)
    projected = forward_product(norm_one, qkv_full) + jnp.concatenate(
        [query_bias, jnp.zeros_like(query_bias), value_bias]
    )
    projected = projected.astype(BF).reshape(image_count, VIS, 3, HEADS, HDIM)
    queries = projected[:, :, 0]
    keys_head = projected[:, :, 1]
    values_head = projected[:, :, 2]
    scale_score = HDIM ** (-0.5)
    raw_scores = (
        jnp.einsum("nqhd,nkhd->nhqk", queries, keys_head, preferred_element_type=F32)
        * scale_score
    )
    score_peak = jnp.max(raw_scores, axis=-1, keepdims=True)
    log_total = score_peak + jnp.log(
        jnp.sum(jnp.exp(raw_scores - score_peak), axis=-1, keepdims=True)
    )
    softmaxed = jnp.exp(raw_scores - log_total)
    mixture = jnp.einsum(
        "nhqk,nkhd->nqhd", softmaxed.astype(BF), values_head, preferred_element_type=F32
    )
    mixture_low = mixture.reshape(row_count, D).astype(BF)
    stream_mid = stream_in + back_product(mixture_low, out_full) + out_bias
    norm_out_two, normed_two, inv_std_two = norm_forward(stream_mid, gain_two, shift_two)
    norm_two = norm_out_two.astype(BF)
    preact = forward_product(norm_two, up_full) + up_bias
    activated = jax.nn.gelu(preact, approximate=False).astype(BF)
    stream_out = stream_mid + back_product(activated, down_full) + down_bias
    stream_low = stream_out.astype(BF)

    if whole_images:
        dec_pieces = angle_pieces(DDEC, 2)
        vis_table = forward_product(angle_hot(spots, scale_rows, 2), dec_pieces)
        vis_rows = (forward_product(stream_low, dec_full) + dec_bias + vis_table).astype(BF)
        vis_in = lax.all_to_all(
            vis_rows.reshape(image_count, VIS, DDEC), "dp", split_axis=0, concat_axis=0, tiled=True
        ).reshape(dp_count, sent_images, VIS, DDEC)
        placed = jnp.einsum(
            "skvqr,skvc->kqsrc", hot_quarter, vis_in, preferred_element_type=F32
        )
        position = jnp.arange(GRID)
        every_hot = angle_hot(
            jnp.tile(position, dp_count * sent_images),
            jnp.repeat(scale_in.reshape(-1), GRID),
            2,
        ).reshape(dp_count, sent_images, 4, QUART, -1)
        every_table = jnp.einsum(
            "skqrt,tc->kqsrc", every_hot, dec_pieces, preferred_element_type=F32
        )
        mask_rows = forward_product(jnp.broadcast_to(mask_token.astype(BF), (8, D)), dec_full)[0]
        empty = vacant_in.transpose(1, 2, 0, 3)[..., None] > 0.5
        decoded = jnp.where(empty, every_table + (mask_rows + dec_bias), placed)
        decoded = decoded.astype(BF).reshape(1, item_count, dp_count, QUART, DDEC)
        out_grad_rows = back_product(dy_rows, dec_full).astype(BF).astype(F32)
        dec_bias_grad = dy_all
        vacant_parts = []
        rest = dy_vacant
        for _ in range(3):
            part = lax.reduce_precision(rest, 8, 7)
            vacant_parts.append(part)
            rest = rest - part
        vacant_low = jnp.stack(vacant_parts).astype(BF)
        mask_grad = jnp.sum(back_product(vacant_low, dec_full), axis=0)

        def dec_extra(at, count):
            token = lax.dynamic_slice_in_dim(mask_token, at, count)
            return token[:, None] * dy_vacant[None, :]

        dec_left, dec_right = stream_low, dy_rows
    else:
        dec_extra = None
        placement = visible[:, :, None] == jnp.arange(GRID)[None, None, :]
        placement_low = placement.astype(BF)
        vacant = 1.0 - jnp.sum(placement.astype(F32), axis=1)
        full_grid = jnp.einsum(
            "nvg,nvd->ngd",
            placement_low,
            stream_low.reshape(image_count, VIS, D),
            preferred_element_type=F32,
        )
        full_grid = (full_grid + vacant[:, :, None] * mask_token).astype(BF)
        quarters = full_grid.reshape(4 * image_count, 1, QUART, D)
        ratio_image = jnp.power(2.0, scale_index.astype(F32) - 1.0)
        ratio_quarter = jnp.repeat(ratio_image, 4).reshape(4 * image_count, 1).astype(BF)
        received = lax.all_to_all(quarters, "dp", split_axis=0, concat_axis=1, tiled=True)
        received_ratio = lax.all_to_all(
            ratio_quarter, "dp", split_axis=0, concat_axis=1, tiled=True
        )
        quarter_id = dp_index * item_count + jnp.arange(item_count)
        position = (quarter_id % 4)[:, None] * QUART + jnp.arange(QUART)[None, :]
        scale_at = jnp.round(jnp.log2(received_ratio.astype(F32))).astype(jnp.int32) + 1
        full = (item_count, dp_count, QUART)
        dec_table = forward_product(
            angle_hot(
                jnp.broadcast_to(position[:, None, :], full).reshape(-1),
                jnp.broadcast_to(scale_at[:, :, None], full).reshape(-1),
                2,
            ),
            angle_pieces(DDEC, 2),
        ).reshape(full + (DDEC,))
        dec_rows = jnp.dot(received, dec_full, preferred_element_type=F32)
        decoded = (dec_rows + dec_bias + dec_table).astype(BF)[None]
        grad_rows = cotangent[0].reshape(-1, DDEC)
        dec_left, dec_right = received.reshape(-1, D), grad_rows
        dec_bias_grad = jnp.sum(grad_rows.astype(F32), axis=0)
        grid_grad = (
            back_product(grad_rows, dec_full).astype(BF).reshape(item_count, dp_count, QUART, D)
        )
        returned = lax.all_to_all(
            grid_grad, "dp", split_axis=1, concat_axis=0, tiled=True
        ).reshape(image_count, GRID, D)
        out_grad_rows = jnp.einsum(
            "nvg,ngd->nvd", placement_low, returned, preferred_element_type=F32
        ).reshape(row_count, D)
        mask_grad = jnp.einsum(
            "ng,ngd->d", vacant.astype(BF), returned, preferred_element_type=F32
        )

    dec_shard = summed_shard(dec_left, dec_right, dec_extra, routed)
    out_rows_low = out_grad_rows.astype(BF)
    down_shard = summed_shard(out_rows_low, activated, None, routed)
    down_bias_grad = jnp.sum(out_grad_rows, axis=0)
    preact_grad = forward_product(out_rows_low, down_full) * gelu_slope(preact)
    up_bias_grad = jnp.sum(preact_grad, axis=0)
    preact_low = preact_grad.astype(BF)
    up_shard = summed_shard(norm_two, preact_low, None, routed)
    two_grad = back_product(preact_low, up_full)
    mid_grad, gain_two_grad, shift_two_grad = norm_backward(
        two_grad, normed_two, inv_std_two, gain_two
    )
    mid_grad = mid_grad + out_grad_rows
    mid_low = mid_grad.astype(BF)
    out_shard = summed_shard(mid_low, mixture_low, None, routed)
    out_bias_grad = jnp.sum(mid_grad, axis=0)
    mixture_grad = (
        forward_product(mid_low, out_full).astype(BF).reshape(image_count, VIS, HEADS, HDIM)
    )
    again_scores = (
        jnp.einsum("nqhd,nkhd->nhqk", queries, keys_head, preferred_element_type=F32)
        * scale_score
    )
    again_probs = jnp.exp(again_scores - log_total)
    value_grad = jnp.einsum(
        "nhqk,nqhd->nkhd", again_probs.astype(BF), mixture_grad, preferred_element_type=F32
    )
    probs_grad = jnp.einsum(
        "nqhd,nkhd->nhqk", mixture_grad, values_head, preferred_element_type=F32
    )
    score_low = (
        again_probs
        * (probs_grad - jnp.sum(probs_grad * again_probs, axis=-1, keepdims=True))
        * scale_score
    ).astype(BF)
    query_grad = jnp.einsum(
        "nhqk,nkhd->nqhd", score_low, keys_head, preferred_element_type=F32
    )
    key_grad = jnp.einsum("nhqk,nqhd->nkhd", score_low, queries, preferred_element_type=F32)
    projected_grad = jnp.stack([query_grad, key_grad, value_grad], axis=2).reshape(row_count, 3 * D)
    query_bias_grad = jnp.sum(projected_grad[:, :D], axis=0)
    value_bias_grad = jnp.sum(projected_grad[:, 2 * D :], axis=0)
    projected_low = projected_grad.astype(BF)
    qkv_shard = summed_shard(norm_one, projected_low, None, routed)
    one_grad = back_product(projected_low, qkv_full)
    in_grad, gain_one_grad, shift_one_grad = norm_backward(
        one_grad, normed_one, inv_std_one, gain_one
    )
    in_grad = in_grad + mid_grad
    pe_bias_grad = jnp.sum(in_grad, axis=0)
    in_low = in_grad.astype(BF)
    pe_shard = summed_shard(in_low, pixel_low, None, routed)
    norm_grad = forward_product(in_low, pe_full).reshape(row_count, BANDS, PATCH * PATCH)
    pixel_grad = (norm_grad * band_scale[None, :, None]).reshape(image_count, VIS, PIX)
    vec_grad = jnp.concatenate(
        [
            gain_one_grad,
            shift_one_grad,
            gain_two_grad,
            shift_two_grad,
            pe_bias_grad,
            query_bias_grad,
            value_bias_grad,
            out_bias_grad,
            down_bias_grad,
            mask_grad,
            up_bias_grad,
            dec_bias_grad,
        ]
    )
    if routed:
        vec_length = vectors.shape[0]
        vec_half = dp_count * vec_length
        core = lax.axis_index("grp")
        away = lax.dynamic_slice_in_dim(vec_grad, (1 - core) * vec_half, vec_half)
        kept = lax.dynamic_slice_in_dim(vec_grad, core * vec_half, vec_half)
        kept = kept + lax.ppermute(away, "grp", core_pairs())
        vec_shard = jnp.sum(
            lax.all_to_all(
                kept.reshape(dp_count, vec_length), "dp", split_axis=0, concat_axis=0, tiled=True
            ),
            axis=0,
        )
    else:
        vec_shard = lax.psum_scatter(vec_grad, AXES, scatter_dimension=0, tiled=True)
    shards = (pe_shard, qkv_shard, out_shard, up_shard, down_shard, dec_shard, vec_shard)
    local_squares = sum((jnp.sum(gradient * gradient) for gradient in shards))
    squares = tiny_sum(local_squares.reshape(1), routed)[0]
    grad_norm = jnp.sqrt(squares)
    clip_factor = jnp.minimum(1.0, CLIP_LEVEL / grad_norm)
    params = (pe_weight, qkv_weight, out_weight, up_weight, down_weight, dec_weight, vectors)
    firsts = (pe_first, qkv_first, out_first, up_first, down_first, dec_first, vec_first)
    seconds = (pe_second, qkv_second, out_second, up_second, down_second, dec_second, vec_second)
    results = []
    for number in range(7):
        step_rate = LR_VECTOR if number == 6 else LR_MATRIX
        decay_rate = 0.0 if number == 6 else DECAY_MATRIX
        gradient = shards[number].T if number in (0, 2, 4) else shards[number]
        results.extend(
            adamw_update(
                params[number],
                firsts[number],
                seconds[number],
                gradient * clip_factor,
                step_rate,
                decay_rate,
            )
        )
    return (decoded, pixel_grad, *results, grad_norm)


def solution(mesh):
    rows = P(AXES, None)
    cols = P(None, AXES)
    vecs = P(AXES)
    images = P(AXES, None, None)
    grids = P("grp", "dp", None, None, None)
    states = (cols,) * 3 + (rows,) * 3 + (cols,) * 3 + (rows,) * 3 + (cols,) * 3 + (rows,) * 3
    states = states + (vecs,) * 3
    return jax.shard_map(
        local,
        mesh=mesh,
        in_specs=(images, rows, vecs, grids) + states,
        out_specs=(grids, images) + states + (P(),),
        check_vma=False,
    )
```

```python
import jax
import jax.numpy as jnp
import ml_dtypes
import numpy as np
from jax import lax
from jax.experimental import pallas as pl
from jax.experimental.pallas import tpu as pltpu
from jax.sharding import PartitionSpec as P

D = 1024
FF = 4096
HEADS = 16
HDIM = 64
DDEC = 512
PATCH = 16
SIDE = 14
BANDS = 3
STEP = 10
PIX = 768
GRID = 196
VIS = 49
QUART = 49
NSCALE = 4
AXES = ("grp", "dp")
BF = jnp.bfloat16
F32 = jnp.float32

EPS_NORM = 1e-05
BETA_ONE = 0.9
BETA_TWO = 0.95
ADAM_EPS = 1e-08
LR_MATRIX = 0.08
LR_VECTOR = 0.3
DECAY_MATRIX = 0.05
CLIP_LEVEL = 1.0


def forward_product(left, right):
    return jnp.dot(left, right, preferred_element_type=F32)


def back_product(left, right):
    return lax.dot_general(left, right, (((1,), (1,)), ((), ())), preferred_element_type=F32)


def weight_product(left, right):
    return lax.dot_general(left, right, (((0,), (0,)), ((), ())), preferred_element_type=F32)


def angle_pieces(channels, pieces):
    quarter = channels // 4
    step = np.float32(-np.log(np.float32(10000.0))) / np.float32(quarter)
    frequency = np.exp(np.arange(quarter, dtype=np.float32) * step)
    ratio = np.float32(2.0) ** (np.arange(NSCALE, dtype=np.float32) - 1)
    spot = np.arange(SIDE, dtype=np.float32)
    angle = (ratio[:, None] * spot[None, :]).reshape(-1, 1) * frequency[None, :]
    half = np.concatenate([np.sin(angle.astype(np.float64)), np.cos(angle.astype(np.float64))], 1)
    zeros = np.zeros_like(half)
    rest = np.concatenate(
        [np.concatenate([half, zeros], 1), np.concatenate([zeros, half], 1)], 0
    ).astype(np.float32)
    cut = []
    for _ in range(pieces):
        part = rest.astype(ml_dtypes.bfloat16)
        cut.append(part)
        rest = rest - part.astype(np.float32)
    return jnp.asarray(np.concatenate(cut, 0))


def angle_hot(spots, scale_rows, pieces):
    row_at = scale_rows * SIDE + spots // SIDE
    col_at = (NSCALE + scale_rows) * SIDE + spots % SIDE
    slot = jnp.arange(2 * NSCALE * SIDE)[None, :]
    hot = ((slot == row_at[:, None]) | (slot == col_at[:, None])).astype(BF)
    return jnp.concatenate([hot] * pieces, axis=1)


def split_vectors(vector_all):
    pieces = tuple((vector_all[number * D : (number + 1) * D] for number in range(10)))
    return (pieces, vector_all[10 * D : 10 * D + FF], vector_all[10 * D + FF :])


def norm_forward(hidden_in, norm_gain, norm_shift):
    center = hidden_in - jnp.mean(hidden_in, axis=-1, keepdims=True)
    inv_std = lax.rsqrt(jnp.mean(center * center, axis=-1, keepdims=True) + EPS_NORM)
    normed = center * inv_std
    return (normed * norm_gain + norm_shift, normed, inv_std)


def norm_backward(grad_out, normed, inv_std, norm_gain):
    scaled = grad_out * norm_gain
    inner = (
        scaled
        - jnp.mean(scaled, axis=-1, keepdims=True)
        - normed * jnp.mean(scaled * normed, axis=-1, keepdims=True)
    )
    return (inner * inv_std, jnp.sum(grad_out * normed, axis=0), jnp.sum(grad_out, axis=0))


def adamw_update(weight, moment_one, moment_two, gradient, step_rate, decay_rate):
    new_one = BETA_ONE * moment_one + (1.0 - BETA_ONE) * gradient
    new_two = BETA_TWO * moment_two + (1.0 - BETA_TWO) * gradient * gradient
    fixed_one = new_one / (1.0 - BETA_ONE**STEP)
    fixed_two = new_two / (1.0 - BETA_TWO**STEP)
    new_weight = weight - step_rate * (
        fixed_one / (jnp.sqrt(fixed_two) + ADAM_EPS) + decay_rate * weight
    )
    return (new_one, new_two, new_weight)


def core_pairs():
    return [(0, 1), (1, 0)]


def dp_pairs(bits):
    return [(i, i ^ bits) for i in range(16)]


def turn_pairs(core_zero, core_one):
    return [(g * 16 + i, g * 16 + (i ^ (core_one if g else core_zero))) for g in range(2) for i in range(16)]


def tiny_sum(value, routed):
    if not routed:
        return lax.psum(value, AXES)
    for bits in (1, 2, 4, 8):
        value = value + lax.ppermute(value, "dp", dp_pairs(bits))
    return value + lax.ppermute(value, "grp", core_pairs())


def tie(*values):
    return lax.optimization_barrier(values)


def take(array, index):
    return lax.dynamic_slice_in_dim(array, index, 1, axis=array.ndim - 3)


def spot_of_chip():
    chip = lax.axis_index("dp")
    return lax.axis_index("grp"), chip % 2, (chip // 2) % 2, chip // 4


class Gathering:
    def __init__(self, shard, direct):
        self.shard, self.direct = shard, direct
        self.core, self.x, self.y, self.z = spot_of_chip()
        steps = (1, 2, 3) if direct else (1,)
        self.near = [lax.ppermute(shard, "dp", dp_pairs(4 * k)) for k in steps]

    def middle(self, after):
        shard, near = tie(self.shard, after)[0], self.near[0]
        even = self.z % 2 == 0
        self.held = jnp.stack([jnp.where(even, shard, near), jnp.where(even, near, shard)])
        self.near = lax.ppermute(self.held, "dp", dp_pairs(8))
        return self

    def first_turn(self, after):
        if self.direct:
            held = jnp.zeros((4,) + self.shard.shape, self.shard.dtype)
            for k, part in enumerate([self.shard] + self.near):
                held = lax.dynamic_update_slice(held, part[None], (self.z ^ k, 0, 0))
        else:
            held, near = self.held, self.near
            front = self.z < 2
            held = jnp.concatenate([jnp.where(front, held, near), jnp.where(front, near, held)])
        self.held = tie(held, after)[0]
        self.near = lax.ppermute(self.held, AXES, turn_pairs(2, 1))
        return self

    def second_turn(self, after):
        mine = jnp.where(self.core == 0, self.y, self.x) == 0
        held, near = tie(self.held, after)[0], self.near
        self.held = jnp.stack([jnp.where(mine, held, near), jnp.where(mine, near, held)])
        self.near = lax.ppermute(self.held, AXES, turn_pairs(1, 2))
        return self

    def cores(self, after):
        blocks = []
        self.held = tie(self.held, after)[0]
        first = self.core == 0
        for at_y in range(2):
            for at_x in range(2):
                if_first = jnp.where(self.x == at_x, self.held[at_y], self.near[at_y])
                if_second = jnp.where(self.y == at_y, self.held[at_x], self.near[at_x])
                blocks.append(jnp.where(first, if_first, if_second))
        self.held = jnp.stack(blocks, axis=1).reshape(D // 2, self.shard.shape[1])
        self.near = lax.ppermute(self.held, "grp", core_pairs())
        return self

    def total(self):
        first = self.core == 0
        return jnp.concatenate(
            [jnp.where(first, self.held, self.near), jnp.where(first, self.near, self.held)]
        )


class Reduction:
    def __init__(self, product, routed):
        self.product, self.routed = product, routed
        self.core, self.x, self.y, self.z = spot_of_chip()
        self.away = self.kept = None

    def cores(self, after):
        if self.routed:
            half = D // 2
            self.away = self.product((1 - self.core) * half, half, after).astype(BF)
            self.came = lax.ppermute(self.away, "grp", core_pairs())
        return self

    def first_turn(self, after):
        if not self.routed:
            return self
        half = D // 2
        own = self.product(self.core * half, half, after)
        held = (own + self.came.astype(F32)).astype(BF)
        columns = held.shape[1]
        held = held.reshape(4, 4, 32, columns)
        first = self.core == 0
        mine = jnp.where(first, self.x, self.y)
        stride, span = jnp.where(first, 1, 2), jnp.where(first, 2, 1)
        other = 1 - mine
        self.away = jnp.concatenate(
            [take(held, other * stride), take(held, other * stride + span)], axis=1
        )
        self.kept = jnp.concatenate(
            [take(held, mine * stride), take(held, mine * stride + span)], axis=1
        )
        self.came = lax.ppermute(self.away, AXES, turn_pairs(1, 2))
        return self

    def second_turn(self, after):
        if not self.routed:
            return self
        kept, _ = tie(self.kept, after)
        held = (kept.astype(F32) + self.came.astype(F32)).astype(BF)
        mine = jnp.where(self.core == 0, self.y, self.x)
        self.away, self.kept = take(held, 1 - mine), take(held, mine)
        self.came = lax.ppermute(self.away, AXES, turn_pairs(2, 1))
        return self

    def along_z(self, after):
        if not self.routed:
            return self
        kept, _ = tie(self.kept, after)
        held = (kept.astype(F32) + self.came.astype(F32)).astype(BF)
        held = held.reshape(4, 32, held.shape[-1])

        def row(index):
            return lax.dynamic_index_in_dim(held, index, axis=0, keepdims=False)

        self.kept = row(self.z)
        self.away = [row(self.z ^ k) for k in (1, 2, 3)]
        self.came = [lax.ppermute(self.away[k - 1], "dp", dp_pairs(4 * k)) for k in (1, 2, 3)]
        return self

    def second_turn_with(self, other, after):
        if not self.routed:
            mine, theirs = self.product, other.product
            self.product = lambda *at: jnp.concatenate([mine(*at), theirs(*at)], axis=1)
            return self
        self.came = jnp.concatenate([self.came, other.came], axis=-1)
        self.kept = jnp.concatenate([self.kept, other.kept], axis=-1)
        return self.second_turn(after)

    def total(self, after=None):
        if not self.routed:
            half = lax.psum_scatter(
                self.product(0, D, None).astype(BF), "grp", scatter_dimension=0, tiled=True
            )
            return lax.psum_scatter(half, "dp", scatter_dimension=0, tiled=True).astype(F32)
        total = self.kept
        if after is not None:
            total, _ = tie(total, after)
        total = total.astype(F32)
        for part in self.came:
            total = total + part.astype(F32)
        self.kept = total
        return total

    def before(self, value):
        if not self.routed:
            return value
        value, self.kept, self.away = tie(value, self.kept, self.away)
        return value


def product_of(left, right):
    def product(at, count, after):
        held = left if after is None else tie(left, after)[0]
        return weight_product(lax.dynamic_slice_in_dim(held, at, count, axis=1), right)

    return product


SPAN = 128


def windows(rows):
    for pair in range(rows // (2 * VIS)):
        start = min(2 * VIS * pair // 16 * 16, rows - SPAN)
        yield start, 2 * VIS * pair - start


def same_image(offset):
    key = lax.broadcasted_iota(jnp.int32, (SPAN, SPAN), 0) - offset
    query = lax.broadcasted_iota(jnp.int32, (SPAN, SPAN), 1) - offset
    inside = (key >= 0) & (key < 2 * VIS)
    match = inside & (query >= 0) & (query < 2 * VIS) & ((key >= VIS) == (query >= VIS))
    weight = match.astype(F32)
    return jnp.concatenate([weight, weight], axis=1) > 0.5, inside


def head_lanes():
    lane = lax.broadcasted_iota(jnp.int32, (SPAN, SPAN), 1)
    low = (lane < HDIM).astype(F32)
    return low.astype(BF), (1.0 - low).astype(BF), lane < HDIM


def nt(left, right):
    return lax.dot_general(left, right, (((1,), (1,)), ((), ())), preferred_element_type=F32)


def tn(left, right):
    return lax.dot_general(left, right, (((0,), (0,)), ((), ())), preferred_element_type=F32)


SCALE = HDIM ** (-0.5)


def attend_kernel(q_ref, k_ref, v_ref, mix_ref, peak_ref):
    low, high, is_low = head_lanes()
    low, high = low * SCALE, high * SCALE
    for number, (start, offset) in enumerate(windows(mix_ref.shape[0])):
        rows = pl.ds(start, SPAN)
        match, inside = same_image(offset)
        q_win = q_ref[rows, :]
        q_two = jnp.concatenate([q_win * low, q_win * high], axis=0)
        scores = jnp.where(match, nt(k_ref[rows, :], q_two), -1e30)
        peak = jnp.max(scores, axis=0, keepdims=True)
        grown = jnp.exp(scores - peak)
        total = jnp.sum(grown, axis=0, keepdims=True)
        probs = (grown * (1.0 / total)).astype(BF)
        peak_ref[0, number : number + 1, :] = peak + jnp.log(total)
        both = tn(probs, v_ref[rows, :])
        mixed = jnp.where(is_low, both[:SPAN], both[SPAN:])
        held = mix_ref[rows, :].astype(F32)
        mix_ref[rows, :] = jnp.where(inside, mixed, held).astype(BF)


def attend(projected):
    rows = projected.shape[0]
    pairs = HEADS // 2
    count = rows // (2 * VIS)
    block = lambda shift: pl.BlockSpec((rows, SPAN), lambda i: (0, i + shift))
    return pl.pallas_call(
        attend_kernel,
        grid=(pairs,),
        in_specs=[block(0), block(pairs), block(2 * pairs)],
        out_specs=[block(0), pl.BlockSpec((1, count, 2 * SPAN), lambda i: (i, 0, 0))],
        out_shape=[
            jax.ShapeDtypeStruct((rows, D), BF),
            jax.ShapeDtypeStruct((pairs, count, 2 * SPAN), F32),
        ],
        compiler_params=pltpu.CompilerParams(vmem_limit_bytes=32 * 2**20),
        cost_estimate=pl.CostEstimate(
            flops=4 * rows * SPAN * D, bytes_accessed=8 * rows * D, transcendentals=rows * SPAN * HEADS
        ),
        name="attend",
    )(projected, projected, projected)


def attend_back_kernel(q_ref, k_ref, v_ref, mix_ref, peak_ref, grad_ref, sums_ref):
    at = pl.program_id(0) * SPAN
    low, high, is_low = head_lanes()
    q_sum = jnp.zeros((1, SPAN), F32)
    v_sum = jnp.zeros((1, SPAN), F32)

    def put(rows, shift, value, inside):
        cols = pl.ds(pl.multiple_of(at + shift * D, SPAN), SPAN)
        held = grad_ref[rows, cols].astype(F32)
        grad_ref[rows, cols] = jnp.where(inside, value, held).astype(BF)

    for number, (start, offset) in enumerate(windows(q_ref.shape[0])):
        rows = pl.ds(start, SPAN)
        match, inside = same_image(offset)
        q_win, k_win, v_win, mix_win = q_ref[rows, :], k_ref[rows, :], v_ref[rows, :], mix_ref[rows, :]
        q_win = q_win * SCALE
        q_two = jnp.concatenate([q_win * low, q_win * high], axis=0)
        mix_two = jnp.concatenate([mix_win * low, mix_win * high], axis=0)
        scores = nt(k_win, q_two) - peak_ref[0, number : number + 1, :]
        probs = jnp.exp(jnp.where(match, scores, -1e30))
        probs_low = probs.astype(BF)
        v_grad = jnp.dot(probs_low, mix_two, preferred_element_type=F32)
        probs_grad = nt(v_win, mix_two)
        inner = jnp.sum(probs_grad * probs, axis=0, keepdims=True)
        score = (probs * (probs_grad - inner)).astype(BF)
        k_grad = jnp.dot(score, q_two, preferred_element_type=F32)
        q_both = tn(score, k_win * SCALE)
        q_grad = jnp.where(is_low, q_both[:SPAN], q_both[SPAN:])
        put(rows, 0, q_grad, inside)
        put(rows, 1, k_grad, inside)
        put(rows, 2, v_grad, inside)
        q_sum += jnp.sum(jnp.where(inside, q_grad, 0.0), axis=0, keepdims=True)
        v_sum += jnp.sum(jnp.where(inside, v_grad, 0.0), axis=0, keepdims=True)
    sums_ref[...] = jnp.concatenate([q_sum, v_sum, jnp.zeros((6, SPAN), F32)], axis=0)


def attend_back(projected, mixture_grad, peaks):
    rows = projected.shape[0]
    pairs = HEADS // 2
    count = rows // (2 * VIS)
    block = lambda shift: pl.BlockSpec((rows, SPAN), lambda i: (0, i + shift))
    return pl.pallas_call(
        attend_back_kernel,
        grid=(pairs,),
        in_specs=[
            block(0),
            block(pairs),
            block(2 * pairs),
            block(0),
            pl.BlockSpec((1, count, 2 * SPAN), lambda i: (i, 0, 0)),
        ],
        out_specs=[
            pl.BlockSpec((rows, 3 * D), lambda i: (0, 0)),
            pl.BlockSpec((8, SPAN), lambda i: (0, i)),
        ],
        out_shape=[
            jax.ShapeDtypeStruct((rows, 3 * D), BF),
            jax.ShapeDtypeStruct((8, D), F32),
        ],
        compiler_params=pltpu.CompilerParams(vmem_limit_bytes=40 * 2**20),
        cost_estimate=pl.CostEstimate(
            flops=10 * rows * SPAN * D, bytes_accessed=14 * rows * D, transcendentals=rows * SPAN * HEADS
        ),
        name="attend_back",
    )(projected, projected, projected, mixture_grad, peaks)


TAIL_STEP = 0.33
TAIL = (
    0.18636611813641438,
    0.1828371164957563,
    0.20192458123233548,
    0.04500824941716716,
    0.41254593072161144,
    -0.3554434272669394,
    0.46269071975152953,
    -0.1359293701595944,
)


def gelu_and_slope(x):
    t = 1.0 / (1.0 + (TAIL_STEP * 0.7071067811865476) * jnp.abs(x))
    bell = jnp.exp(-0.5 * x * x)
    tail = jnp.full_like(x, 0.5 * TAIL[-1])
    for factor in TAIL[-2::-1]:
        tail = tail * t + 0.5 * factor
    tail = tail * t * bell
    normal = jnp.where(x >= 0.0, 1.0 - tail, tail)
    return x * normal, normal + x * bell * 0.3989422804014327


UP_TILE = 512


def expand_kernel(x_ref, w_ref, bias_ref, act_ref, slope_ref):
    preact = jnp.dot(x_ref[...], w_ref[...], preferred_element_type=F32) + bias_ref[...]
    activated, slope = gelu_and_slope(preact)
    act_ref[...] = activated.astype(BF)
    slope_ref[...] = slope.astype(slope_ref.dtype)


def expand(x, weight_all, first_column, bias):
    rows = x.shape[0]
    shift = first_column // UP_TILE
    tile = pl.BlockSpec((rows, UP_TILE), lambda i: (0, i))
    return pl.pallas_call(
        expand_kernel,
        grid=(FF // UP_TILE,),
        in_specs=[
            pl.BlockSpec((rows, D), lambda i: (0, 0)),
            pl.BlockSpec((D, UP_TILE), lambda i: (0, i + shift)),
            pl.BlockSpec((1, UP_TILE), lambda i: (0, i)),
        ],
        out_specs=[tile, tile],
        out_shape=[jax.ShapeDtypeStruct((rows, FF), BF), jax.ShapeDtypeStruct((rows, FF), BF)],
        compiler_params=pltpu.CompilerParams(vmem_limit_bytes=40 * 2**20),
        cost_estimate=pl.CostEstimate(
            flops=2 * rows * D * FF, bytes_accessed=2 * D * FF + 4 * rows * FF, transcendentals=2 * rows * FF
        ),
        name="expand",
    )(x, weight_all, bias.reshape(1, FF))


def local(
    pixels,
    visible,
    scale_index,
    cotangent,
    pe_weight,
    pe_first,
    pe_second,
    qkv_weight,
    qkv_first,
    qkv_second,
    out_weight,
    out_first,
    out_second,
    up_weight,
    up_first,
    up_second,
    down_weight,
    down_first,
    down_second,
    dec_weight,
    dec_first,
    dec_second,
    vectors,
    vec_first,
    vec_second,
):
    image_count = pixels.shape[0]
    row_count = image_count * VIS
    device_count = lax.axis_size(AXES)
    dp_count = lax.axis_size("dp")
    shard_rows = D // device_count
    routed = dp_count == 16 and device_count == 32
    item_count = 4 * image_count // dp_count
    whole_images = item_count % 4 == 0

    pixel_rows = pixels.astype(F32).reshape(row_count, BANDS, PATCH * PATCH)
    late = jnp.concatenate([up_weight, down_weight.T, out_weight.T, dec_weight], axis=1).astype(BF)
    late_full = lax.all_gather(late, AXES, axis=0, tiled=True)
    sent_images = max(image_count // dp_count, 1)
    if routed:
        vec_length = vectors.shape[0]
        vec_low = jnp.pad(vectors.astype(BF), (0, 4 * SPAN - vec_length)).reshape(4, SPAN)
        vec_low = jnp.pad(vec_low, ((0, shard_rows - 4), (0, 0)))
        pe_shard = jnp.concatenate([pe_weight.T.astype(BF), vec_low], axis=1)
        pe_gather = Gathering(tie(pe_shard, late)[0], True)
        qkv_gather = Gathering(tie(qkv_weight.astype(BF), late)[0], False)
    band_sum = jnp.sum(pixel_rows, axis=(0, 2))
    band_square = jnp.sum(pixel_rows * pixel_rows, axis=(0, 2))
    stats = jnp.concatenate([band_sum, band_square])
    cotangent_rows = cotangent[0]
    if routed:
        pe_gather.first_turn(stats)
        stats = tie(stats, pe_gather.held)[0]
    if whole_images:
        marks = jnp.concatenate([visible, scale_index[:, None]], axis=1).astype(F32)
        marks = marks.reshape(dp_count, sent_images * (VIS + 1))
        marks = jnp.concatenate(
            [marks, jnp.broadcast_to(stats[None], (dp_count, 2 * BANDS))], axis=1
        )
        marks_in = lax.all_to_all(marks, "dp", split_axis=0, concat_axis=0, tiled=True)
        stats = jnp.sum(marks_in[:, -2 * BANDS :], axis=0)
        stats = stats + lax.ppermute(stats, "grp", core_pairs())
    else:
        stats = lax.psum(stats, AXES)
    spots = visible.reshape(row_count)
    scale_rows = jnp.repeat(scale_index, VIS)
    if routed:
        qkv_gather.middle(stats)
        pe_gather.second_turn(qkv_gather.held)
        spots, scale_rows, cotangent_rows, marks_in = tie(
            spots, scale_rows, cotangent_rows, marks_in, pe_gather.held
        )[:4]
    else:
        early = jnp.concatenate([pe_weight.T, qkv_weight], axis=1).astype(BF)
        early_full = lax.all_gather(early, AXES, axis=0, tiled=True)
        pe_full, qkv_full = early_full[:, :PIX], early_full[:, PIX:]
        vector_all = lax.all_gather(vectors.astype(BF), AXES, axis=0, tiled=True)
    up_full, down_full = late_full[:, :FF], late_full[:, FF : 2 * FF]
    out_full, dec_full = late_full[:, 2 * FF : 2 * FF + D], late_full[:, 2 * FF + D :]

    dp_index = lax.axis_index("dp")
    if whole_images:
        image_order = marks_in[:, : -2 * BANDS].astype(jnp.int32)
        image_order = image_order.reshape(dp_count, sent_images, VIS + 1)
        visible_in, scale_in = image_order[:, :, :VIS], image_order[:, :, VIS]
        grids = cotangent_rows.reshape(sent_images, 4, dp_count, QUART, DDEC)
        hot_in = (
            visible_in[..., None] == jnp.arange(GRID).reshape(1, 1, 1, GRID)
        ).astype(BF)
        hot_quarter = hot_in.reshape(dp_count, sent_images, VIS, 4, QUART)
        dy_sent = jnp.einsum(
            "skvqr,kqsrc->skvc", hot_quarter, grids, preferred_element_type=F32
        ).astype(BF)
        dy_rows = lax.all_to_all(
            dy_sent.reshape(image_count, VIS, DDEC), "dp", split_axis=0, concat_axis=0, tiled=True
        )
        dy_rows = dy_rows.reshape(row_count, DDEC)
    if routed:
        qkv_gather.first_turn(dy_sent)
        spots, scale_rows = tie(spots, scale_rows, qkv_gather.held)[:2]
    enc_table = forward_product(angle_hot(spots, scale_rows, 3), angle_pieces(D, 3))
    if routed:
        pe_gather.cores(enc_table)
        first_full = pe_gather.total()
        pe_full = first_full[:, :PIX]
        vector_all = first_full[:, PIX:].reshape(device_count, shard_rows, SPAN)[:, :4]
        vector_all = vector_all.reshape(device_count, 4 * SPAN)[:, :vec_length].reshape(-1)
        qkv_gather.second_turn(first_full)

    entry_count = row_count * device_count * PATCH * PATCH
    band_mean = stats[:BANDS] / entry_count
    band_scale = lax.rsqrt(stats[BANDS:] / entry_count - band_mean * band_mean + EPS_NORM)
    pixel_norm = (pixel_rows - band_mean[None, :, None]) * band_scale[None, :, None]
    pixel_low = pixel_norm.reshape(row_count, PIX).astype(BF)
    pieces, up_bias, dec_bias = split_vectors(vector_all.astype(F32))
    (
        gain_one,
        shift_one,
        gain_two,
        shift_two,
        pe_bias,
        query_bias,
        value_bias,
        out_bias,
        down_bias,
        mask_token,
    ) = pieces

    if whole_images:
        vacant_in = 1.0 - jnp.sum(hot_quarter.astype(F32), axis=2)
        dy_all = jnp.sum(cotangent_rows.astype(F32), axis=(0, 1, 2))
        dy_vacant = jnp.einsum(
            "skqr,kqsrc->c", vacant_in.astype(BF), grids, preferred_element_type=F32
        )

    stream_in = back_product(pixel_low, pe_full) + pe_bias + enc_table
    norm_out_one, normed_one, inv_std_one = norm_forward(stream_in, gain_one, shift_one)
    norm_one = norm_out_one.astype(BF)
    if routed:
        qkv_gather.cores(tie(dy_rows, norm_one)[0])
        qkv_full = qkv_gather.total()
    projected = forward_product(norm_one, qkv_full) + jnp.concatenate(
        [query_bias, jnp.zeros_like(query_bias), value_bias]
    )
    projected = projected.astype(BF)
    mixture_low, peaks = attend(projected)
    stream_mid = stream_in + back_product(mixture_low, out_full) + out_bias
    norm_out_two, normed_two, inv_std_two = norm_forward(stream_mid, gain_two, shift_two)
    norm_two = norm_out_two.astype(BF)
    if whole_images:
        out_low = back_product(dy_rows, dec_full).astype(BF)
        dec_bias_grad = dy_all
        vacant_parts = []
        rest = dy_vacant
        for _ in range(3):
            part = lax.reduce_precision(rest, 8, 7)
            vacant_parts.append(part)
            rest = rest - part
        vacant_low = jnp.stack(vacant_parts).astype(BF)
        mask_grad = jnp.sum(back_product(vacant_low, dec_full), axis=0)
    else:
        placement = visible[:, :, None] == jnp.arange(GRID)[None, None, :]
        placement_low = placement.astype(BF)
        vacant = 1.0 - jnp.sum(placement.astype(F32), axis=1)
        grad_rows = cotangent[0].reshape(-1, DDEC)
        dec_bias_grad = jnp.sum(grad_rows.astype(F32), axis=0)
        grid_grad = (
            back_product(grad_rows, dec_full).astype(BF).reshape(item_count, dp_count, QUART, D)
        )
        returned = lax.all_to_all(
            grid_grad, "dp", split_axis=1, concat_axis=0, tiled=True
        ).reshape(image_count, GRID, D)
        out_low = jnp.einsum(
            "nvg,ngd->nvd", placement_low, returned, preferred_element_type=F32
        )
        out_low = out_low.reshape(row_count, D).astype(BF)
        mask_grad = jnp.einsum(
            "ng,ngd->d", vacant.astype(BF), returned, preferred_element_type=F32
        )
    out_grad_rows = out_low.astype(F32)

    activated, slope = expand(norm_two, late_full, 0, up_bias)
    down_part = Reduction(product_of(out_low, activated), routed).cores(slope)
    out_rows_after = down_part.before(out_low)
    preact_grad = forward_product(out_rows_after, down_full) * slope.astype(F32)
    up_bias_grad = jnp.sum(preact_grad, axis=0)
    preact_low = preact_grad.astype(BF)
    down_part.first_turn(preact_low)
    activated = down_part.before(activated)
    stream_out = stream_mid + back_product(activated, down_full) + down_bias
    stream_low = stream_out.astype(BF)

    if whole_images:
        dec_product = product_of(stream_low, dy_rows)

        def dec_rows_at(at, count, after):
            token = lax.dynamic_slice_in_dim(mask_token, at, count)
            return dec_product(at, count, after) + token[:, None] * dy_vacant[None, :]

    else:
        full_grid = jnp.einsum(
            "nvg,nvd->ngd",
            placement_low,
            stream_low.reshape(image_count, VIS, D),
            preferred_element_type=F32,
        )
        full_grid = (full_grid + vacant[:, :, None] * mask_token).astype(BF)
        quarters = full_grid.reshape(4 * image_count, 1, QUART, D)
        ratio_image = jnp.power(2.0, scale_index.astype(F32) - 1.0)
        ratio_quarter = jnp.repeat(ratio_image, 4).reshape(4 * image_count, 1).astype(BF)
        received = lax.all_to_all(quarters, "dp", split_axis=0, concat_axis=1, tiled=True)
        received_ratio = lax.all_to_all(
            ratio_quarter, "dp", split_axis=0, concat_axis=1, tiled=True
        )
        quarter_id = dp_index * item_count + jnp.arange(item_count)
        position = (quarter_id % 4)[:, None] * QUART + jnp.arange(QUART)[None, :]
        scale_at = jnp.round(jnp.log2(received_ratio.astype(F32))).astype(jnp.int32) + 1
        full = (item_count, dp_count, QUART)
        dec_table = forward_product(
            angle_hot(
                jnp.broadcast_to(position[:, None, :], full).reshape(-1),
                jnp.broadcast_to(scale_at[:, :, None], full).reshape(-1),
                2,
            ),
            angle_pieces(DDEC, 2),
        ).reshape(full + (DDEC,))
        decoded_rows = jnp.dot(received, dec_full, preferred_element_type=F32)
        decoded = (decoded_rows + dec_bias + dec_table).astype(BF)[None]
        dec_rows_at = product_of(received.reshape(-1, D), grad_rows)

    down_bias_grad = jnp.sum(out_grad_rows, axis=0)
    up_part = Reduction(product_of(norm_two, preact_low), routed).cores(stream_low)
    two_grad = back_product(up_part.before(preact_low), up_full)
    mid_grad, gain_two_grad, shift_two_grad = norm_backward(
        two_grad, normed_two, inv_std_two, gain_two
    )
    mid_grad = mid_grad + out_grad_rows
    mid_low = mid_grad.astype(BF)
    out_bias_grad = jnp.sum(mid_grad, axis=0)
    up_part.first_turn(mid_low)
    down_part.second_turn(mid_low)
    mid_after = down_part.before(up_part.before(mid_low))
    mixture_grad = forward_product(mid_after, out_full).astype(BF)
    projected_low, attend_sums = attend_back(projected, mixture_grad, peaks)
    query_bias_grad, value_bias_grad = attend_sums[0], attend_sums[1]
    down_part.along_z(projected_low)
    out_product, qkv_product = product_of(mid_low, mixture_low), product_of(norm_one, projected_low)
    qkv_part = Reduction(
        lambda at, count, after: jnp.concatenate(
            [out_product(at, count, after), qkv_product(at, count, after)], axis=1
        ),
        routed,
    )
    qkv_part.cores(projected_low)
    up_part.second_turn(projected_low)
    projected_after = up_part.before(qkv_part.before(down_part.before(projected_low)))
    one_grad = back_product(projected_after, qkv_full)
    in_grad, gain_one_grad, shift_one_grad = norm_backward(
        one_grad, normed_one, inv_std_one, gain_one
    )
    in_grad = in_grad + mid_grad
    pe_bias_grad = jnp.sum(in_grad, axis=0)
    in_low = in_grad.astype(BF)
    qkv_part.first_turn(in_low)
    down_shard = down_part.total(in_low)
    up_part.along_z(down_shard)
    in_after = up_part.before(qkv_part.before(in_low))
    vec_grad = jnp.concatenate(
        [
            gain_one_grad,
            shift_one_grad,
            gain_two_grad,
            shift_two_grad,
            pe_bias_grad,
            query_bias_grad,
            value_bias_grad,
            out_bias_grad,
            down_bias_grad,
            mask_grad,
            up_bias_grad,
            dec_bias_grad,
        ]
    )
    pe_product = product_of(in_after, pixel_low)
    if routed:
        vec_rows = jnp.pad(
            vec_grad.reshape(device_count, vec_length), ((0, 0), (0, 4 * SPAN - vec_length))
        ).reshape(device_count, 4, SPAN)
        vec_rows = jnp.pad(vec_rows, ((0, 0), (0, shard_rows - 4), (0, 0))).reshape(D, SPAN)
        pe_part = Reduction(
            lambda at, count, after: jnp.concatenate(
                [
                    pe_product(at, count, after),
                    lax.dynamic_slice_in_dim(vec_rows, at, count),
                    dec_rows_at(at, count, after),
                ],
                axis=1,
            ),
            routed,
        )
    else:
        pe_part = Reduction(
            lambda at, count, after: jnp.concatenate(
                [pe_product(at, count, after), dec_rows_at(at, count, after)], axis=1
            ),
            routed,
        )
    pe_part.cores(in_after)
    in_after = pe_part.before(in_after)
    if whole_images:
        stream_late = tie(stream_low, in_after)[0]
        dec_pieces = angle_pieces(DDEC, 2)
        vis_table = forward_product(angle_hot(spots, scale_rows, 2), dec_pieces)
        vis_rows = (forward_product(stream_late, dec_full) + dec_bias + vis_table).astype(BF)
        vis_in = lax.all_to_all(
            vis_rows.reshape(image_count, VIS, DDEC), "dp", split_axis=0, concat_axis=0, tiled=True
        ).reshape(dp_count, sent_images, VIS, DDEC)
        placed = jnp.einsum(
            "skvqr,skvc->kqsrc", hot_quarter, vis_in, preferred_element_type=F32
        )
        position = jnp.arange(GRID)
        every_hot = angle_hot(
            jnp.tile(position, dp_count * sent_images),
            jnp.repeat(scale_in.reshape(-1), GRID),
            2,
        ).reshape(dp_count, sent_images, 4, QUART, -1)
        every_table = jnp.einsum(
            "skqrt,tc->kqsrc", every_hot, dec_pieces, preferred_element_type=F32
        )
        mask_rows = forward_product(jnp.broadcast_to(mask_token.astype(BF), (8, D)), dec_full)[0]
        empty = vacant_in.transpose(1, 2, 0, 3)[..., None] > 0.5
        decoded = jnp.where(empty, every_table + (mask_rows + dec_bias), placed)
        decoded = decoded.astype(BF).reshape(1, item_count, dp_count, QUART, DDEC)
    norm_grad = forward_product(in_after, pe_full)
    pe_part.first_turn(norm_grad)
    norm_grad = pe_part.before(norm_grad).reshape(row_count, BANDS, PATCH * PATCH)
    pixel_grad = (norm_grad * band_scale[None, :, None]).reshape(image_count, VIS, PIX)
    up_shard = up_part.total(pixel_grad)
    qkv_part.second_turn_with(pe_part, up_shard).along_z(up_shard)
    last_total = qkv_part.total()
    out_shard, qkv_shard = last_total[:, :D], last_total[:, D : 4 * D]
    pe_shard, dec_shard = last_total[:, 4 * D : 4 * D + PIX], last_total[:, -DDEC:]
    if routed:
        vec_shard = last_total[:4, 4 * D + PIX : 4 * D + PIX + SPAN].reshape(-1)[:vec_length]
    else:
        vec_shard = lax.psum_scatter(vec_grad, AXES, scatter_dimension=0, tiled=True)
    shards = (pe_shard, qkv_shard, out_shard, up_shard, down_shard, dec_shard, vec_shard)
    local_squares = sum((jnp.sum(gradient * gradient) for gradient in shards))
    squares = tiny_sum(local_squares.reshape(1), routed)[0]
    grad_norm = jnp.sqrt(squares)
    clip_factor = jnp.minimum(1.0, CLIP_LEVEL / grad_norm)
    params = (pe_weight, qkv_weight, out_weight, up_weight, down_weight, dec_weight, vectors)
    firsts = (pe_first, qkv_first, out_first, up_first, down_first, dec_first, vec_first)
    seconds = (pe_second, qkv_second, out_second, up_second, down_second, dec_second, vec_second)
    results = []
    for number in range(7):
        step_rate = LR_VECTOR if number == 6 else LR_MATRIX
        decay_rate = 0.0 if number == 6 else DECAY_MATRIX
        gradient = shards[number].T if number in (0, 2, 4) else shards[number]
        results.extend(
            adamw_update(
                params[number],
                firsts[number],
                seconds[number],
                gradient * clip_factor,
                step_rate,
                decay_rate,
            )
        )
    return (decoded, pixel_grad, *results, grad_norm)


def solution(mesh):
    rows = P(AXES, None)
    cols = P(None, AXES)
    vecs = P(AXES)
    images = P(AXES, None, None)
    grids = P("grp", "dp", None, None, None)
    states = (cols,) * 3 + (rows,) * 3 + (cols,) * 3 + (rows,) * 3 + (cols,) * 3 + (rows,) * 3
    states = states + (vecs,) * 3
    return jax.shard_map(
        local,
        mesh=mesh,
        in_specs=(images, rows, vecs, grids) + states,
        out_specs=(grids, images) + states + (P(),),
        check_vma=False,
    )
```

```python
import functools

import jax
import jax.numpy as jnp
import ml_dtypes
import numpy as np
from jax import lax
from jax.experimental import pallas as pl
from jax.experimental.pallas import tpu as pltpu
from jax.sharding import PartitionSpec as P

D = 1024
FF = 4096
HEADS = 16
HDIM = 64
DDEC = 512
PATCH = 16
SIDE = 14
BANDS = 3
STEP = 10
PIX = 768
GRID = 196
VIS = 49
QUART = 49
NSCALE = 4
AXES = ("grp", "dp")
HALF = D // 2
BF = jnp.bfloat16
F32 = jnp.float32

EPS_NORM = 1e-05
BETA_ONE = 0.9
BETA_TWO = 0.95
ADAM_EPS = 1e-08
LR_MATRIX = 0.08
LR_VECTOR = 0.3
DECAY_MATRIX = 0.05
CLIP_LEVEL = 1.0


def forward_product(left, right):
    return jnp.dot(left, right, preferred_element_type=F32)


def back_product(left, right):
    return lax.dot_general(left, right, (((1,), (1,)), ((), ())), preferred_element_type=F32)


def weight_product(left, right):
    return lax.dot_general(left, right, (((0,), (0,)), ((), ())), preferred_element_type=F32)


def angle_pieces(channels, pieces):
    quarter = channels // 4
    step = np.float32(-np.log(np.float32(10000.0))) / np.float32(quarter)
    frequency = np.exp(np.arange(quarter, dtype=np.float32) * step)
    ratio = np.float32(2.0) ** (np.arange(NSCALE, dtype=np.float32) - 1)
    spot = np.arange(SIDE, dtype=np.float32)
    angle = (ratio[:, None] * spot[None, :]).reshape(-1, 1) * frequency[None, :]
    half = np.concatenate([np.sin(angle.astype(np.float64)), np.cos(angle.astype(np.float64))], 1)
    zeros = np.zeros_like(half)
    rest = np.concatenate(
        [np.concatenate([half, zeros], 1), np.concatenate([zeros, half], 1)], 0
    ).astype(np.float32)
    cut = []
    for _ in range(pieces):
        part = rest.astype(ml_dtypes.bfloat16)
        cut.append(part)
        rest = rest - part.astype(np.float32)
    return jnp.asarray(np.concatenate(cut, 0))


def angle_hot(spots, scale_rows, pieces):
    row_at = scale_rows * SIDE + spots // SIDE
    col_at = (NSCALE + scale_rows) * SIDE + spots % SIDE
    slot = jnp.arange(2 * NSCALE * SIDE)[None, :]
    hot = ((slot == row_at[:, None]) | (slot == col_at[:, None])).astype(BF)
    return jnp.concatenate([hot] * pieces, axis=1)


def split_vectors(vector_all):
    pieces = tuple((vector_all[number * D : (number + 1) * D] for number in range(10)))
    return (pieces, vector_all[10 * D : 10 * D + FF], vector_all[10 * D + FF :])


def halves(array):
    return (array[..., :HALF], array[..., HALF:])


def row_mean(pair):
    return sum(jnp.sum(part, axis=-1, keepdims=True) for part in pair) * (1.0 / D)


def norm_forward(hidden_in, norm_gain, norm_shift):
    mean = row_mean(hidden_in)
    center = [part - mean for part in hidden_in]
    inv_std = lax.rsqrt(row_mean([part * part for part in center]) + EPS_NORM)
    normed = [part * inv_std for part in center]
    low = [
        (part * gain + shift).astype(BF) for part, gain, shift in zip(normed, norm_gain, norm_shift)
    ]
    return (low, normed, inv_std)


def norm_backward(grad_out, normed, inv_std, norm_gain):
    scaled = [part * gain for part, gain in zip(grad_out, norm_gain)]
    mean = row_mean(scaled)
    along = row_mean([part * unit for part, unit in zip(scaled, normed)])
    inner = [(part - mean - unit * along) * inv_std for part, unit in zip(scaled, normed)]
    gain_grad = [jnp.sum(part * unit, axis=0) for part, unit in zip(grad_out, normed)]
    return (inner, gain_grad, [jnp.sum(part, axis=0) for part in grad_out])


def inward(pair, weights, first, count):
    return sum(
        forward_product(part, weight[:, first : first + count]) for part, weight in zip(pair, weights)
    )


def outward(left, weights, first, count):
    return [back_product(left, weight[:, first : first + count]) for weight in weights]


def adamw_update(weight, moment_one, moment_two, gradient, step_rate, decay_rate):
    new_one = BETA_ONE * moment_one + (1.0 - BETA_ONE) * gradient
    new_two = BETA_TWO * moment_two + (1.0 - BETA_TWO) * gradient * gradient
    fixed_one = new_one / (1.0 - BETA_ONE**STEP)
    fixed_two = new_two / (1.0 - BETA_TWO**STEP)
    new_weight = weight - step_rate * (
        fixed_one / (jnp.sqrt(fixed_two) + ADAM_EPS) + decay_rate * weight
    )
    return (new_one, new_two, new_weight)


def core_pairs():
    return [(0, 1), (1, 0)]


def dp_pairs(bits):
    return [(i, i ^ bits) for i in range(16)]


def turn_pairs(core_zero, core_one):
    return [(g * 16 + i, g * 16 + (i ^ (core_one if g else core_zero))) for g in range(2) for i in range(16)]


def tiny_sum(value, routed):
    if not routed:
        return lax.psum(value, AXES)
    for unit in (1, 4):
        one, two, three = [lax.ppermute(value, "dp", dp_pairs(unit * k)) for k in (1, 2, 3)]
        value = (value + one) + (two + three)
    return value + lax.ppermute(value, "grp", core_pairs())


class Order:
    def __init__(self, token):
        self.token = token

    def __call__(self, *values):
        *values, self.token = lax.optimization_barrier((*values, self.token))
        return values[0] if len(values) == 1 else values


def spot_of_chip():
    chip = lax.axis_index("dp")
    return lax.axis_index("grp"), chip % 2, (chip // 2) % 2, chip // 4


def block_order():
    core, x, y, z = spot_of_chip()
    place = jnp.arange(32)
    far, turn_one, turn_two, step = place // 16, (place // 8) % 2, (place // 4) % 2, place % 4
    at_core = core ^ far
    at_x = x ^ jnp.where(at_core == 0, turn_one, turn_two)
    at_y = y ^ jnp.where(at_core == 0, turn_two, turn_one)
    owner = at_core * 16 + (z ^ step) * 4 + at_y * 2 + at_x
    return (owner[:, None] == jnp.arange(32)[None, :]).astype(BF)


class Gathering:
    def __init__(self, shard, direct, order):
        self.order = order
        self.held = order(shard)
        steps = (1, 2, 3) if direct else (1,)
        self.near = [lax.ppermute(self.held, "dp", dp_pairs(4 * k)) for k in steps]

    def grow(self):
        held = self.order(self.held)
        self.held = self.order(jnp.concatenate([held] + self.near))
        return self.held

    def middle(self):
        self.near = [lax.ppermute(self.grow(), "dp", dp_pairs(8))]

    def first_turn(self):
        self.near = [lax.ppermute(self.grow(), AXES, turn_pairs(2, 1))]

    def second_turn(self):
        self.near = [lax.ppermute(self.grow(), AXES, turn_pairs(1, 2))]

    def cores(self):
        self.near = [lax.ppermute(self.grow(), "grp", core_pairs())]

    def total(self):
        return (self.held, self.near[0])


class Reduction:
    def __init__(self, product, routed, order):
        self.product, self.routed, self.order = product, routed, order

    def cores(self):
        if self.routed:
            away = self.order(self.product(1, None))
            self.came = lax.ppermute(away, "grp", core_pairs())

    def first_turn(self):
        if self.routed:
            self.kept, away = self.order(*self.product(0, self.came))
            self.came = lax.ppermute(away, AXES, turn_pairs(1, 2))

    def sum_of(self, first, count):
        part = self.kept[first : first + count].astype(F32)
        return (part + self.came[first : first + count].astype(F32)).astype(BF)

    def second_turn(self):
        if self.routed:
            self.kept = self.order(self.kept)
            half = HALF // 4
            away, self.kept = self.order(self.sum_of(half, half), self.sum_of(0, half))
            self.came = lax.ppermute(away, AXES, turn_pairs(2, 1))

    def along_z(self):
        if self.routed:
            self.kept = self.order(self.kept)
            parts = self.order(*[self.sum_of(32 * k, 32) for k in range(4)])
            self.kept = parts[0]
            self.came = [lax.ppermute(parts[k], "dp", dp_pairs(4 * k)) for k in (1, 2, 3)]

    def join(self, other):
        if self.routed:
            self.came = jnp.concatenate([self.came, other.came], axis=-1)
            self.kept = jnp.concatenate([self.kept, other.kept], axis=-1)
        else:
            mine, theirs = self.product, other.product
            self.product = lambda *at: jnp.concatenate([mine(*at), theirs(*at)], axis=1)

    def total(self):
        if not self.routed:
            full = jnp.concatenate([self.product(half, None) for half in range(2)])
            half = lax.psum_scatter(full, "grp", scatter_dimension=0, tiled=True)
            return lax.psum_scatter(half, "dp", scatter_dimension=0, tiled=True).astype(F32)
        total = self.order(self.kept).astype(F32)
        for part in self.came:
            total = total + part.astype(F32)
        return self.order(total)


WEIGHT_TILE = 1024


def weight_kernel(edges, added, *refs):
    tile = pl.program_id(0)
    sides = refs[: 2 * len(edges)]
    outs = refs[2 * len(edges) + added :]
    first = 0
    for number, last in enumerate(edges):

        @pl.when((tile >= first) & (tile < last))
        def _(left=sides[2 * number], right=sides[2 * number + 1]):
            value = tn(left[...], right[...])
            if added:
                value = value + refs[2 * len(edges)][...].astype(F32)
                outs[0][...] = value[: HALF // 2].astype(BF)
                outs[1][...] = value[HALF // 2 :].astype(BF)
            else:
                outs[0][...] = value.astype(BF)

        first = last


def weight_call(pairs, came):
    edges, specs, count = [], [], 0
    for left, right in pairs:
        start, tiles = count, right.shape[1] // WEIGHT_TILE
        count += tiles

        def at(i, start=start, tiles=tiles):
            return (0, jnp.clip(i - start, 0, tiles - 1))

        specs.append(pl.BlockSpec(left.shape, lambda i: (0, 0)))
        specs.append(pl.BlockSpec((right.shape[0], WEIGHT_TILE), at))
        edges.append(count)
    columns = count * WEIGHT_TILE
    sides = [side for pair in pairs for side in pair]
    if came is None:
        shapes = [(HALF, columns)]
    else:
        shapes = [(HALF // 2, columns)] * 2
        sides.append(came)
        specs.append(pl.BlockSpec((HALF, WEIGHT_TILE), lambda i: (0, i)))
    outs = pl.pallas_call(
        functools.partial(weight_kernel, tuple(edges), int(came is not None)),
        grid=(count,),
        in_specs=specs,
        out_specs=[pl.BlockSpec((shape[0], WEIGHT_TILE), lambda i: (0, i)) for shape in shapes],
        out_shape=[jax.ShapeDtypeStruct(shape, BF) for shape in shapes],
        compiler_params=pltpu.CompilerParams(vmem_limit_bytes=40 * 2**20),
        cost_estimate=SMALL,
        name="weight_product",
    )(*sides)
    return outs if came is not None else outs[0]


def product_of(order, *pairs):
    def product(half, came):
        lefts = order(*[left[half] for left, _ in pairs])
        lefts = lefts if len(pairs) > 1 else [lefts]
        return weight_call([(left, right) for left, (_, right) in zip(lefts, pairs)], came)

    return product


def last_kernel(added, in_ref, pixel_ref, vec_ref, stream_ref, dy_ref, token_ref, vacant_ref, *refs):
    outs = refs[added:]
    parts = (
        (0, PIX, tn(in_ref[...], pixel_ref[...])),
        (PIX, SPAN, vec_ref[...]),
        (PIX + SPAN, DDEC, tn(stream_ref[...], dy_ref[...]) + token_ref[...] * vacant_ref[...]),
    )
    for first, count, value in parts:
        cols = pl.ds(first, count)
        if added:
            value = value + refs[0][:, cols].astype(F32)
            outs[0][:, cols] = value[: HALF // 2].astype(BF)
            outs[1][:, cols] = value[HALF // 2 :].astype(BF)
        else:
            outs[0][:, cols] = value.astype(BF)


def last_call(operands, came):
    columns = PIX + SPAN + DDEC
    shapes = [(HALF, columns)] if came is None else [(HALF // 2, columns)] * 2
    extra = [] if came is None else [came]
    outs = pl.pallas_call(
        functools.partial(last_kernel, len(extra)),
        out_shape=[jax.ShapeDtypeStruct(shape, BF) for shape in shapes],
        compiler_params=pltpu.CompilerParams(vmem_limit_bytes=40 * 2**20),
        cost_estimate=SMALL,
        name="last_product",
    )(*operands, *extra)
    return outs if came is not None else outs[0]


SPAN = 128
SMALL = pl.CostEstimate(flops=10**6, bytes_accessed=10**5, transcendentals=0)


def windows(rows):
    for pair in range(rows // (2 * VIS)):
        start = min(2 * VIS * pair // 16 * 16, rows - SPAN)
        yield start, 2 * VIS * pair - start


def same_image(offset):
    key = lax.broadcasted_iota(jnp.int32, (SPAN, SPAN), 0) - offset
    query = lax.broadcasted_iota(jnp.int32, (SPAN, SPAN), 1) - offset
    inside = (key >= 0) & (key < 2 * VIS)
    match = inside & (query >= 0) & (query < 2 * VIS) & ((key >= VIS) == (query >= VIS))
    weight = match.astype(F32)
    return jnp.concatenate([weight, weight], axis=1) > 0.5, inside


def head_lanes():
    lane = lax.broadcasted_iota(jnp.int32, (SPAN, SPAN), 1)
    low = (lane < HDIM).astype(F32)
    return low.astype(BF), (1.0 - low).astype(BF), lane < HDIM


def nt(left, right):
    return lax.dot_general(left, right, (((1,), (1,)), ((), ())), preferred_element_type=F32)


def tn(left, right):
    return lax.dot_general(left, right, (((0,), (0,)), ((), ())), preferred_element_type=F32)


SCALE = HDIM ** (-0.5)


def attend_kernel(q_ref, k_ref, v_ref, mix_ref, peak_ref):
    low, high, is_low = head_lanes()
    low, high = low * SCALE, high * SCALE
    for number, (start, offset) in enumerate(windows(mix_ref.shape[0])):
        rows = pl.ds(start, SPAN)
        match, inside = same_image(offset)
        q_win = q_ref[rows, :]
        q_two = jnp.concatenate([q_win * low, q_win * high], axis=0)
        scores = jnp.where(match, nt(k_ref[rows, :], q_two), -1e30)
        peak = jnp.max(scores, axis=0, keepdims=True)
        grown = jnp.exp(scores - peak)
        total = jnp.sum(grown, axis=0, keepdims=True)
        probs = (grown * (1.0 / total)).astype(BF)
        peak_ref[0, number : number + 1, :] = peak + jnp.log(total)
        both = tn(probs, v_ref[rows, :])
        mixed = jnp.where(is_low, both[:SPAN], both[SPAN:])
        held = mix_ref[rows, :].astype(F32)
        mix_ref[rows, :] = jnp.where(inside, mixed, held).astype(BF)


def attend(projected):
    rows = projected.shape[0]
    pairs = HEADS // 2
    count = rows // (2 * VIS)
    block = lambda shift: pl.BlockSpec((rows, SPAN), lambda i: (0, i + shift))
    return pl.pallas_call(
        attend_kernel,
        grid=(pairs,),
        in_specs=[block(0), block(pairs), block(2 * pairs)],
        out_specs=[block(0), pl.BlockSpec((1, count, 2 * SPAN), lambda i: (i, 0, 0))],
        out_shape=[
            jax.ShapeDtypeStruct((rows, D), BF),
            jax.ShapeDtypeStruct((pairs, count, 2 * SPAN), F32),
        ],
        compiler_params=pltpu.CompilerParams(vmem_limit_bytes=32 * 2**20),
        cost_estimate=SMALL,
        name="attend",
    )(projected, projected, projected)


def attend_back_kernel(q_ref, k_ref, v_ref, mix_ref, peak_ref, grad_ref, sums_ref):
    at = pl.program_id(0) * SPAN
    low, high, is_low = head_lanes()
    q_sum = jnp.zeros((1, SPAN), F32)
    v_sum = jnp.zeros((1, SPAN), F32)

    def put(rows, shift, value, inside):
        cols = pl.ds(pl.multiple_of(at + shift * D, SPAN), SPAN)
        held = grad_ref[rows, cols].astype(F32)
        grad_ref[rows, cols] = jnp.where(inside, value, held).astype(BF)

    for number, (start, offset) in enumerate(windows(q_ref.shape[0])):
        rows = pl.ds(start, SPAN)
        match, inside = same_image(offset)
        q_win, k_win, v_win, mix_win = q_ref[rows, :], k_ref[rows, :], v_ref[rows, :], mix_ref[rows, :]
        q_win = q_win * SCALE
        q_two = jnp.concatenate([q_win * low, q_win * high], axis=0)
        mix_two = jnp.concatenate([mix_win * low, mix_win * high], axis=0)
        scores = nt(k_win, q_two) - peak_ref[0, number : number + 1, :]
        probs = jnp.exp(jnp.where(match, scores, -1e30))
        probs_low = probs.astype(BF)
        v_grad = jnp.dot(probs_low, mix_two, preferred_element_type=F32)
        probs_grad = nt(v_win, mix_two)
        inner = jnp.sum(probs_grad * probs, axis=0, keepdims=True)
        score = (probs * (probs_grad - inner)).astype(BF)
        k_grad = jnp.dot(score, q_two, preferred_element_type=F32)
        q_both = tn(score, k_win * SCALE)
        q_grad = jnp.where(is_low, q_both[:SPAN], q_both[SPAN:])
        put(rows, 0, q_grad, inside)
        put(rows, 1, k_grad, inside)
        put(rows, 2, v_grad, inside)
        q_sum += jnp.sum(jnp.where(inside, q_grad, 0.0), axis=0, keepdims=True)
        v_sum += jnp.sum(jnp.where(inside, v_grad, 0.0), axis=0, keepdims=True)
    sums_ref[...] = jnp.concatenate([q_sum, v_sum, jnp.zeros((6, SPAN), F32)], axis=0)


def attend_back(projected, mixture_grad, peaks):
    rows = projected.shape[0]
    pairs = HEADS // 2
    count = rows // (2 * VIS)
    block = lambda shift: pl.BlockSpec((rows, SPAN), lambda i: (0, i + shift))
    return pl.pallas_call(
        attend_back_kernel,
        grid=(pairs,),
        in_specs=[
            block(0),
            block(pairs),
            block(2 * pairs),
            block(0),
            pl.BlockSpec((1, count, 2 * SPAN), lambda i: (i, 0, 0)),
        ],
        out_specs=[
            pl.BlockSpec((rows, 3 * D), lambda i: (0, 0)),
            pl.BlockSpec((8, SPAN), lambda i: (0, i)),
        ],
        out_shape=[
            jax.ShapeDtypeStruct((rows, 3 * D), BF),
            jax.ShapeDtypeStruct((8, D), F32),
        ],
        compiler_params=pltpu.CompilerParams(vmem_limit_bytes=40 * 2**20),
        cost_estimate=SMALL,
        name="attend_back",
    )(projected, projected, projected, mixture_grad, peaks)


TAIL_STEP = 0.33
TAIL = (
    0.18636611813641438,
    0.1828371164957563,
    0.20192458123233548,
    0.04500824941716716,
    0.41254593072161144,
    -0.3554434272669394,
    0.46269071975152953,
    -0.1359293701595944,
)


def gelu_and_slope(x):
    t = 1.0 / (1.0 + (TAIL_STEP * 0.7071067811865476) * jnp.abs(x))
    bell = jnp.exp(-0.5 * x * x)
    tail = jnp.full_like(x, 0.5 * TAIL[-1])
    for factor in TAIL[-2::-1]:
        tail = tail * t + 0.5 * factor
    tail = tail * t * bell
    normal = jnp.where(x >= 0.0, 1.0 - tail, tail)
    return x * normal, normal + x * bell * 0.3989422804014327


UP_TILE = 512


def both(near_ref, far_ref, near_w_ref, far_w_ref):
    product = jnp.dot(near_ref[...], near_w_ref[...], preferred_element_type=F32)
    return product + jnp.dot(far_ref[...], far_w_ref[...], preferred_element_type=F32)


def expand_kernel(near_ref, far_ref, near_w_ref, far_w_ref, bias_ref, act_ref, slope_ref):
    preact = both(near_ref, far_ref, near_w_ref, far_w_ref) + bias_ref[...]
    activated, slope = gelu_and_slope(preact)
    act_ref[...] = activated.astype(BF)
    slope_ref[...] = slope.astype(BF)


def shift_kernel(near_ref, far_ref, near_w_ref, far_w_ref, bias_ref, out_ref):
    out_ref[...] = (both(near_ref, far_ref, near_w_ref, far_w_ref) + bias_ref[...]).astype(BF)


def scale_kernel(near_ref, far_ref, near_w_ref, far_w_ref, scale_ref, out_ref):
    out_ref[...] = both(near_ref, far_ref, near_w_ref, far_w_ref) * scale_ref[...]


def slope_kernel(near_ref, far_ref, near_w_ref, far_w_ref, slope_ref, out_ref, sums_ref):
    grad = both(near_ref, far_ref, near_w_ref, far_w_ref) * slope_ref[...].astype(F32)
    out_ref[...] = grad.astype(BF)
    sums_ref[...] = jnp.sum(grad, axis=0, keepdims=True)


def inward_call(kernel, pair, weights, first_column, columns, extra, outs, width=UP_TILE):
    rows = pair[0].shape[0]
    shift = first_column // width
    whole = pl.BlockSpec((rows, HALF), lambda i: (0, 0))
    weight = pl.BlockSpec((HALF, width), lambda i: (0, i + shift))
    tile = lambda array: pl.BlockSpec((array.shape[0], width), lambda i: (0, i))
    return pl.pallas_call(
        kernel,
        grid=(columns // width,),
        in_specs=[whole, whole, weight, weight, tile(extra)],
        out_specs=[tile(out) for out in outs],
        out_shape=outs,
        compiler_params=pltpu.CompilerParams(vmem_limit_bytes=40 * 2**20),
        cost_estimate=SMALL,
        name=kernel.__name__,
    )(*pair, *weights, extra)


def expand(pair, weights, first_column, bias):
    out = jax.ShapeDtypeStruct((pair[0].shape[0], FF), BF)
    return inward_call(expand_kernel, pair, weights, first_column, FF, bias.reshape(1, FF), [out, out])


def sums_kernel(pixel_ref, out_ref):
    sums = [jnp.zeros((1, PIX), F32)] * 2
    for image in range(pixel_ref.shape[0]):
        values = pixel_ref[image].astype(F32)
        sums[0] = sums[0] + jnp.sum(values, axis=0, keepdims=True)
        sums[1] = sums[1] + jnp.sum(values * values, axis=0, keepdims=True)
    out_ref[...] = jnp.concatenate(sums, axis=0)


def column_sums(pixels):
    return pl.pallas_call(
        sums_kernel,
        out_shape=jax.ShapeDtypeStruct((2, PIX), F32),
        compiler_params=pltpu.CompilerParams(vmem_limit_bytes=20 * 2**20),
        cost_estimate=SMALL,
        name="column_sums",
    )(pixels)


def grid_spec():
    return pl.BlockSpec((1, 4, 1, QUART, DDEC), lambda i: (0, 0, i, 0, 0))


def pick_kernel(spot_ref, dy_ref, rows_ref, sums_ref, pieces_ref):
    spot = spot_ref[0]
    rows = jnp.zeros((VIS, DDEC), F32)
    sums = jnp.zeros((8, DDEC), F32)
    for quarter in range(4):
        place = lax.broadcasted_iota(jnp.int32, (VIS, QUART), 1) + quarter * QUART
        hot = (spot == place).astype(F32)
        values = dy_ref[0, quarter, 0]
        rows = rows + jnp.dot(hot.astype(BF), values, preferred_element_type=F32)
        vacant = 1.0 - jnp.sum(hot, axis=0, keepdims=True)
        weights = jnp.concatenate([jnp.ones_like(vacant), vacant, jnp.zeros((6, QUART), F32)], axis=0)
        sums = sums + jnp.dot(weights.astype(BF), values, preferred_element_type=F32)
    rows_ref[0] = rows.astype(BF)

    @pl.when(pl.program_id(0) == 0)
    def _():
        sums_ref[...] = jnp.zeros_like(sums_ref)

    sums_ref[...] += sums

    @pl.when(pl.program_id(0) == pl.num_programs(0) - 1)
    def _():
        rest = sums_ref[1:2]
        pieces = []
        for _ in range(3):
            pieces.append(rest.astype(BF))
            rest = rest - pieces[-1].astype(F32)
        zeros = jnp.zeros((5, DDEC), BF)
        pieces_ref[...] = jnp.concatenate(pieces + [zeros], axis=0)


def pick_rows(visible_in, grids):
    images = visible_in.shape[0]
    return pl.pallas_call(
        pick_kernel,
        grid=(images,),
        in_specs=[pl.BlockSpec((1, VIS, 1), lambda i: (i, 0, 0)), grid_spec()],
        out_specs=[
            pl.BlockSpec((1, VIS, DDEC), lambda i: (i, 0, 0)),
            pl.BlockSpec((8, DDEC), lambda i: (0, 0)),
            pl.BlockSpec((8, DDEC), lambda i: (0, 0)),
        ],
        out_shape=[
            jax.ShapeDtypeStruct((images, VIS, DDEC), BF),
            jax.ShapeDtypeStruct((8, DDEC), F32),
            jax.ShapeDtypeStruct((8, DDEC), BF),
        ],
        compiler_params=pltpu.CompilerParams(vmem_limit_bytes=20 * 2**20),
        cost_estimate=SMALL,
        name="pick_rows",
    )(visible_in[:, :, None], grids)


def place_kernel(scale_ref, spot_ref, rows_ref, table_ref, base_ref, out_ref):
    scale = scale_ref[pl.program_id(0)]
    spot = spot_ref[0]
    for quarter in range(4):
        place = lax.broadcasted_iota(jnp.int32, (QUART, VIS), 0) + quarter * QUART
        hot = (spot == place).astype(F32)
        vacant = jnp.sum(hot, axis=1, keepdims=True) < 0.5
        placed = jnp.dot(hot.astype(BF), rows_ref[0], preferred_element_type=F32)
        slot = lax.broadcasted_iota(jnp.int32, (QUART, 2 * NSCALE * SIDE), 1)
        place = lax.broadcasted_iota(jnp.int32, slot.shape, 0) + quarter * QUART
        line = lax.shift_right_logical(place * 1171, 14)
        row_at = scale * SIDE + line
        col_at = (NSCALE + scale) * SIDE + place - line * SIDE
        angle_at = ((slot == row_at) | (slot == col_at)).astype(F32).astype(BF)
        angle_at = jnp.concatenate([angle_at, angle_at], axis=1)
        empty = jnp.dot(angle_at, table_ref[...], preferred_element_type=F32) + base_ref[...]
        out_ref[0, quarter, 0] = jnp.where(vacant, empty, placed).astype(BF)


def place_rows(visible_in, scale_in, rows, table, base):
    images = visible_in.shape[0]
    return pl.pallas_call(
        place_kernel,
        grid_spec=pltpu.PrefetchScalarGridSpec(
            num_scalar_prefetch=1,
            grid=(images,),
            in_specs=[
                pl.BlockSpec((1, 1, VIS), lambda i, scale: (i, 0, 0)),
                pl.BlockSpec((1, VIS, DDEC), lambda i, scale: (i, 0, 0)),
                pl.BlockSpec(table.shape, lambda i, scale: (0, 0)),
                pl.BlockSpec((1, DDEC), lambda i, scale: (0, 0)),
            ],
            out_specs=pl.BlockSpec((1, 4, 1, QUART, DDEC), lambda i, scale: (0, 0, i, 0, 0)),
        ),
        out_shape=jax.ShapeDtypeStruct((1, 4, images, QUART, DDEC), BF),
        compiler_params=pltpu.CompilerParams(vmem_limit_bytes=20 * 2**20),
        cost_estimate=SMALL,
        name="place_rows",
    )(scale_in, visible_in[:, None, :], rows, table, base)


def local(
    pixels,
    visible,
    scale_index,
    cotangent,
    pe_weight,
    pe_first,
    pe_second,
    qkv_weight,
    qkv_first,
    qkv_second,
    out_weight,
    out_first,
    out_second,
    up_weight,
    up_first,
    up_second,
    down_weight,
    down_first,
    down_second,
    dec_weight,
    dec_first,
    dec_second,
    vectors,
    vec_first,
    vec_second,
):
    image_count = pixels.shape[0]
    row_count = image_count * VIS
    device_count = lax.axis_size(AXES)
    dp_count = lax.axis_size("dp")
    shard_rows = D // device_count
    routed = dp_count == 16 and device_count == 32
    item_count = 4 * image_count // dp_count
    whole_images = item_count == 4

    order = Order(vec_first)
    vec_length = vectors.shape[0]
    pe_rows = pe_weight.T.astype(BF)
    middle_rows = jnp.concatenate([out_weight.T, up_weight, dec_weight], axis=1).astype(BF)
    if routed:
        vec_low = jnp.pad(vectors.astype(BF), (0, 4 * SPAN - vec_length)).reshape(4, SPAN)
        vec_low = jnp.pad(vec_low, ((0, shard_rows - 4), (0, 0)))
        pe_gather = Gathering(jnp.concatenate([pe_rows, vec_low], axis=1), True, order)
        middle_gather = Gathering(middle_rows, False, order)
        qkv_gather = Gathering(qkv_weight.astype(BF), False, order)
        owners = block_order()
    stats = column_sums(order(pixels)).reshape(2, BANDS, PATCH * PATCH)
    stats = order(jnp.sum(stats, axis=2).reshape(2 * BANDS))
    if routed:
        pe_gather.first_turn()
        qkv_gather.middle()
        middle_gather.middle()
    if whole_images:
        marks = jnp.concatenate([visible, scale_index[:, None]], axis=1).astype(F32)
        marks = jnp.concatenate(
            [marks, jnp.broadcast_to(stats[None], (dp_count, 2 * BANDS))], axis=1
        )
        marks_in = lax.all_to_all(order(marks), "dp", split_axis=0, concat_axis=0, tiled=True)
        stats = jnp.sum(marks_in[:, -2 * BANDS :], axis=0)
        marks_in, stats = order(marks_in, stats + lax.ppermute(stats, "grp", core_pairs()))
    else:
        stats = lax.psum(stats, AXES)
    down_rows = order(down_weight).T.astype(BF)
    if routed:
        pe_gather.second_turn()
        down_gather = Gathering(down_rows, False, order)

    dp_index = lax.axis_index("dp")
    cotangent_rows = order(cotangent)
    if whole_images:
        image_order = marks_in[:, : -2 * BANDS].astype(jnp.int32)
        visible_in, scale_in = image_order[:, :VIS], image_order[:, VIS]
        dy_sent, dy_sums, vacant_low = order(*pick_rows(visible_in, cotangent_rows))
        dec_bias_grad, dy_vacant = dy_sums[0], dy_sums[1]
        dy_rows = lax.all_to_all(dy_sent, "dp", split_axis=0, concat_axis=0, tiled=True)
    spots, scale_rows = order(visible.reshape(row_count), jnp.repeat(scale_index, VIS))
    table = angle_pieces(D, 3)
    if routed:
        pe_gather.cores()
        table = table.reshape(-1, 32, shard_rows)
        table = jnp.einsum("pb,kbr->kpr", owners, table, preferred_element_type=F32).astype(BF)
        table = table.reshape(-1, D)
    hot = angle_hot(spots, scale_rows, 3)
    enc_table = order(*[forward_product(hot, part) for part in halves(table)])
    if routed:
        qkv_gather.first_turn()
    if routed:
        pe_pair = pe_gather.total()
        vector_all = jnp.concatenate([part[:, PIX:] for part in pe_pair])
        vector_all = vector_all.reshape(device_count, shard_rows, SPAN)[:, :4].reshape(device_count, -1)
        vector_all = jnp.einsum("pb,pv->bv", owners, vector_all, preferred_element_type=F32)
        vector_all = vector_all[:, :vec_length].reshape(-1)
    else:
        early = jnp.concatenate([pe_rows, qkv_weight.astype(BF)], axis=1)
        early_full = lax.all_gather(early, AXES, axis=0, tiled=True)
        middle_full = lax.all_gather(middle_rows, AXES, axis=0, tiled=True)
        down_full = lax.all_gather(down_rows, AXES, axis=0, tiled=True)
        vector_all = lax.all_gather(vectors.astype(BF), AXES, axis=0, tiled=True).astype(F32)
        pe_pair = (early_full[:HALF, :PIX], early_full[HALF:, :PIX])
        qkv_pair = (early_full[:HALF, PIX:], early_full[HALF:, PIX:])
        middle_pair = (middle_full[:HALF], middle_full[HALF:])
        down_pair = (down_full[:HALF], down_full[HALF:])

    entry_count = row_count * device_count * PATCH * PATCH
    band_mean = stats[:BANDS] / entry_count
    band_scale = lax.rsqrt(stats[BANDS:] / entry_count - band_mean * band_mean + EPS_NORM)
    scale_row = jnp.repeat(band_scale, PATCH * PATCH)[None]
    pixel_norm = pixels.reshape(row_count, PIX).astype(F32) - jnp.repeat(band_mean, PATCH * PATCH)[None]
    pixel_low = order((pixel_norm * scale_row).astype(BF))
    pieces, up_bias, dec_bias = split_vectors(vector_all)
    query_bias, value_bias = pieces[5], pieces[6]
    wide = jnp.stack(pieces[:5] + pieces[7:])
    if routed:
        wide = wide.astype(BF).reshape(8, 32, shard_rows)
        wide = jnp.einsum("pb,nbr->npr", owners, wide, preferred_element_type=F32).reshape(8, D)
    gain_one, shift_one, gain_two, shift_two, pe_bias, out_bias, down_bias, mask_token = [
        halves(wide[number]) for number in range(8)
    ]

    stream_in = outward(pixel_low, pe_pair, 0, PIX)
    stream_in = [part + bias + angle for part, bias, angle in zip(stream_in, pe_bias, enc_table)]
    norm_one, normed_one, inv_std_one = norm_forward(stream_in, gain_one, shift_one)
    norm_one = order(*norm_one)
    if routed:
        middle_gather.first_turn()
        down_gather.middle()
        qkv_gather.second_turn()
    if whole_images:
        dy_rows = order(dy_rows).reshape(row_count, DDEC)
    if routed:
        middle_gather.second_turn()
        qkv_gather.cores()
        qkv_pair = qkv_gather.total()
    norm_one = order(*norm_one)
    low_rows = jax.ShapeDtypeStruct((row_count, 3 * D), BF)
    qkv_bias = jnp.concatenate([query_bias, jnp.zeros_like(query_bias), value_bias])
    (projected,) = inward_call(
        shift_kernel, norm_one, qkv_pair, 0, 3 * D, qkv_bias.reshape(1, 3 * D), [low_rows]
    )
    projected = order(projected)
    mixture_low, peaks = order(*attend(projected))
    if routed:
        down_gather.first_turn()
        middle_gather.cores()
        middle_pair = middle_gather.total()
        down_gather.second_turn()
    mixture_low = order(mixture_low)
    UP, DEC = D, D + FF
    stream_mid = outward(mixture_low, middle_pair, 0, D)
    stream_mid = [part + more + bias for part, more, bias in zip(stream_in, stream_mid, out_bias)]
    norm_two, normed_two, inv_std_two = norm_forward(stream_mid, gain_two, shift_two)

    if whole_images:
        out_low = [part.astype(BF) for part in outward(dy_rows, middle_pair, DEC, DDEC)]
    else:
        placement = visible[:, :, None] == jnp.arange(GRID)[None, None, :]
        placement_low = placement.astype(BF)
        vacant = 1.0 - jnp.sum(placement.astype(F32), axis=1)
        grad_rows = cotangent_rows[0].reshape(-1, DDEC)
        dec_bias_grad = jnp.sum(grad_rows.astype(F32), axis=0)
        grid_grad = jnp.concatenate(outward(grad_rows, middle_pair, DEC, DDEC), axis=1)
        grid_grad = grid_grad.astype(BF).reshape(item_count, dp_count, QUART, D)
        returned = lax.all_to_all(
            grid_grad, "dp", split_axis=1, concat_axis=0, tiled=True
        ).reshape(image_count, GRID, D)
        out_low = jnp.einsum(
            "nvg,ngd->nvd", placement_low, returned, preferred_element_type=F32
        )
        out_low = halves(out_low.reshape(row_count, D).astype(BF))
        mask_grad = halves(
            jnp.einsum("ng,ngd->d", vacant.astype(BF), returned, preferred_element_type=F32)
        )
    out_grad_rows = [part.astype(F32) for part in out_low]

    out_low = order(*out_low)
    norm_two = order(*norm_two)
    activated, slope = order(*expand(norm_two, middle_pair, UP, up_bias))
    if routed:
        down_gather.cores()
        down_pair = down_gather.total()
    down_part = Reduction(product_of(order, (out_low, activated)), routed, order)
    down_part.cores()
    out_low = order(*out_low)
    hidden = jax.ShapeDtypeStruct((row_count, FF), BF)
    preact_low, up_bias_grad = order(
        *inward_call(
            slope_kernel,
            out_low,
            down_pair,
            0,
            FF,
            slope,
            [hidden, jax.ShapeDtypeStruct((1, FF), F32)],
        )
    )
    up_bias_grad = up_bias_grad[0]
    down_part.first_turn()
    activated = order(activated)
    stream_out = outward(activated, down_pair, 0, FF)
    stream_low = order(
        *[
            (part + more + bias).astype(BF)
            for part, more, bias in zip(stream_mid, stream_out, down_bias)
        ]
    )

    if not whole_images:
        full_grid = jnp.einsum(
            "nvg,nvd->ngd",
            placement_low,
            jnp.concatenate(stream_low, axis=1).reshape(image_count, VIS, D),
            preferred_element_type=F32,
        )
        full_grid = full_grid + vacant[:, :, None] * jnp.concatenate(mask_token)
        quarters = full_grid.astype(BF).reshape(4 * image_count, 1, QUART, D)
        ratio_image = jnp.power(2.0, scale_index.astype(F32) - 1.0)
        ratio_quarter = jnp.repeat(ratio_image, 4).reshape(4 * image_count, 1).astype(BF)
        received = lax.all_to_all(quarters, "dp", split_axis=0, concat_axis=1, tiled=True)
        received_ratio = lax.all_to_all(
            ratio_quarter, "dp", split_axis=0, concat_axis=1, tiled=True
        )
        quarter_id = dp_index * item_count + jnp.arange(item_count)
        position = (quarter_id % 4)[:, None] * QUART + jnp.arange(QUART)[None, :]
        scale_at = jnp.round(jnp.log2(received_ratio.astype(F32))).astype(jnp.int32) + 1
        full = (item_count, dp_count, QUART)
        dec_table = forward_product(
            angle_hot(
                jnp.broadcast_to(position[:, None, :], full).reshape(-1),
                jnp.broadcast_to(scale_at[:, :, None], full).reshape(-1),
                2,
            ),
            angle_pieces(DDEC, 2),
        )
        received = halves(received.reshape(-1, D))
        decoded = inward(received, middle_pair, DEC, DDEC) + dec_bias + dec_table
        decoded = decoded.astype(BF).reshape((1,) + full + (DDEC,))

    down_bias_grad = [jnp.sum(part, axis=0) for part in out_grad_rows]
    up_part = Reduction(product_of(order, (norm_two, preact_low)), routed, order)
    up_part.cores()
    down_part.second_turn()
    two_grad = outward(order(preact_low), middle_pair, UP, FF)
    mid_grad, gain_two_grad, shift_two_grad = norm_backward(
        two_grad, normed_two, inv_std_two, gain_two
    )
    mid_grad = [part + more for part, more in zip(mid_grad, out_grad_rows)]
    out_bias_grad = [jnp.sum(part, axis=0) for part in mid_grad]
    mid_low = order(*[part.astype(BF) for part in mid_grad])
    up_part.first_turn()
    down_part.along_z()
    mid_low = order(*mid_low)
    mixture_grad = order(inward(mid_low, middle_pair, 0, D).astype(BF))
    projected_low, attend_sums = order(*attend_back(projected, mixture_grad, peaks))
    query_bias_grad, value_bias_grad = attend_sums[0], attend_sums[1]
    down_shard = down_part.total()
    up_part.second_turn()
    qkv_part = Reduction(
        product_of(order, (mid_low, mixture_low), (norm_one, projected_low)), routed, order
    )
    qkv_part.cores()
    one_grad = outward(order(projected_low), qkv_pair, 0, 3 * D)
    in_grad, gain_one_grad, shift_one_grad = norm_backward(
        one_grad, normed_one, inv_std_one, gain_one
    )
    in_grad = [part + more for part, more in zip(in_grad, mid_grad)]
    pe_bias_grad = [jnp.sum(part, axis=0) for part in in_grad]
    in_low = order(*[part.astype(BF) for part in in_grad])
    qkv_part.first_turn()
    up_part.along_z()
    if whole_images:
        mask_grad = [
            jnp.sum(part, axis=0) for part in outward(order(vacant_low), middle_pair, DEC, DDEC)
        ]
    wide_grad = jnp.stack(
        [
            jnp.concatenate(pair)
            for pair in (
                gain_one_grad,
                shift_one_grad,
                gain_two_grad,
                shift_two_grad,
                pe_bias_grad,
                out_bias_grad,
                down_bias_grad,
                mask_grad,
            )
        ]
    )
    if routed:
        wide_grad = wide_grad.astype(BF).reshape(8, 32, shard_rows)
        wide_grad = jnp.einsum("pb,npr->nbr", owners, wide_grad, preferred_element_type=F32)
        wide_grad = wide_grad.reshape(8, D)
    vec_grad = jnp.concatenate(
        [
            wide_grad[:5].reshape(-1),
            query_bias_grad,
            value_bias_grad,
            wide_grad[5:].reshape(-1),
            up_bias_grad,
            dec_bias_grad,
        ]
    )
    if routed:
        vec_rows = jnp.pad(
            vec_grad.reshape(device_count, vec_length), ((0, 0), (0, 4 * SPAN - vec_length))
        )
        vec_rows = jnp.einsum("pb,bv->pv", owners, vec_rows.astype(BF), preferred_element_type=F32)
        vec_rows = vec_rows.reshape(device_count, 4, SPAN)
        vec_rows = jnp.pad(vec_rows, ((0, 0), (0, shard_rows - 4), (0, 0))).reshape(2, HALF, SPAN)

        def last_product(half, came):
            left, stream = order(in_low[half], stream_low[half])
            token = mask_token[half].reshape(HALF, 1)
            operands = (left, pixel_low, vec_rows[half], stream, dy_rows, token, dy_vacant[None])
            return last_call(operands, came)

    else:

        def last_product(half, came):
            return jnp.concatenate(
                [
                    weight_product(in_low[half], pixel_low),
                    weight_product(received[half], grad_rows),
                ],
                axis=1,
            ).astype(BF)

    pe_part = Reduction(last_product, routed, order)
    pe_part.cores()
    (norm_grad,) = inward_call(
        scale_kernel,
        order(*in_low),
        pe_pair,
        0,
        PIX,
        scale_row,
        [jax.ShapeDtypeStruct((row_count, PIX), F32)],
        256,
    )
    norm_grad = order(norm_grad)
    pe_part.first_turn()
    qkv_part.join(pe_part)
    qkv_part.second_turn()
    if whole_images:
        dec_pieces = angle_pieces(DDEC, 2)
        vis_table = forward_product(angle_hot(spots, scale_rows, 2), dec_pieces)
        vis_rows = inward(order(*stream_low), middle_pair, DEC, DDEC) + dec_bias + vis_table
        vis_rows = order(vis_rows.astype(BF).reshape(image_count, VIS, DDEC))
        vis_in = lax.all_to_all(vis_rows, "dp", split_axis=0, concat_axis=0, tiled=True)
        tokens = [jnp.broadcast_to(part.astype(BF), (8, HALF)) for part in mask_token]
        mask_rows = inward(tokens, middle_pair, DEC, DDEC)[:1] + dec_bias
    up_shard = up_part.total()
    qkv_part.along_z()
    pixel_grad = order(norm_grad).reshape(image_count, VIS, PIX)
    if whole_images:
        decoded = order(place_rows(visible_in, scale_in, order(vis_in), dec_pieces, mask_rows))
    last_total = qkv_part.total()
    out_shard, qkv_shard = last_total[:, :D], last_total[:, D : 4 * D]
    pe_shard, dec_shard = last_total[:, 4 * D : 4 * D + PIX], last_total[:, -DDEC:]
    if routed:
        vec_shard = last_total[:4, 4 * D + PIX : 4 * D + PIX + SPAN].reshape(-1)[:vec_length]
    else:
        vec_shard = lax.psum_scatter(vec_grad, AXES, scatter_dimension=0, tiled=True)
    shards = (pe_shard, qkv_shard, out_shard, up_shard, down_shard, dec_shard, vec_shard)
    parts = (last_total, up_shard, down_shard) if routed else shards
    local_squares = sum((jnp.sum(gradient * gradient) for gradient in parts))
    squares = tiny_sum(local_squares.reshape(1), routed)[0]
    grad_norm = jnp.sqrt(squares)
    vec_first = order.token
    clip_factor = jnp.minimum(1.0, CLIP_LEVEL / grad_norm)
    params = (pe_weight, qkv_weight, out_weight, up_weight, down_weight, dec_weight, vectors)
    firsts = (pe_first, qkv_first, out_first, up_first, down_first, dec_first, vec_first)
    seconds = (pe_second, qkv_second, out_second, up_second, down_second, dec_second, vec_second)
    results = []
    for number in range(7):
        step_rate = LR_VECTOR if number == 6 else LR_MATRIX
        decay_rate = 0.0 if number == 6 else DECAY_MATRIX
        gradient = shards[number].T if number in (0, 2, 4) else shards[number]
        results.extend(
            adamw_update(
                params[number],
                firsts[number],
                seconds[number],
                gradient * clip_factor,
                step_rate,
                decay_rate,
            )
        )
    return (decoded, pixel_grad, *results, grad_norm)


def solution(mesh):
    rows = P(AXES, None)
    cols = P(None, AXES)
    vecs = P(AXES)
    images = P(AXES, None, None)
    grids = P("grp", "dp", None, None, None)
    states = (cols,) * 3 + (rows,) * 3 + (cols,) * 3 + (rows,) * 3 + (cols,) * 3 + (rows,) * 3
    states = states + (vecs,) * 3
    return jax.shard_map(
        local,
        mesh=mesh,
        in_specs=(images, rows, vecs, grids) + states,
        out_specs=(grids, images) + states + (P(),),
        check_vma=False,
    )
```

```python
import functools

import jax
import jax.numpy as jnp
import ml_dtypes
import numpy as np
from jax import lax
from jax.experimental import pallas as pl
from jax.experimental.pallas import tpu as pltpu
from jax.sharding import PartitionSpec as P

D = 1024
FF = 4096
HEADS = 16
HDIM = 64
DDEC = 512
PATCH = 16
SIDE = 14
BANDS = 3
STEP = 10
PIX = 768
GRID = 196
VIS = 49
QUART = 49
NSCALE = 4
AXES = ("grp", "dp")
HALF = D // 2
BF = jnp.bfloat16
F32 = jnp.float32

EPS_NORM = 1e-05
BETA_ONE = 0.9
BETA_TWO = 0.95
ADAM_EPS = 1e-08
LR_MATRIX = 0.08
LR_VECTOR = 0.3
DECAY_MATRIX = 0.05
CLIP_LEVEL = 1.0


def forward_product(left, right):
    return jnp.dot(left, right, preferred_element_type=F32)


def back_product(left, right):
    return lax.dot_general(left, right, (((1,), (1,)), ((), ())), preferred_element_type=F32)


def weight_product(left, right):
    return lax.dot_general(left, right, (((0,), (0,)), ((), ())), preferred_element_type=F32)


def angle_pieces(channels, pieces):
    quarter = channels // 4
    step = np.float32(-np.log(np.float32(10000.0))) / np.float32(quarter)
    frequency = np.exp(np.arange(quarter, dtype=np.float32) * step)
    ratio = np.float32(2.0) ** (np.arange(NSCALE, dtype=np.float32) - 1)
    spot = np.arange(SIDE, dtype=np.float32)
    angle = (ratio[:, None] * spot[None, :]).reshape(-1, 1) * frequency[None, :]
    half = np.concatenate([np.sin(angle.astype(np.float64)), np.cos(angle.astype(np.float64))], 1)
    zeros = np.zeros_like(half)
    rest = np.concatenate(
        [np.concatenate([half, zeros], 1), np.concatenate([zeros, half], 1)], 0
    ).astype(np.float32)
    cut = []
    for _ in range(pieces):
        part = rest.astype(ml_dtypes.bfloat16)
        cut.append(part)
        rest = rest - part.astype(np.float32)
    return jnp.asarray(np.concatenate(cut, 0))


def angle_hot(spots, scale_rows, pieces):
    row_at = scale_rows * SIDE + spots // SIDE
    col_at = (NSCALE + scale_rows) * SIDE + spots % SIDE
    slot = jnp.arange(2 * NSCALE * SIDE)[None, :]
    hot = ((slot == row_at[:, None]) | (slot == col_at[:, None])).astype(BF)
    return jnp.concatenate([hot] * pieces, axis=1)


def split_vectors(vector_all):
    pieces = tuple((vector_all[number * D : (number + 1) * D] for number in range(10)))
    return (pieces, vector_all[10 * D : 10 * D + FF], vector_all[10 * D + FF :])


def halves(array):
    return (array[..., :HALF], array[..., HALF:])


def row_mean(pair):
    return sum(jnp.sum(part, axis=-1, keepdims=True) for part in pair) * (1.0 / D)


def norm_forward(hidden_in, norm_gain, norm_shift):
    mean = row_mean(hidden_in)
    center = [part - mean for part in hidden_in]
    inv_std = lax.rsqrt(row_mean([part * part for part in center]) + EPS_NORM)
    normed = [part * inv_std for part in center]
    low = [
        (part * gain + shift).astype(BF) for part, gain, shift in zip(normed, norm_gain, norm_shift)
    ]
    return (low, normed, inv_std)


def norm_backward(grad_out, normed, inv_std, norm_gain):
    scaled = [part * gain for part, gain in zip(grad_out, norm_gain)]
    mean = row_mean(scaled)
    along = row_mean([part * unit for part, unit in zip(scaled, normed)])
    inner = [(part - mean - unit * along) * inv_std for part, unit in zip(scaled, normed)]
    gain_grad = [jnp.sum(part * unit, axis=0) for part, unit in zip(grad_out, normed)]
    return (inner, gain_grad, [jnp.sum(part, axis=0) for part in grad_out])


def inward(pair, weights, first, count):
    return sum(
        forward_product(part, weight[:, first : first + count]) for part, weight in zip(pair, weights)
    )


def outward(left, weights, first, count):
    return [back_product(left, weight[:, first : first + count]) for weight in weights]


def adamw_update(weight, moment_one, moment_two, gradient, step_rate, decay_rate):
    new_one = BETA_ONE * moment_one + (1.0 - BETA_ONE) * gradient
    new_two = BETA_TWO * moment_two + (1.0 - BETA_TWO) * gradient * gradient
    fixed_one = new_one / (1.0 - BETA_ONE**STEP)
    fixed_two = new_two / (1.0 - BETA_TWO**STEP)
    new_weight = weight - step_rate * (
        fixed_one / (jnp.sqrt(fixed_two) + ADAM_EPS) + decay_rate * weight
    )
    return (new_one, new_two, new_weight)


def core_pairs():
    return [(0, 1), (1, 0)]


def dp_pairs(bits):
    return [(i, i ^ bits) for i in range(16)]


def turn_pairs(core_zero, core_one):
    return [(g * 16 + i, g * 16 + (i ^ (core_one if g else core_zero))) for g in range(2) for i in range(16)]


def tiny_sum(value, routed):
    if not routed:
        return lax.psum(value, AXES)
    for unit in (1, 4):
        one, two, three = [lax.ppermute(value, "dp", dp_pairs(unit * k)) for k in (1, 2, 3)]
        value = (value + one) + (two + three)
    return value + lax.ppermute(value, "grp", core_pairs())


class Order:
    def __init__(self, token):
        self.token = token

    def __call__(self, *values):
        *values, self.token = lax.optimization_barrier((*values, self.token))
        return values[0] if len(values) == 1 else values


def spot_of_chip():
    chip = lax.axis_index("dp")
    return lax.axis_index("grp"), chip % 2, (chip // 2) % 2, chip // 4


def block_order():
    core, x, y, z = spot_of_chip()
    place = jnp.arange(32)
    far, turn_one, turn_two, step = place // 16, (place // 8) % 2, (place // 4) % 2, place % 4
    at_core = core ^ far
    at_x = x ^ jnp.where(at_core == 0, turn_one, turn_two)
    at_y = y ^ jnp.where(at_core == 0, turn_two, turn_one)
    owner = at_core * 16 + (z ^ step) * 4 + at_y * 2 + at_x
    return (owner[:, None] == jnp.arange(32)[None, :]).astype(BF)


class Gathering:
    def __init__(self, shard, direct, order):
        self.order = order
        self.held = order(shard)
        steps = (1, 2, 3) if direct else (1,)
        self.near = [lax.ppermute(self.held, "dp", dp_pairs(4 * k)) for k in steps]

    def grow(self):
        held = self.order(self.held)
        self.held = self.order(jnp.concatenate([held] + self.near))
        return self.held

    def middle(self):
        self.near = [lax.ppermute(self.grow(), "dp", dp_pairs(8))]

    def first_turn(self):
        self.near = [lax.ppermute(self.grow(), AXES, turn_pairs(2, 1))]

    def second_turn(self):
        self.near = [lax.ppermute(self.grow(), AXES, turn_pairs(1, 2))]

    def cores(self):
        self.near = [lax.ppermute(self.grow(), "grp", core_pairs())]

    def total(self):
        return (self.held, self.near[0])


class Reduction:
    def __init__(self, product, routed, order):
        self.product, self.routed, self.order = product, routed, order

    def cores(self):
        if self.routed:
            away = self.order(self.product(1, None))
            self.came = lax.ppermute(away, "grp", core_pairs())

    def first_turn(self):
        if self.routed:
            self.kept, away = self.order(*self.product(0, self.came))
            self.came = lax.ppermute(away, AXES, turn_pairs(1, 2))

    def sum_of(self, first, count):
        part = self.kept[first : first + count].astype(F32)
        return (part + self.came[first : first + count].astype(F32)).astype(BF)

    def second_turn(self):
        if self.routed:
            self.kept = self.order(self.kept)
            half = HALF // 4
            away, self.kept = self.order(self.sum_of(half, half), self.sum_of(0, half))
            self.came = lax.ppermute(away, AXES, turn_pairs(2, 1))

    def along_z(self):
        if self.routed:
            self.kept = self.order(self.kept)
            parts = self.order(*[self.sum_of(32 * k, 32) for k in range(4)])
            self.kept = parts[0]
            self.came = [lax.ppermute(parts[k], "dp", dp_pairs(4 * k)) for k in (1, 2, 3)]

    def join(self, other):
        if self.routed:
            self.came = jnp.concatenate([self.came, other.came], axis=-1)
            self.kept = jnp.concatenate([self.kept, other.kept], axis=-1)
        else:
            mine, theirs = self.product, other.product
            self.product = lambda *at: jnp.concatenate([mine(*at), theirs(*at)], axis=1)

    def total(self):
        if not self.routed:
            full = jnp.concatenate([self.product(half, None) for half in range(2)])
            half = lax.psum_scatter(full, "grp", scatter_dimension=0, tiled=True)
            return lax.psum_scatter(half, "dp", scatter_dimension=0, tiled=True).astype(F32)
        total = self.order(self.kept).astype(F32)
        for part in self.came:
            total = total + part.astype(F32)
        return self.order(total)


WEIGHT_TILE = 1024


def weight_kernel(edges, added, *refs):
    tile = pl.program_id(0)
    sides = refs[: 2 * len(edges)]
    outs = refs[2 * len(edges) + added :]
    first = 0
    for number, last in enumerate(edges):

        @pl.when((tile >= first) & (tile < last))
        def _(left=sides[2 * number], right=sides[2 * number + 1]):
            value = tn(left[...], right[...])
            if added:
                value = value + refs[2 * len(edges)][...].astype(F32)
                outs[0][...] = value[: HALF // 2].astype(BF)
                outs[1][...] = value[HALF // 2 :].astype(BF)
            else:
                outs[0][...] = value.astype(BF)

        first = last


def weight_call(pairs, came):
    edges, specs, count = [], [], 0
    for left, right in pairs:
        start, tiles = count, right.shape[1] // WEIGHT_TILE
        count += tiles

        def at(i, start=start, tiles=tiles):
            return (0, jnp.clip(i - start, 0, tiles - 1))

        specs.append(pl.BlockSpec(left.shape, lambda i: (0, 0)))
        specs.append(pl.BlockSpec((right.shape[0], WEIGHT_TILE), at))
        edges.append(count)
    columns = count * WEIGHT_TILE
    sides = [side for pair in pairs for side in pair]
    if came is None:
        shapes = [(HALF, columns)]
    else:
        shapes = [(HALF // 2, columns)] * 2
        sides.append(came)
        specs.append(pl.BlockSpec((HALF, WEIGHT_TILE), lambda i: (0, i)))
    outs = pl.pallas_call(
        functools.partial(weight_kernel, tuple(edges), int(came is not None)),
        grid=(count,),
        in_specs=specs,
        out_specs=[pl.BlockSpec((shape[0], WEIGHT_TILE), lambda i: (0, i)) for shape in shapes],
        out_shape=[jax.ShapeDtypeStruct(shape, BF) for shape in shapes],
        compiler_params=pltpu.CompilerParams(vmem_limit_bytes=40 * 2**20),
        cost_estimate=SMALL,
        name="weight_product",
    )(*sides)
    return outs if came is not None else outs[0]


def product_of(order, *pairs):
    def product(half, came):
        lefts = order(*[left[half] for left, _ in pairs])
        lefts = lefts if len(pairs) > 1 else [lefts]
        return weight_call([(left, right) for left, (_, right) in zip(lefts, pairs)], came)

    return product


def last_kernel(added, in_ref, pixel_ref, vec_ref, stream_ref, dy_ref, token_ref, vacant_ref, *refs):
    outs = refs[added:]
    parts = (
        (0, PIX, tn(in_ref[...], pixel_ref[...])),
        (PIX, SPAN, vec_ref[...]),
        (PIX + SPAN, DDEC, tn(stream_ref[...], dy_ref[...]) + token_ref[...] * vacant_ref[...]),
    )
    for first, count, value in parts:
        cols = pl.ds(first, count)
        if added:
            value = value + refs[0][:, cols].astype(F32)
            outs[0][:, cols] = value[: HALF // 2].astype(BF)
            outs[1][:, cols] = value[HALF // 2 :].astype(BF)
        else:
            outs[0][:, cols] = value.astype(BF)


def last_call(operands, came):
    columns = PIX + SPAN + DDEC
    shapes = [(HALF, columns)] if came is None else [(HALF // 2, columns)] * 2
    extra = [] if came is None else [came]
    outs = pl.pallas_call(
        functools.partial(last_kernel, len(extra)),
        out_shape=[jax.ShapeDtypeStruct(shape, BF) for shape in shapes],
        compiler_params=pltpu.CompilerParams(vmem_limit_bytes=40 * 2**20),
        cost_estimate=SMALL,
        name="last_product",
    )(*operands, *extra)
    return outs if came is not None else outs[0]


SPAN = 128
SMALL = pl.CostEstimate(flops=10**6, bytes_accessed=10**5, transcendentals=0)


def windows(rows):
    for pair in range(rows // (2 * VIS)):
        start = min(2 * VIS * pair // 16 * 16, rows - SPAN)
        yield start, 2 * VIS * pair - start


def same_image(offset):
    key = lax.broadcasted_iota(jnp.int32, (SPAN, SPAN), 0) - offset
    query = lax.broadcasted_iota(jnp.int32, (SPAN, SPAN), 1) - offset
    inside = (key >= 0) & (key < 2 * VIS)
    match = inside & (query >= 0) & (query < 2 * VIS) & ((key >= VIS) == (query >= VIS))
    weight = match.astype(F32)
    return jnp.concatenate([weight, weight], axis=1) > 0.5, inside


def head_lanes():
    lane = lax.broadcasted_iota(jnp.int32, (SPAN, SPAN), 1)
    low = (lane < HDIM).astype(F32)
    return low.astype(BF), (1.0 - low).astype(BF), lane < HDIM


def nt(left, right):
    return lax.dot_general(left, right, (((1,), (1,)), ((), ())), preferred_element_type=F32)


def tn(left, right):
    return lax.dot_general(left, right, (((0,), (0,)), ((), ())), preferred_element_type=F32)


SCALE = HDIM ** (-0.5)


def attend_kernel(q_ref, k_ref, v_ref, mix_ref, peak_ref):
    low, high, is_low = head_lanes()
    low, high = low * SCALE, high * SCALE
    for number, (start, offset) in enumerate(windows(mix_ref.shape[0])):
        rows = pl.ds(start, SPAN)
        match, inside = same_image(offset)
        q_win = q_ref[rows, :]
        q_two = jnp.concatenate([q_win * low, q_win * high], axis=0)
        scores = jnp.where(match, nt(k_ref[rows, :], q_two), -1e30)
        peak = jnp.max(scores, axis=0, keepdims=True)
        grown = jnp.exp(scores - peak)
        total = jnp.sum(grown, axis=0, keepdims=True)
        probs = (grown * (1.0 / total)).astype(BF)
        peak_ref[0, number : number + 1, :] = peak + jnp.log(total)
        both = tn(probs, v_ref[rows, :])
        mixed = jnp.where(is_low, both[:SPAN], both[SPAN:])
        held = mix_ref[rows, :].astype(F32)
        mix_ref[rows, :] = jnp.where(inside, mixed, held).astype(BF)


def attend(projected):
    rows = projected.shape[0]
    pairs = HEADS // 2
    count = rows // (2 * VIS)
    block = lambda shift: pl.BlockSpec((rows, SPAN), lambda i: (0, i + shift))
    return pl.pallas_call(
        attend_kernel,
        grid=(pairs,),
        in_specs=[block(0), block(pairs), block(2 * pairs)],
        out_specs=[block(0), pl.BlockSpec((1, count, 2 * SPAN), lambda i: (i, 0, 0))],
        out_shape=[
            jax.ShapeDtypeStruct((rows, D), BF),
            jax.ShapeDtypeStruct((pairs, count, 2 * SPAN), F32),
        ],
        compiler_params=pltpu.CompilerParams(vmem_limit_bytes=32 * 2**20),
        cost_estimate=SMALL,
        name="attend",
    )(projected, projected, projected)


def attend_back_kernel(q_ref, k_ref, v_ref, mix_ref, peak_ref, grad_ref, sums_ref):
    at = pl.program_id(0) * SPAN
    low, high, is_low = head_lanes()
    q_sum = jnp.zeros((1, SPAN), F32)
    v_sum = jnp.zeros((1, SPAN), F32)

    def put(rows, shift, value, inside):
        cols = pl.ds(pl.multiple_of(at + shift * D, SPAN), SPAN)
        held = grad_ref[rows, cols].astype(F32)
        grad_ref[rows, cols] = jnp.where(inside, value, held).astype(BF)

    for number, (start, offset) in enumerate(windows(q_ref.shape[0])):
        rows = pl.ds(start, SPAN)
        match, inside = same_image(offset)
        q_win, k_win, v_win, mix_win = q_ref[rows, :], k_ref[rows, :], v_ref[rows, :], mix_ref[rows, :]
        q_win = q_win * SCALE
        q_two = jnp.concatenate([q_win * low, q_win * high], axis=0)
        mix_two = jnp.concatenate([mix_win * low, mix_win * high], axis=0)
        scores = nt(k_win, q_two) - peak_ref[0, number : number + 1, :]
        probs = jnp.exp(jnp.where(match, scores, -1e30))
        probs_low = probs.astype(BF)
        v_grad = jnp.dot(probs_low, mix_two, preferred_element_type=F32)
        probs_grad = nt(v_win, mix_two)
        inner = jnp.sum(probs_grad * probs, axis=0, keepdims=True)
        score = (probs * (probs_grad - inner)).astype(BF)
        k_grad = jnp.dot(score, q_two, preferred_element_type=F32)
        q_both = tn(score, k_win * SCALE)
        q_grad = jnp.where(is_low, q_both[:SPAN], q_both[SPAN:])
        put(rows, 0, q_grad, inside)
        put(rows, 1, k_grad, inside)
        put(rows, 2, v_grad, inside)
        q_sum += jnp.sum(jnp.where(inside, q_grad, 0.0), axis=0, keepdims=True)
        v_sum += jnp.sum(jnp.where(inside, v_grad, 0.0), axis=0, keepdims=True)
    sums_ref[...] = jnp.concatenate([q_sum, v_sum, jnp.zeros((6, SPAN), F32)], axis=0)


def attend_back(projected, mixture_grad, peaks):
    rows = projected.shape[0]
    pairs = HEADS // 2
    count = rows // (2 * VIS)
    block = lambda shift: pl.BlockSpec((rows, SPAN), lambda i: (0, i + shift))
    return pl.pallas_call(
        attend_back_kernel,
        grid=(pairs,),
        in_specs=[
            block(0),
            block(pairs),
            block(2 * pairs),
            block(0),
            pl.BlockSpec((1, count, 2 * SPAN), lambda i: (i, 0, 0)),
        ],
        out_specs=[
            pl.BlockSpec((rows, 3 * D), lambda i: (0, 0)),
            pl.BlockSpec((8, SPAN), lambda i: (0, i)),
        ],
        out_shape=[
            jax.ShapeDtypeStruct((rows, 3 * D), BF),
            jax.ShapeDtypeStruct((8, D), F32),
        ],
        compiler_params=pltpu.CompilerParams(vmem_limit_bytes=40 * 2**20),
        cost_estimate=SMALL,
        name="attend_back",
    )(projected, projected, projected, mixture_grad, peaks)


TAIL_STEP = 0.33
TAIL = (
    0.18636611813641438,
    0.1828371164957563,
    0.20192458123233548,
    0.04500824941716716,
    0.41254593072161144,
    -0.3554434272669394,
    0.46269071975152953,
    -0.1359293701595944,
)


def gelu_and_slope(x):
    t = 1.0 / (1.0 + (TAIL_STEP * 0.7071067811865476) * jnp.abs(x))
    bell = jnp.exp(-0.5 * x * x)
    tail = jnp.full_like(x, 0.5 * TAIL[-1])
    for factor in TAIL[-2::-1]:
        tail = tail * t + 0.5 * factor
    tail = tail * t * bell
    normal = jnp.where(x >= 0.0, 1.0 - tail, tail)
    return x * normal, normal + x * bell * 0.3989422804014327


UP_TILE = 512


def both(near_ref, far_ref, near_w_ref, far_w_ref):
    product = jnp.dot(near_ref[...], near_w_ref[...], preferred_element_type=F32)
    return product + jnp.dot(far_ref[...], far_w_ref[...], preferred_element_type=F32)


def expand_kernel(near_ref, far_ref, near_w_ref, far_w_ref, bias_ref, act_ref, slope_ref):
    preact = both(near_ref, far_ref, near_w_ref, far_w_ref) + bias_ref[...]
    activated, slope = gelu_and_slope(preact)
    act_ref[...] = activated.astype(BF)
    slope_ref[...] = slope.astype(BF)


def shift_kernel(near_ref, far_ref, near_w_ref, far_w_ref, bias_ref, out_ref):
    out_ref[...] = (both(near_ref, far_ref, near_w_ref, far_w_ref) + bias_ref[...]).astype(BF)


def scale_kernel(near_ref, far_ref, near_w_ref, far_w_ref, scale_ref, out_ref):
    out_ref[...] = both(near_ref, far_ref, near_w_ref, far_w_ref) * scale_ref[...]


def slope_kernel(near_ref, far_ref, near_w_ref, far_w_ref, slope_ref, out_ref, sums_ref):
    grad = both(near_ref, far_ref, near_w_ref, far_w_ref) * slope_ref[...].astype(F32)
    out_ref[...] = grad.astype(BF)
    sums_ref[...] = jnp.sum(grad, axis=0, keepdims=True)


def inward_call(kernel, pair, weights, first_column, columns, extra, outs, width=UP_TILE):
    rows = pair[0].shape[0]
    shift = first_column // width
    whole = pl.BlockSpec((rows, HALF), lambda i: (0, 0))
    weight = pl.BlockSpec((HALF, width), lambda i: (0, i + shift))
    tile = lambda array: pl.BlockSpec((array.shape[0], width), lambda i: (0, i))
    return pl.pallas_call(
        kernel,
        grid=(columns // width,),
        in_specs=[whole, whole, weight, weight, tile(extra)],
        out_specs=[tile(out) for out in outs],
        out_shape=outs,
        compiler_params=pltpu.CompilerParams(vmem_limit_bytes=40 * 2**20),
        cost_estimate=SMALL,
        name=kernel.__name__,
    )(*pair, *weights, extra)


def expand(pair, weights, first_column, bias):
    out = jax.ShapeDtypeStruct((pair[0].shape[0], FF), BF)
    return inward_call(expand_kernel, pair, weights, first_column, FF, bias.reshape(1, FF), [out, out])


def sums_kernel(first, pixel_ref, vec_ref, out_ref):
    sums = [jnp.zeros((1, PIX), F32)] * 2
    for image in range(pixel_ref.shape[0]):
        values = pixel_ref[image].astype(F32)
        sums[0] = sums[0] + jnp.sum(values, axis=0, keepdims=True)
        sums[1] = sums[1] + jnp.sum(values * values, axis=0, keepdims=True)
    place = lax.broadcasted_iota(jnp.int32, vec_ref.shape, 0) * SPAN
    place = place + lax.broadcasted_iota(jnp.int32, vec_ref.shape, 1)
    values = vec_ref[...]
    for number in range(2 * BANDS):
        band = number % BANDS
        rest = sums[number // BANDS][:, band * PATCH * PATCH : (band + 1) * PATCH * PATCH]
        rest = jnp.sum(rest, axis=1, keepdims=True)
        for piece in range(3):
            part = rest.astype(BF).astype(F32)
            rest = rest - part
            values = jnp.where(place == first + 3 * number + piece, part, values)
    out_ref[...] = values.astype(BF)


def vectors_and_sums(pixels, vec_rows, first):
    return pl.pallas_call(
        functools.partial(sums_kernel, first),
        out_shape=jax.ShapeDtypeStruct(vec_rows.shape, BF),
        compiler_params=pltpu.CompilerParams(vmem_limit_bytes=20 * 2**20),
        cost_estimate=SMALL,
        name="vectors_and_sums",
    )(pixels, vec_rows)


def pick_kernel(spot_ref, source_ref, dy_ref, rows_ref, sums_ref, pieces_ref, total_ref):
    quarter = pl.program_id(0)

    @pl.when(quarter == 0)
    def _():
        sums_ref[...] = jnp.zeros_like(sums_ref)
        total_ref[...] = jnp.zeros_like(total_ref)

    count = dy_ref.shape[1]
    place = spot_ref[...] - quarter * QUART
    target = jnp.where((place >= 0) & (place < QUART), place * (count // QUART) + source_ref[...], -1)
    hot = (lax.broadcasted_iota(jnp.int32, (count, count), 1) == target).astype(F32)
    values = dy_ref[0]
    total_ref[...] += jnp.dot(hot.astype(BF), values, preferred_element_type=F32)
    vacant = 1.0 - jnp.sum(hot, axis=0, keepdims=True)
    weights = jnp.concatenate([jnp.ones_like(vacant), vacant, jnp.zeros((6, count), F32)], axis=0)
    sums_ref[...] += jnp.dot(weights.astype(BF), values, preferred_element_type=F32)

    @pl.when(quarter == pl.num_programs(0) - 1)
    def _():
        rows_ref[...] = total_ref[...].astype(BF)
        rest = sums_ref[1:2]
        pieces = []
        for _ in range(3):
            pieces.append(rest.astype(BF))
            rest = rest - pieces[-1].astype(F32)
        zeros = jnp.zeros((5, DDEC), BF)
        pieces_ref[...] = jnp.concatenate(pieces + [zeros], axis=0)


def pick_rows(visible_in, grids):
    images = visible_in.shape[0]
    count = images * QUART
    grids = grids[0].transpose(0, 2, 1, 3).reshape(4, count, DDEC)
    source = jnp.asarray(np.repeat(np.arange(images, dtype=np.int32), VIS)[:, None])
    column = pl.BlockSpec((count, 1), lambda i: (0, 0))
    small = pl.BlockSpec((8, DDEC), lambda i: (0, 0))
    return pl.pallas_call(
        pick_kernel,
        grid=(4,),
        in_specs=[column, column, pl.BlockSpec((1, count, DDEC), lambda i: (i, 0, 0))],
        out_specs=[pl.BlockSpec((count, DDEC), lambda i: (0, 0)), small, small],
        out_shape=[
            jax.ShapeDtypeStruct((count, DDEC), BF),
            jax.ShapeDtypeStruct((8, DDEC), F32),
            jax.ShapeDtypeStruct((8, DDEC), BF),
        ],
        scratch_shapes=[pltpu.VMEM((count, DDEC), F32)],
        compiler_params=pltpu.CompilerParams(vmem_limit_bytes=40 * 2**20),
        cost_estimate=SMALL,
        name="pick_rows",
    )(visible_in.reshape(count, 1), source, grids)


def place_kernel(scale_ref, spot_ref, rows_ref, table_ref, base_ref, out_ref):
    scale = scale_ref[pl.program_id(0)]
    spot = spot_ref[0]
    for quarter in range(4):
        place = lax.broadcasted_iota(jnp.int32, (QUART, VIS), 0) + quarter * QUART
        hot = (spot == place).astype(F32)
        vacant = jnp.sum(hot, axis=1, keepdims=True) < 0.5
        placed = jnp.dot(hot.astype(BF), rows_ref[0], preferred_element_type=F32)
        slot = lax.broadcasted_iota(jnp.int32, (QUART, 2 * NSCALE * SIDE), 1)
        place = lax.broadcasted_iota(jnp.int32, slot.shape, 0) + quarter * QUART
        line = lax.shift_right_logical(place * 1171, 14)
        row_at = scale * SIDE + line
        col_at = (NSCALE + scale) * SIDE + place - line * SIDE
        angle_at = ((slot == row_at) | (slot == col_at)).astype(F32).astype(BF)
        angle_at = jnp.concatenate([angle_at, angle_at], axis=1)
        empty = jnp.dot(angle_at, table_ref[...], preferred_element_type=F32) + base_ref[...]
        out_ref[0, quarter, 0] = jnp.where(vacant, empty, placed).astype(BF)


def place_rows(visible_in, scale_in, rows, table, base):
    images = visible_in.shape[0]
    return pl.pallas_call(
        place_kernel,
        grid_spec=pltpu.PrefetchScalarGridSpec(
            num_scalar_prefetch=1,
            grid=(images,),
            in_specs=[
                pl.BlockSpec((1, 1, VIS), lambda i, scale: (i, 0, 0)),
                pl.BlockSpec((1, VIS, DDEC), lambda i, scale: (i, 0, 0)),
                pl.BlockSpec(table.shape, lambda i, scale: (0, 0)),
                pl.BlockSpec((1, DDEC), lambda i, scale: (0, 0)),
            ],
            out_specs=pl.BlockSpec((1, 4, 1, QUART, DDEC), lambda i, scale: (0, 0, i, 0, 0)),
        ),
        out_shape=jax.ShapeDtypeStruct((1, 4, images, QUART, DDEC), BF),
        compiler_params=pltpu.CompilerParams(vmem_limit_bytes=20 * 2**20),
        cost_estimate=SMALL,
        name="place_rows",
    )(scale_in, visible_in[:, None, :], rows, table, base)


def local(
    pixels,
    visible,
    scale_index,
    cotangent,
    pe_weight,
    pe_first,
    pe_second,
    qkv_weight,
    qkv_first,
    qkv_second,
    out_weight,
    out_first,
    out_second,
    up_weight,
    up_first,
    up_second,
    down_weight,
    down_first,
    down_second,
    dec_weight,
    dec_first,
    dec_second,
    vectors,
    vec_first,
    vec_second,
):
    image_count = pixels.shape[0]
    row_count = image_count * VIS
    device_count = lax.axis_size(AXES)
    dp_count = lax.axis_size("dp")
    shard_rows = D // device_count
    routed = dp_count == 16 and device_count == 32
    item_count = 4 * image_count // dp_count
    whole_images = item_count == 4

    order = Order(vec_first)
    dp_index = lax.axis_index("dp")
    vec_length = vectors.shape[0]
    if whole_images:
        marks = jnp.concatenate([visible, scale_index[:, None]], axis=1)
        marks_in = lax.all_to_all(marks, "dp", split_axis=0, concat_axis=0, tiled=True)
    pe_rows = pe_weight.T.astype(BF)
    middle_rows = jnp.concatenate([out_weight.T, up_weight, dec_weight], axis=1).astype(BF)
    if routed:
        qkv_gather = Gathering(qkv_weight.astype(BF), False, order)
        middle_gather = Gathering(middle_rows, False, order)
        owners = block_order()
        vec_low = jnp.pad(vectors.astype(BF).astype(F32), (0, shard_rows * SPAN - vec_length))
        vec_low = vec_low.reshape(shard_rows, SPAN)
        table = order(angle_pieces(D, 3)).reshape(-1, 32, shard_rows)
        table = jnp.einsum("pb,kbr->kpr", owners, table, preferred_element_type=F32).astype(BF)
        table, pixel_flat = order(table.reshape(-1, D), pixels.reshape(row_count, PIX))
        vec_low = vectors_and_sums(order(pixels), vec_low, vec_length)
        pe_gather = Gathering(jnp.concatenate([pe_rows, vec_low], axis=1), True, order)
        qkv_gather.middle()
        middle_gather.middle()
    else:
        pixel_rows = pixels.astype(F32).reshape(row_count, BANDS, PATCH * PATCH)
        band_sum = jnp.sum(pixel_rows, axis=(0, 2))
        band_square = jnp.sum(pixel_rows * pixel_rows, axis=(0, 2))
        stats = lax.psum(jnp.concatenate([band_sum, band_square]), AXES)
    down_rows = order(down_weight).T.astype(BF)
    if routed:
        pe_gather.first_turn()
        down_gather = Gathering(down_rows, False, order)

    cotangent_rows = order(cotangent)
    if whole_images:
        marks_in = order(marks_in)
        visible_in, scale_in = marks_in[:, :VIS], marks_in[:, VIS]
        dy_sent, dy_sums, vacant_low = order(*pick_rows(visible_in, cotangent_rows))
        dec_bias_grad, dy_vacant = dy_sums[0], dy_sums[1]
        dy_sent = dy_sent.reshape(image_count, VIS, DDEC)
        dy_rows = lax.all_to_all(dy_sent, "dp", split_axis=0, concat_axis=0, tiled=True)
    if routed:
        pe_gather.second_turn()
        qkv_gather.first_turn()
    spots, scale_rows = order(visible.reshape(row_count), jnp.repeat(scale_index, VIS))
    if routed:
        pe_gather.cores()
    else:
        table, pixel_flat = angle_pieces(D, 3), pixels.reshape(row_count, PIX)
    hot = angle_hot(spots, scale_rows, 3)
    enc_table = order(*[forward_product(hot, part) for part in halves(table)])
    if routed:
        pe_pair = pe_gather.total()
        vector_all = jnp.concatenate([part[:, PIX:] for part in pe_pair])
        vector_all = vector_all.reshape(device_count, shard_rows, SPAN)[:, :4].reshape(device_count, -1)
        vector_all = jnp.einsum("pb,pv->bv", owners, vector_all, preferred_element_type=F32)
        stats = vector_all[:, vec_length : vec_length + 6 * BANDS].reshape(-1, 2 * BANDS, 3)
        stats = jnp.sum(stats, axis=(0, 2))
        vector_all = vector_all[:, :vec_length].reshape(-1)
    else:
        early = jnp.concatenate([pe_rows, qkv_weight.astype(BF)], axis=1)
        early_full = lax.all_gather(early, AXES, axis=0, tiled=True)
        middle_full = lax.all_gather(middle_rows, AXES, axis=0, tiled=True)
        down_full = lax.all_gather(down_rows, AXES, axis=0, tiled=True)
        vector_all = lax.all_gather(vectors.astype(BF), AXES, axis=0, tiled=True).astype(F32)
        pe_pair = (early_full[:HALF, :PIX], early_full[HALF:, :PIX])
        qkv_pair = (early_full[:HALF, PIX:], early_full[HALF:, PIX:])
        middle_pair = (middle_full[:HALF], middle_full[HALF:])
        down_pair = (down_full[:HALF], down_full[HALF:])

    entry_count = row_count * device_count * PATCH * PATCH
    band_mean = stats[:BANDS] / entry_count
    band_scale = lax.rsqrt(stats[BANDS:] / entry_count - band_mean * band_mean + EPS_NORM)
    scale_row = jnp.repeat(band_scale, PATCH * PATCH)[None]
    pixel_norm = pixel_flat.astype(F32) - jnp.repeat(band_mean, PATCH * PATCH)[None]
    pixel_low = order((pixel_norm * scale_row).astype(BF))
    pieces, up_bias, dec_bias = split_vectors(vector_all)
    query_bias, value_bias = pieces[5], pieces[6]
    wide = jnp.stack(pieces[:5] + pieces[7:])
    if routed:
        wide = wide.astype(BF).reshape(8, 32, shard_rows)
        wide = jnp.einsum("pb,nbr->npr", owners, wide, preferred_element_type=F32).reshape(8, D)
    gain_one, shift_one, gain_two, shift_two, pe_bias, out_bias, down_bias, mask_token = [
        halves(wide[number]) for number in range(8)
    ]

    stream_in = outward(pixel_low, pe_pair, 0, PIX)
    stream_in = [part + bias + angle for part, bias, angle in zip(stream_in, pe_bias, enc_table)]
    norm_one, normed_one, inv_std_one = norm_forward(stream_in, gain_one, shift_one)
    norm_one = order(*norm_one)
    if routed:
        middle_gather.first_turn()
        down_gather.middle()
        qkv_gather.second_turn()
    if whole_images:
        dy_rows = order(dy_rows).reshape(row_count, DDEC)
    if routed:
        down_gather.first_turn()
        middle_gather.second_turn()
        qkv_gather.cores()
        qkv_pair = qkv_gather.total()
    norm_one = order(*norm_one)
    low_rows = jax.ShapeDtypeStruct((row_count, 3 * D), BF)
    qkv_bias = jnp.concatenate([query_bias, jnp.zeros_like(query_bias), value_bias])
    (projected,) = inward_call(
        shift_kernel, norm_one, qkv_pair, 0, 3 * D, qkv_bias.reshape(1, 3 * D), [low_rows]
    )
    projected = order(projected)
    mixture_low, peaks = order(*attend(projected))
    if routed:
        down_gather.second_turn()
        middle_gather.cores()
        middle_pair = middle_gather.total()
    mixture_low = order(mixture_low)
    UP, DEC = D, D + FF
    stream_mid = outward(mixture_low, middle_pair, 0, D)
    stream_mid = [part + more + bias for part, more, bias in zip(stream_in, stream_mid, out_bias)]
    norm_two, normed_two, inv_std_two = norm_forward(stream_mid, gain_two, shift_two)

    if whole_images:
        out_low = [part.astype(BF) for part in outward(dy_rows, middle_pair, DEC, DDEC)]
    else:
        placement = visible[:, :, None] == jnp.arange(GRID)[None, None, :]
        placement_low = placement.astype(BF)
        vacant = 1.0 - jnp.sum(placement.astype(F32), axis=1)
        grad_rows = cotangent_rows[0].reshape(-1, DDEC)
        dec_bias_grad = jnp.sum(grad_rows.astype(F32), axis=0)
        grid_grad = jnp.concatenate(outward(grad_rows, middle_pair, DEC, DDEC), axis=1)
        grid_grad = grid_grad.astype(BF).reshape(item_count, dp_count, QUART, D)
        returned = lax.all_to_all(
            grid_grad, "dp", split_axis=1, concat_axis=0, tiled=True
        ).reshape(image_count, GRID, D)
        out_low = jnp.einsum(
            "nvg,ngd->nvd", placement_low, returned, preferred_element_type=F32
        )
        out_low = halves(out_low.reshape(row_count, D).astype(BF))
        mask_grad = halves(
            jnp.einsum("ng,ngd->d", vacant.astype(BF), returned, preferred_element_type=F32)
        )
    out_grad_rows = [part.astype(F32) for part in out_low]

    out_low = order(*out_low)
    norm_two = order(*norm_two)
    activated, slope = order(*expand(norm_two, middle_pair, UP, up_bias))
    if routed:
        down_gather.cores()
        down_pair = down_gather.total()
    down_part = Reduction(product_of(order, (out_low, activated)), routed, order)
    down_part.cores()
    out_low = order(*out_low)
    hidden = jax.ShapeDtypeStruct((row_count, FF), BF)
    preact_low, up_bias_grad = order(
        *inward_call(
            slope_kernel,
            out_low,
            down_pair,
            0,
            FF,
            slope,
            [hidden, jax.ShapeDtypeStruct((1, FF), F32)],
        )
    )
    up_bias_grad = up_bias_grad[0]
    down_part.first_turn()
    activated = order(activated)
    stream_out = outward(activated, down_pair, 0, FF)
    stream_low = order(
        *[
            (part + more + bias).astype(BF)
            for part, more, bias in zip(stream_mid, stream_out, down_bias)
        ]
    )

    if not whole_images:
        full_grid = jnp.einsum(
            "nvg,nvd->ngd",
            placement_low,
            jnp.concatenate(stream_low, axis=1).reshape(image_count, VIS, D),
            preferred_element_type=F32,
        )
        full_grid = full_grid + vacant[:, :, None] * jnp.concatenate(mask_token)
        quarters = full_grid.astype(BF).reshape(4 * image_count, 1, QUART, D)
        ratio_image = jnp.power(2.0, scale_index.astype(F32) - 1.0)
        ratio_quarter = jnp.repeat(ratio_image, 4).reshape(4 * image_count, 1).astype(BF)
        received = lax.all_to_all(quarters, "dp", split_axis=0, concat_axis=1, tiled=True)
        received_ratio = lax.all_to_all(
            ratio_quarter, "dp", split_axis=0, concat_axis=1, tiled=True
        )
        quarter_id = dp_index * item_count + jnp.arange(item_count)
        position = (quarter_id % 4)[:, None] * QUART + jnp.arange(QUART)[None, :]
        scale_at = jnp.round(jnp.log2(received_ratio.astype(F32))).astype(jnp.int32) + 1
        full = (item_count, dp_count, QUART)
        dec_table = forward_product(
            angle_hot(
                jnp.broadcast_to(position[:, None, :], full).reshape(-1),
                jnp.broadcast_to(scale_at[:, :, None], full).reshape(-1),
                2,
            ),
            angle_pieces(DDEC, 2),
        )
        received = halves(received.reshape(-1, D))
        decoded = inward(received, middle_pair, DEC, DDEC) + dec_bias + dec_table
        decoded = decoded.astype(BF).reshape((1,) + full + (DDEC,))

    down_bias_grad = [jnp.sum(part, axis=0) for part in out_grad_rows]
    up_part = Reduction(product_of(order, (norm_two, preact_low)), routed, order)
    up_part.cores()
    down_part.second_turn()
    two_grad = outward(order(preact_low), middle_pair, UP, FF)
    mid_grad, gain_two_grad, shift_two_grad = norm_backward(
        two_grad, normed_two, inv_std_two, gain_two
    )
    mid_grad = [part + more for part, more in zip(mid_grad, out_grad_rows)]
    out_bias_grad = [jnp.sum(part, axis=0) for part in mid_grad]
    mid_low = order(*[part.astype(BF) for part in mid_grad])
    up_part.first_turn()
    down_part.along_z()
    mid_low = order(*mid_low)
    mixture_grad = order(inward(mid_low, middle_pair, 0, D).astype(BF))
    projected_low, attend_sums = order(*attend_back(projected, mixture_grad, peaks))
    query_bias_grad, value_bias_grad = attend_sums[0], attend_sums[1]
    down_shard = down_part.total()
    up_part.second_turn()
    qkv_part = Reduction(
        product_of(order, (mid_low, mixture_low), (norm_one, projected_low)), routed, order
    )
    qkv_part.cores()
    one_grad = outward(order(projected_low), qkv_pair, 0, 3 * D)
    in_grad, gain_one_grad, shift_one_grad = norm_backward(
        one_grad, normed_one, inv_std_one, gain_one
    )
    in_grad = [part + more for part, more in zip(in_grad, mid_grad)]
    pe_bias_grad = [jnp.sum(part, axis=0) for part in in_grad]
    in_low = order(*[part.astype(BF) for part in in_grad])
    qkv_part.first_turn()
    up_part.along_z()
    if whole_images:
        mask_grad = [
            jnp.sum(part, axis=0) for part in outward(order(vacant_low), middle_pair, DEC, DDEC)
        ]
    wide_grad = jnp.stack(
        [
            jnp.concatenate(pair)
            for pair in (
                gain_one_grad,
                shift_one_grad,
                gain_two_grad,
                shift_two_grad,
                pe_bias_grad,
                out_bias_grad,
                down_bias_grad,
                mask_grad,
            )
        ]
    )
    if routed:
        wide_grad = wide_grad.astype(BF).reshape(8, 32, shard_rows)
        wide_grad = jnp.einsum("pb,npr->nbr", owners, wide_grad, preferred_element_type=F32)
        wide_grad = wide_grad.reshape(8, D)
    vec_grad = jnp.concatenate(
        [
            wide_grad[:5].reshape(-1),
            query_bias_grad,
            value_bias_grad,
            wide_grad[5:].reshape(-1),
            up_bias_grad,
            dec_bias_grad,
        ]
    )
    if routed:
        vec_rows = jnp.pad(
            vec_grad.reshape(device_count, vec_length), ((0, 0), (0, 4 * SPAN - vec_length))
        )
        vec_rows = jnp.einsum("pb,bv->pv", owners, vec_rows.astype(BF), preferred_element_type=F32)
        vec_rows = vec_rows.reshape(device_count, 4, SPAN)
        vec_rows = jnp.pad(vec_rows, ((0, 0), (0, shard_rows - 4), (0, 0))).reshape(2, HALF, SPAN)

        def last_product(half, came):
            left, stream = order(in_low[half], stream_low[half])
            token = mask_token[half].reshape(HALF, 1)
            operands = (left, pixel_low, vec_rows[half], stream, dy_rows, token, dy_vacant[None])
            return last_call(operands, came)

    else:

        def last_product(half, came):
            return jnp.concatenate(
                [
                    weight_product(in_low[half], pixel_low),
                    weight_product(received[half], grad_rows),
                ],
                axis=1,
            ).astype(BF)

    pe_part = Reduction(last_product, routed, order)
    pe_part.cores()
    (norm_grad,) = inward_call(
        scale_kernel,
        order(*in_low),
        pe_pair,
        0,
        PIX,
        scale_row,
        [jax.ShapeDtypeStruct((row_count, PIX), F32)],
        256,
    )
    norm_grad = order(norm_grad)
    pe_part.first_turn()
    qkv_part.join(pe_part)
    qkv_part.second_turn()
    if whole_images:
        dec_pieces = angle_pieces(DDEC, 2)
        vis_table = forward_product(angle_hot(spots, scale_rows, 2), dec_pieces)
        vis_rows = inward(order(*stream_low), middle_pair, DEC, DDEC) + dec_bias + vis_table
        vis_rows = order(vis_rows.astype(BF).reshape(image_count, VIS, DDEC))
        vis_in = lax.all_to_all(vis_rows, "dp", split_axis=0, concat_axis=0, tiled=True)
        tokens = [jnp.broadcast_to(part.astype(BF), (8, HALF)) for part in mask_token]
        mask_rows = inward(tokens, middle_pair, DEC, DDEC)[:1] + dec_bias
    up_shard = up_part.total()
    qkv_part.along_z()
    pixel_grad = order(norm_grad).reshape(image_count, VIS, PIX)
    if whole_images:
        decoded = order(place_rows(visible_in, scale_in, order(vis_in), dec_pieces, mask_rows))
    last_total = qkv_part.total()
    out_shard, qkv_shard = last_total[:, :D], last_total[:, D : 4 * D]
    pe_shard, dec_shard = last_total[:, 4 * D : 4 * D + PIX], last_total[:, -DDEC:]
    if routed:
        vec_shard = last_total[:4, 4 * D + PIX : 4 * D + PIX + SPAN].reshape(-1)[:vec_length]
    else:
        vec_shard = lax.psum_scatter(vec_grad, AXES, scatter_dimension=0, tiled=True)
    shards = (pe_shard, qkv_shard, out_shard, up_shard, down_shard, dec_shard, vec_shard)
    parts = (last_total, up_shard, down_shard) if routed else shards
    local_squares = sum((jnp.sum(gradient * gradient) for gradient in parts))
    squares = tiny_sum(local_squares.reshape(1), routed)[0]
    grad_norm = jnp.sqrt(squares)
    vec_first = order.token
    clip_factor = jnp.minimum(1.0, CLIP_LEVEL / grad_norm)
    params = (pe_weight, qkv_weight, out_weight, up_weight, down_weight, dec_weight, vectors)
    firsts = (pe_first, qkv_first, out_first, up_first, down_first, dec_first, vec_first)
    seconds = (pe_second, qkv_second, out_second, up_second, down_second, dec_second, vec_second)
    results = []
    for number in range(7):
        step_rate = LR_VECTOR if number == 6 else LR_MATRIX
        decay_rate = 0.0 if number == 6 else DECAY_MATRIX
        gradient = shards[number].T if number in (0, 2, 4) else shards[number]
        results.extend(
            adamw_update(
                params[number],
                firsts[number],
                seconds[number],
                gradient * clip_factor,
                step_rate,
                decay_rate,
            )
        )
    return (decoded, pixel_grad, *results, grad_norm)


def solution(mesh):
    rows = P(AXES, None)
    cols = P(None, AXES)
    vecs = P(AXES)
    images = P(AXES, None, None)
    grids = P("grp", "dp", None, None, None)
    states = (cols,) * 3 + (rows,) * 3 + (cols,) * 3 + (rows,) * 3 + (cols,) * 3 + (rows,) * 3
    states = states + (vecs,) * 3
    return jax.shard_map(
        local,
        mesh=mesh,
        in_specs=(images, rows, vecs, grids) + states,
        out_specs=(grids, images) + states + (P(),),
        check_vma=False,
    )
```

```python
import functools

import jax
import jax.numpy as jnp
import ml_dtypes
import numpy as np
from jax import lax
from jax.experimental import pallas as pl
from jax.experimental.pallas import tpu as pltpu
from jax.sharding import PartitionSpec as P

D = 1024
FF = 4096
HEADS = 16
HDIM = 64
DDEC = 512
PATCH = 16
SIDE = 14
BANDS = 3
STEP = 10
PIX = 768
GRID = 196
VIS = 49
QUART = 49
NSCALE = 4
AXES = ("grp", "dp")
HALF = D // 2
BF = jnp.bfloat16
F32 = jnp.float32

EPS_NORM = 1e-05
BETA_ONE = 0.9
BETA_TWO = 0.95
ADAM_EPS = 1e-08
LR_MATRIX = 0.08
LR_VECTOR = 0.3
DECAY_MATRIX = 0.05
CLIP_LEVEL = 1.0


def forward_product(left, right):
    return jnp.dot(left, right, preferred_element_type=F32)


def back_product(left, right):
    return lax.dot_general(left, right, (((1,), (1,)), ((), ())), preferred_element_type=F32)


def weight_product(left, right):
    return lax.dot_general(left, right, (((0,), (0,)), ((), ())), preferred_element_type=F32)


def angle_pieces(channels, pieces):
    quarter = channels // 4
    step = np.float32(-np.log(np.float32(10000.0))) / np.float32(quarter)
    frequency = np.exp(np.arange(quarter, dtype=np.float32) * step)
    ratio = np.float32(2.0) ** (np.arange(NSCALE, dtype=np.float32) - 1)
    spot = np.arange(SIDE, dtype=np.float32)
    angle = (ratio[:, None] * spot[None, :]).reshape(-1, 1) * frequency[None, :]
    half = np.concatenate([np.sin(angle.astype(np.float64)), np.cos(angle.astype(np.float64))], 1)
    zeros = np.zeros_like(half)
    rest = np.concatenate(
        [np.concatenate([half, zeros], 1), np.concatenate([zeros, half], 1)], 0
    ).astype(np.float32)
    cut = []
    for _ in range(pieces):
        part = rest.astype(ml_dtypes.bfloat16)
        cut.append(part)
        rest = rest - part.astype(np.float32)
    return jnp.asarray(np.concatenate(cut, 0))


def angle_hot(spots, scale_rows, pieces):
    row_at = scale_rows * SIDE + spots // SIDE
    col_at = (NSCALE + scale_rows) * SIDE + spots % SIDE
    slot = jnp.arange(2 * NSCALE * SIDE)[None, :]
    hot = ((slot == row_at[:, None]) | (slot == col_at[:, None])).astype(BF)
    return jnp.concatenate([hot] * pieces, axis=1)


def split_vectors(vector_all):
    pieces = tuple((vector_all[number * D : (number + 1) * D] for number in range(10)))
    return (pieces, vector_all[10 * D : 10 * D + FF], vector_all[10 * D + FF :])


def halves(array):
    return (array[..., :HALF], array[..., HALF:])


def row_mean(pair):
    return sum(jnp.sum(part, axis=-1, keepdims=True) for part in pair) * (1.0 / D)


def norm_forward(hidden_in, norm_gain, norm_shift):
    mean = row_mean(hidden_in)
    center = [part - mean for part in hidden_in]
    inv_std = lax.rsqrt(row_mean([part * part for part in center]) + EPS_NORM)
    normed = [part * inv_std for part in center]
    low = [
        (part * gain + shift).astype(BF) for part, gain, shift in zip(normed, norm_gain, norm_shift)
    ]
    return (low, normed, inv_std)


def norm_backward(grad_out, normed, inv_std, norm_gain):
    scaled = [part * gain for part, gain in zip(grad_out, norm_gain)]
    mean = row_mean(scaled)
    along = row_mean([part * unit for part, unit in zip(scaled, normed)])
    inner = [(part - mean - unit * along) * inv_std for part, unit in zip(scaled, normed)]
    gain_grad = [jnp.sum(part * unit, axis=0) for part, unit in zip(grad_out, normed)]
    return (inner, gain_grad, [jnp.sum(part, axis=0) for part in grad_out])


def inward(pair, weights, first, count):
    return sum(
        forward_product(part, weight[:, first : first + count]) for part, weight in zip(pair, weights)
    )


def outward(left, weights, first, count):
    return [back_product(left, weight[:, first : first + count]) for weight in weights]


def adamw_update(weight, moment_one, moment_two, gradient, step_rate, decay_rate):
    new_one = BETA_ONE * moment_one + (1.0 - BETA_ONE) * gradient
    new_two = BETA_TWO * moment_two + (1.0 - BETA_TWO) * gradient * gradient
    fixed_one = new_one / (1.0 - BETA_ONE**STEP)
    fixed_two = new_two / (1.0 - BETA_TWO**STEP)
    new_weight = weight - step_rate * (
        fixed_one / (jnp.sqrt(fixed_two) + ADAM_EPS) + decay_rate * weight
    )
    return (new_one, new_two, new_weight)


def core_pairs():
    return [(0, 1), (1, 0)]


def dp_pairs(bits):
    return [(i, i ^ bits) for i in range(16)]


def turn_pairs(core_zero, core_one):
    return [(g * 16 + i, g * 16 + (i ^ (core_one if g else core_zero))) for g in range(2) for i in range(16)]


def tiny_sum(value, routed):
    if not routed:
        return lax.psum(value, AXES)
    for unit in (1, 4):
        one, two, three = [lax.ppermute(value, "dp", dp_pairs(unit * k)) for k in (1, 2, 3)]
        value = (value + one) + (two + three)
    return value + lax.ppermute(value, "grp", core_pairs())


class Order:
    def __init__(self, token):
        self.token = token

    def __call__(self, *values):
        *values, self.token = lax.optimization_barrier((*values, self.token))
        return values[0] if len(values) == 1 else values


def spot_of_chip():
    chip = lax.axis_index("dp")
    return lax.axis_index("grp"), chip % 2, (chip // 2) % 2, chip // 4


def block_order():
    core, x, y, z = spot_of_chip()
    place = jnp.arange(32)
    far, turn_one, turn_two, step = place // 16, (place // 8) % 2, (place // 4) % 2, place % 4
    at_core = core ^ far
    at_x = x ^ jnp.where(at_core == 0, turn_one, turn_two)
    at_y = y ^ jnp.where(at_core == 0, turn_two, turn_one)
    owner = at_core * 16 + (z ^ step) * 4 + at_y * 2 + at_x
    return (owner[:, None] == jnp.arange(32)[None, :]).astype(BF)


class Gathering:
    def __init__(self, shard, direct, order):
        self.order = order
        self.held = order(shard)
        steps = (1, 2, 3) if direct else (1,)
        self.near = [lax.ppermute(self.held, "dp", dp_pairs(4 * k)) for k in steps]

    def grow(self):
        held = self.order(self.held)
        self.held = self.order(jnp.concatenate([held] + self.near))
        return self.held

    def middle(self):
        self.near = [lax.ppermute(self.grow(), "dp", dp_pairs(8))]

    def first_turn(self):
        self.near = [lax.ppermute(self.grow(), AXES, turn_pairs(2, 1))]

    def second_turn(self):
        self.near = [lax.ppermute(self.grow(), AXES, turn_pairs(1, 2))]

    def cores(self):
        self.near = [lax.ppermute(self.grow(), "grp", core_pairs())]

    def total(self):
        return (self.held, self.near[0])


class Reduction:
    def __init__(self, product, routed, order):
        self.product, self.routed, self.order = product, routed, order

    def cores(self):
        if self.routed:
            away = self.order(self.product(1, None))
            self.came = lax.ppermute(away, "grp", core_pairs())

    def first_turn(self):
        if self.routed:
            self.kept, away = self.order(*self.product(0, self.came))
            self.came = lax.ppermute(away, AXES, turn_pairs(1, 2))

    def sum_of(self, first, count):
        part = self.kept[first : first + count].astype(F32)
        return (part + self.came[first : first + count].astype(F32)).astype(BF)

    def second_turn(self):
        if self.routed:
            self.kept = self.order(self.kept)
            half = HALF // 4
            away, self.kept = self.order(self.sum_of(half, half), self.sum_of(0, half))
            self.came = lax.ppermute(away, AXES, turn_pairs(2, 1))

    def along_z(self):
        if self.routed:
            self.kept = self.order(self.kept)
            parts = self.order(*[self.sum_of(32 * k, 32) for k in range(4)])
            self.kept = parts[0]
            self.came = [lax.ppermute(parts[k], "dp", dp_pairs(4 * k)) for k in (1, 2, 3)]

    def join(self, other):
        if self.routed:
            self.came = jnp.concatenate([self.came, other.came], axis=-1)
            self.kept = jnp.concatenate([self.kept, other.kept], axis=-1)
        else:
            mine, theirs = self.product, other.product
            self.product = lambda *at: jnp.concatenate([mine(*at), theirs(*at)], axis=1)

    def total(self):
        if not self.routed:
            full = jnp.concatenate([self.product(half, None) for half in range(2)])
            half = lax.psum_scatter(full, "grp", scatter_dimension=0, tiled=True)
            return lax.psum_scatter(half, "dp", scatter_dimension=0, tiled=True).astype(F32)
        total = self.order(self.kept).astype(F32)
        for part in self.came:
            total = total + part.astype(F32)
        return self.order(total)


WEIGHT_TILE = 1024


def weight_kernel(edges, added, *refs):
    tile = pl.program_id(0)
    sides = refs[: 2 * len(edges)]
    outs = refs[2 * len(edges) + added :]
    first = 0
    for number, last in enumerate(edges):

        @pl.when((tile >= first) & (tile < last))
        def _(left=sides[2 * number], right=sides[2 * number + 1]):
            value = tn(left[...], right[...])
            if added:
                value = value + refs[2 * len(edges)][...].astype(F32)
                outs[0][...] = value[: HALF // 2].astype(BF)
                outs[1][...] = value[HALF // 2 :].astype(BF)
            else:
                outs[0][...] = value.astype(BF)

        first = last


def weight_call(pairs, came):
    edges, specs, count = [], [], 0
    for left, right in pairs:
        start, tiles = count, right.shape[1] // WEIGHT_TILE
        count += tiles

        def at(i, start=start, tiles=tiles):
            return (0, jnp.clip(i - start, 0, tiles - 1))

        specs.append(pl.BlockSpec(left.shape, lambda i: (0, 0)))
        specs.append(pl.BlockSpec((right.shape[0], WEIGHT_TILE), at))
        edges.append(count)
    columns = count * WEIGHT_TILE
    sides = [side for pair in pairs for side in pair]
    if came is None:
        shapes = [(HALF, columns)]
    else:
        shapes = [(HALF // 2, columns)] * 2
        sides.append(came)
        specs.append(pl.BlockSpec((HALF, WEIGHT_TILE), lambda i: (0, i)))
    outs = pl.pallas_call(
        functools.partial(weight_kernel, tuple(edges), int(came is not None)),
        grid=(count,),
        in_specs=specs,
        out_specs=[pl.BlockSpec((shape[0], WEIGHT_TILE), lambda i: (0, i)) for shape in shapes],
        out_shape=[jax.ShapeDtypeStruct(shape, BF) for shape in shapes],
        compiler_params=pltpu.CompilerParams(vmem_limit_bytes=40 * 2**20),
        cost_estimate=SMALL,
        name="weight_product",
    )(*sides)
    return outs if came is not None else outs[0]


def product_of(order, *pairs):
    def product(half, came):
        lefts = order(*[left[half] for left, _ in pairs])
        lefts = lefts if len(pairs) > 1 else [lefts]
        return weight_call([(left, right) for left, (_, right) in zip(lefts, pairs)], came)

    return product


def last_kernel(added, in_ref, pixel_ref, vec_ref, stream_ref, dy_ref, token_ref, vacant_ref, *refs):
    outs = refs[added:]
    parts = (
        (0, PIX, tn(in_ref[...], pixel_ref[...])),
        (PIX, SPAN, vec_ref[...]),
        (PIX + SPAN, DDEC, tn(stream_ref[...], dy_ref[...]) + token_ref[...] * vacant_ref[...]),
    )
    for first, count, value in parts:
        cols = pl.ds(first, count)
        if added:
            value = value + refs[0][:, cols].astype(F32)
            outs[0][:, cols] = value[: HALF // 2].astype(BF)
            outs[1][:, cols] = value[HALF // 2 :].astype(BF)
        else:
            outs[0][:, cols] = value.astype(BF)


def last_call(operands, came):
    columns = PIX + SPAN + DDEC
    shapes = [(HALF, columns)] if came is None else [(HALF // 2, columns)] * 2
    extra = [] if came is None else [came]
    outs = pl.pallas_call(
        functools.partial(last_kernel, len(extra)),
        out_shape=[jax.ShapeDtypeStruct(shape, BF) for shape in shapes],
        compiler_params=pltpu.CompilerParams(vmem_limit_bytes=40 * 2**20),
        cost_estimate=SMALL,
        name="last_product",
    )(*operands, *extra)
    return outs if came is not None else outs[0]


SPAN = 128
SMALL = pl.CostEstimate(flops=10**6, bytes_accessed=10**5, transcendentals=0)


def windows(rows):
    for pair in range(rows // (2 * VIS)):
        start = min(2 * VIS * pair // 16 * 16, rows - SPAN)
        yield start, 2 * VIS * pair - start


def same_image(offset):
    key = lax.broadcasted_iota(jnp.int32, (SPAN, SPAN), 0) - offset
    query = lax.broadcasted_iota(jnp.int32, (SPAN, SPAN), 1) - offset
    inside = (key >= 0) & (key < 2 * VIS)
    match = inside & (query >= 0) & (query < 2 * VIS) & ((key >= VIS) == (query >= VIS))
    weight = match.astype(F32)
    return jnp.concatenate([weight, weight], axis=1) > 0.5, inside


def head_lanes():
    lane = lax.broadcasted_iota(jnp.int32, (SPAN, SPAN), 1)
    low = (lane < HDIM).astype(F32)
    return low.astype(BF), (1.0 - low).astype(BF), lane < HDIM


def nt(left, right):
    return lax.dot_general(left, right, (((1,), (1,)), ((), ())), preferred_element_type=F32)


def tn(left, right):
    return lax.dot_general(left, right, (((0,), (0,)), ((), ())), preferred_element_type=F32)


SCALE = HDIM ** (-0.5)


def attend_kernel(q_ref, k_ref, v_ref, mix_ref, peak_ref):
    low, high, is_low = head_lanes()
    low, high = low * SCALE, high * SCALE
    for number, (start, offset) in enumerate(windows(mix_ref.shape[0])):
        rows = pl.ds(start, SPAN)
        match, inside = same_image(offset)
        q_win = q_ref[rows, :]
        q_two = jnp.concatenate([q_win * low, q_win * high], axis=0)
        scores = jnp.where(match, nt(k_ref[rows, :], q_two), -1e30)
        peak = jnp.max(scores, axis=0, keepdims=True)
        grown = jnp.exp(scores - peak)
        total = jnp.sum(grown, axis=0, keepdims=True)
        probs = (grown * (1.0 / total)).astype(BF)
        peak_ref[0, number : number + 1, :] = peak + jnp.log(total)
        both = tn(probs, v_ref[rows, :])
        mixed = jnp.where(is_low, both[:SPAN], both[SPAN:])
        held = mix_ref[rows, :].astype(F32)
        mix_ref[rows, :] = jnp.where(inside, mixed, held).astype(BF)


def attend(projected):
    rows = projected.shape[0]
    pairs = HEADS // 2
    count = rows // (2 * VIS)
    block = lambda shift: pl.BlockSpec((rows, SPAN), lambda i: (0, i + shift))
    return pl.pallas_call(
        attend_kernel,
        grid=(pairs,),
        in_specs=[block(0), block(pairs), block(2 * pairs)],
        out_specs=[block(0), pl.BlockSpec((1, count, 2 * SPAN), lambda i: (i, 0, 0))],
        out_shape=[
            jax.ShapeDtypeStruct((rows, D), BF),
            jax.ShapeDtypeStruct((pairs, count, 2 * SPAN), F32),
        ],
        compiler_params=pltpu.CompilerParams(vmem_limit_bytes=32 * 2**20),
        cost_estimate=SMALL,
        name="attend",
    )(projected, projected, projected)


def attend_back_kernel(q_ref, k_ref, v_ref, mix_ref, peak_ref, grad_ref, sums_ref):
    at = pl.program_id(0) * SPAN
    low, high, is_low = head_lanes()
    q_sum = jnp.zeros((1, SPAN), F32)
    v_sum = jnp.zeros((1, SPAN), F32)

    def put(rows, shift, value, inside):
        cols = pl.ds(pl.multiple_of(at + shift * D, SPAN), SPAN)
        held = grad_ref[rows, cols].astype(F32)
        grad_ref[rows, cols] = jnp.where(inside, value, held).astype(BF)

    for number, (start, offset) in enumerate(windows(q_ref.shape[0])):
        rows = pl.ds(start, SPAN)
        match, inside = same_image(offset)
        q_win, k_win, v_win, mix_win = q_ref[rows, :], k_ref[rows, :], v_ref[rows, :], mix_ref[rows, :]
        q_win = q_win * SCALE
        q_two = jnp.concatenate([q_win * low, q_win * high], axis=0)
        mix_two = jnp.concatenate([mix_win * low, mix_win * high], axis=0)
        scores = nt(k_win, q_two) - peak_ref[0, number : number + 1, :]
        probs = jnp.exp(jnp.where(match, scores, -1e30))
        probs_low = probs.astype(BF)
        v_grad = jnp.dot(probs_low, mix_two, preferred_element_type=F32)
        probs_grad = nt(v_win, mix_two)
        inner = jnp.sum(probs_grad * probs, axis=0, keepdims=True)
        score = (probs * (probs_grad - inner)).astype(BF)
        k_grad = jnp.dot(score, q_two, preferred_element_type=F32)
        q_both = tn(score, k_win * SCALE)
        q_grad = jnp.where(is_low, q_both[:SPAN], q_both[SPAN:])
        put(rows, 0, q_grad, inside)
        put(rows, 1, k_grad, inside)
        put(rows, 2, v_grad, inside)
        q_sum += jnp.sum(jnp.where(inside, q_grad, 0.0), axis=0, keepdims=True)
        v_sum += jnp.sum(jnp.where(inside, v_grad, 0.0), axis=0, keepdims=True)
    sums_ref[...] = jnp.concatenate([q_sum, v_sum, jnp.zeros((6, SPAN), F32)], axis=0)


def attend_back(projected, mixture_grad, peaks):
    rows = projected.shape[0]
    pairs = HEADS // 2
    count = rows // (2 * VIS)
    block = lambda shift: pl.BlockSpec((rows, SPAN), lambda i: (0, i + shift))
    return pl.pallas_call(
        attend_back_kernel,
        grid=(pairs,),
        in_specs=[
            block(0),
            block(pairs),
            block(2 * pairs),
            block(0),
            pl.BlockSpec((1, count, 2 * SPAN), lambda i: (i, 0, 0)),
        ],
        out_specs=[
            pl.BlockSpec((rows, 3 * D), lambda i: (0, 0)),
            pl.BlockSpec((8, SPAN), lambda i: (0, i)),
        ],
        out_shape=[
            jax.ShapeDtypeStruct((rows, 3 * D), BF),
            jax.ShapeDtypeStruct((8, D), F32),
        ],
        compiler_params=pltpu.CompilerParams(vmem_limit_bytes=40 * 2**20),
        cost_estimate=SMALL,
        name="attend_back",
    )(projected, projected, projected, mixture_grad, peaks)


TAIL_STEP = 0.33
TAIL = (
    0.18636611813641438,
    0.1828371164957563,
    0.20192458123233548,
    0.04500824941716716,
    0.41254593072161144,
    -0.3554434272669394,
    0.46269071975152953,
    -0.1359293701595944,
)


def gelu_and_slope(x):
    t = 1.0 / (1.0 + (TAIL_STEP * 0.7071067811865476) * jnp.abs(x))
    bell = jnp.exp(-0.5 * x * x)
    tail = jnp.full_like(x, 0.5 * TAIL[-1])
    for factor in TAIL[-2::-1]:
        tail = tail * t + 0.5 * factor
    tail = tail * t * bell
    normal = jnp.where(x >= 0.0, 1.0 - tail, tail)
    return x * normal, normal + x * bell * 0.3989422804014327


UP_TILE = 512


def both(near_ref, far_ref, near_w_ref, far_w_ref):
    product = jnp.dot(near_ref[...], near_w_ref[...], preferred_element_type=F32)
    return product + jnp.dot(far_ref[...], far_w_ref[...], preferred_element_type=F32)


def expand_kernel(near_ref, far_ref, near_w_ref, far_w_ref, bias_ref, act_ref, slope_ref):
    preact = both(near_ref, far_ref, near_w_ref, far_w_ref) + bias_ref[...]
    activated, slope = gelu_and_slope(preact)
    act_ref[...] = activated.astype(BF)
    slope_ref[...] = slope.astype(BF)


def shift_kernel(near_ref, far_ref, near_w_ref, far_w_ref, bias_ref, out_ref):
    out_ref[...] = (both(near_ref, far_ref, near_w_ref, far_w_ref) + bias_ref[...]).astype(BF)


def scale_kernel(near_ref, far_ref, near_w_ref, far_w_ref, scale_ref, out_ref):
    out_ref[...] = both(near_ref, far_ref, near_w_ref, far_w_ref) * scale_ref[...]


def slope_kernel(near_ref, far_ref, near_w_ref, far_w_ref, slope_ref, out_ref, sums_ref):
    grad = both(near_ref, far_ref, near_w_ref, far_w_ref) * slope_ref[...].astype(F32)
    out_ref[...] = grad.astype(BF)
    sums_ref[...] = jnp.sum(grad, axis=0, keepdims=True)


def inward_call(kernel, pair, weights, first_column, columns, extra, outs, width=UP_TILE):
    rows = pair[0].shape[0]
    shift = first_column // width
    whole = pl.BlockSpec((rows, HALF), lambda i: (0, 0))
    weight = pl.BlockSpec((HALF, width), lambda i: (0, i + shift))
    tile = lambda array: pl.BlockSpec((array.shape[0], width), lambda i: (0, i))
    return pl.pallas_call(
        kernel,
        grid=(columns // width,),
        in_specs=[whole, whole, weight, weight, tile(extra)],
        out_specs=[tile(out) for out in outs],
        out_shape=outs,
        compiler_params=pltpu.CompilerParams(vmem_limit_bytes=40 * 2**20),
        cost_estimate=SMALL,
        name=kernel.__name__,
    )(*pair, *weights, extra)


def expand(pair, weights, first_column, bias):
    out = jax.ShapeDtypeStruct((pair[0].shape[0], FF), BF)
    return inward_call(expand_kernel, pair, weights, first_column, FF, bias.reshape(1, FF), [out, out])


def sums_kernel(first, pixel_ref, vec_ref, out_ref):
    sums = [jnp.zeros((1, PIX), F32)] * 2
    for image in range(pixel_ref.shape[0]):
        values = pixel_ref[image].astype(F32)
        sums[0] = sums[0] + jnp.sum(values, axis=0, keepdims=True)
        sums[1] = sums[1] + jnp.sum(values * values, axis=0, keepdims=True)
    place = lax.broadcasted_iota(jnp.int32, vec_ref.shape, 0) * SPAN
    place = place + lax.broadcasted_iota(jnp.int32, vec_ref.shape, 1)
    values = vec_ref[...]
    for number in range(2 * BANDS):
        band = number % BANDS
        rest = sums[number // BANDS][:, band * PATCH * PATCH : (band + 1) * PATCH * PATCH]
        rest = jnp.sum(rest, axis=1, keepdims=True)
        for piece in range(3):
            part = rest.astype(BF).astype(F32)
            rest = rest - part
            values = jnp.where(place == first + 3 * number + piece, part, values)
    out_ref[...] = values.astype(BF)


def vectors_and_sums(pixels, vec_rows, first):
    return pl.pallas_call(
        functools.partial(sums_kernel, first),
        out_shape=jax.ShapeDtypeStruct(vec_rows.shape, BF),
        compiler_params=pltpu.CompilerParams(vmem_limit_bytes=20 * 2**20),
        cost_estimate=SMALL,
        name="vectors_and_sums",
    )(pixels, vec_rows)


def pick_kernel(spot_ref, source_ref, dy_ref, rows_ref, sums_ref, pieces_ref, total_ref):
    quarter = pl.program_id(0)

    @pl.when(quarter == 0)
    def _():
        sums_ref[...] = jnp.zeros_like(sums_ref)
        total_ref[...] = jnp.zeros_like(total_ref)

    count = dy_ref.shape[1]
    place = spot_ref[...] - quarter * QUART
    target = jnp.where((place >= 0) & (place < QUART), place * (count // QUART) + source_ref[...], -1)
    hot = (lax.broadcasted_iota(jnp.int32, (count, count), 1) == target).astype(F32)
    values = dy_ref[0]
    total_ref[...] += jnp.dot(hot.astype(BF), values, preferred_element_type=F32)
    vacant = 1.0 - jnp.sum(hot, axis=0, keepdims=True)
    weights = jnp.concatenate([jnp.ones_like(vacant), vacant, jnp.zeros((6, count), F32)], axis=0)
    sums_ref[...] += jnp.dot(weights.astype(BF), values, preferred_element_type=F32)

    @pl.when(quarter == pl.num_programs(0) - 1)
    def _():
        rows_ref[...] = total_ref[...].astype(BF)
        rest = sums_ref[1:2]
        pieces = []
        for _ in range(3):
            pieces.append(rest.astype(BF))
            rest = rest - pieces[-1].astype(F32)
        zeros = jnp.zeros((5, DDEC), BF)
        pieces_ref[...] = jnp.concatenate(pieces + [zeros], axis=0)


def pick_rows(visible_in, grids):
    images = visible_in.shape[0]
    count = images * QUART
    grids = grids[0].transpose(0, 2, 1, 3).reshape(4, count, DDEC)
    source = jnp.asarray(np.repeat(np.arange(images, dtype=np.int32), VIS)[:, None])
    column = pl.BlockSpec((count, 1), lambda i: (0, 0))
    small = pl.BlockSpec((8, DDEC), lambda i: (0, 0))
    return pl.pallas_call(
        pick_kernel,
        grid=(4,),
        in_specs=[column, column, pl.BlockSpec((1, count, DDEC), lambda i: (i, 0, 0))],
        out_specs=[pl.BlockSpec((count, DDEC), lambda i: (0, 0)), small, small],
        out_shape=[
            jax.ShapeDtypeStruct((count, DDEC), BF),
            jax.ShapeDtypeStruct((8, DDEC), F32),
            jax.ShapeDtypeStruct((8, DDEC), BF),
        ],
        scratch_shapes=[pltpu.VMEM((count, DDEC), F32)],
        compiler_params=pltpu.CompilerParams(vmem_limit_bytes=40 * 2**20),
        cost_estimate=SMALL,
        name="pick_rows",
    )(visible_in.reshape(count, 1), source, grids)


def place_kernel(scale_ref, spot_ref, rows_ref, table_ref, base_ref, out_ref):
    scale = scale_ref[pl.program_id(0)]
    spot = spot_ref[0]
    for quarter in range(4):
        place = lax.broadcasted_iota(jnp.int32, (QUART, VIS), 0) + quarter * QUART
        hot = (spot == place).astype(F32)
        vacant = jnp.sum(hot, axis=1, keepdims=True) < 0.5
        placed = jnp.dot(hot.astype(BF), rows_ref[0], preferred_element_type=F32)
        slot = lax.broadcasted_iota(jnp.int32, (QUART, 2 * NSCALE * SIDE), 1)
        place = lax.broadcasted_iota(jnp.int32, slot.shape, 0) + quarter * QUART
        line = lax.shift_right_logical(place * 1171, 14)
        row_at = scale * SIDE + line
        col_at = (NSCALE + scale) * SIDE + place - line * SIDE
        angle_at = ((slot == row_at) | (slot == col_at)).astype(F32).astype(BF)
        angle_at = jnp.concatenate([angle_at, angle_at], axis=1)
        empty = jnp.dot(angle_at, table_ref[...], preferred_element_type=F32) + base_ref[...]
        out_ref[0, quarter, 0] = jnp.where(vacant, empty, placed).astype(BF)


def place_rows(visible_in, scale_in, rows, table, base):
    images = visible_in.shape[0]
    return pl.pallas_call(
        place_kernel,
        grid_spec=pltpu.PrefetchScalarGridSpec(
            num_scalar_prefetch=1,
            grid=(images,),
            in_specs=[
                pl.BlockSpec((1, 1, VIS), lambda i, scale: (i, 0, 0)),
                pl.BlockSpec((1, VIS, DDEC), lambda i, scale: (i, 0, 0)),
                pl.BlockSpec(table.shape, lambda i, scale: (0, 0)),
                pl.BlockSpec((1, DDEC), lambda i, scale: (0, 0)),
            ],
            out_specs=pl.BlockSpec((1, 4, 1, QUART, DDEC), lambda i, scale: (0, 0, i, 0, 0)),
        ),
        out_shape=jax.ShapeDtypeStruct((1, 4, images, QUART, DDEC), BF),
        compiler_params=pltpu.CompilerParams(vmem_limit_bytes=20 * 2**20),
        cost_estimate=SMALL,
        name="place_rows",
    )(scale_in, visible_in[:, None, :], rows, table, base)


def local(
    pixels,
    visible,
    scale_index,
    cotangent,
    pe_weight,
    pe_first,
    pe_second,
    qkv_weight,
    qkv_first,
    qkv_second,
    out_weight,
    out_first,
    out_second,
    up_weight,
    up_first,
    up_second,
    down_weight,
    down_first,
    down_second,
    dec_weight,
    dec_first,
    dec_second,
    vectors,
    vec_first,
    vec_second,
):
    image_count = pixels.shape[0]
    row_count = image_count * VIS
    device_count = lax.axis_size(AXES)
    dp_count = lax.axis_size("dp")
    shard_rows = D // device_count
    routed = dp_count == 16 and device_count == 32
    item_count = 4 * image_count // dp_count
    whole_images = item_count == 4

    order = Order(vec_first)
    dp_index = lax.axis_index("dp")
    vec_length = vectors.shape[0]
    if whole_images:
        marks = jnp.concatenate([visible, scale_index[:, None]], axis=1)
        marks_in = lax.all_to_all(marks, "dp", split_axis=0, concat_axis=0, tiled=True)
    pe_rows = pe_weight.T.astype(BF)
    middle_rows = jnp.concatenate([out_weight.T, up_weight, dec_weight], axis=1).astype(BF)
    if routed:
        qkv_gather = Gathering(qkv_weight.astype(BF), False, order)
        middle_gather = Gathering(middle_rows, False, order)
        owners = block_order()
        vec_low = jnp.pad(vectors.astype(BF).astype(F32), (0, shard_rows * SPAN - vec_length))
        vec_low = vec_low.reshape(shard_rows, SPAN)
        table = order(angle_pieces(D, 3)).reshape(-1, 32, shard_rows)
        table = jnp.einsum("pb,kbr->kpr", owners, table, preferred_element_type=F32).astype(BF)
        table, pixel_flat = order(table.reshape(-1, D), pixels.reshape(row_count, PIX))
        vec_low = vectors_and_sums(order(pixels), vec_low, vec_length)
        pe_gather = Gathering(jnp.concatenate([pe_rows, vec_low], axis=1), True, order)
        qkv_gather.middle()
        middle_gather.middle()
    else:
        pixel_rows = pixels.astype(F32).reshape(row_count, BANDS, PATCH * PATCH)
        band_sum = jnp.sum(pixel_rows, axis=(0, 2))
        band_square = jnp.sum(pixel_rows * pixel_rows, axis=(0, 2))
        stats = lax.psum(jnp.concatenate([band_sum, band_square]), AXES)
    down_rows = order(down_weight).T.astype(BF)
    if routed:
        pe_gather.first_turn()
        down_gather = Gathering(down_rows, False, order)

    cotangent_rows = order(cotangent)
    if whole_images:
        marks_in = order(marks_in)
        visible_in, scale_in = marks_in[:, :VIS], marks_in[:, VIS]
        dy_sent, dy_sums, vacant_low = order(*pick_rows(visible_in, cotangent_rows))
        dec_bias_grad, dy_vacant = dy_sums[0], dy_sums[1]
        dy_sent = dy_sent.reshape(image_count, VIS, DDEC)
        dy_rows = lax.all_to_all(dy_sent, "dp", split_axis=0, concat_axis=0, tiled=True)
    if routed:
        pe_gather.second_turn()
        qkv_gather.first_turn()
    spots, scale_rows = order(visible.reshape(row_count), jnp.repeat(scale_index, VIS))
    if routed:
        pe_gather.cores()
    else:
        table, pixel_flat = angle_pieces(D, 3), pixels.reshape(row_count, PIX)
    hot = angle_hot(spots, scale_rows, 3)
    enc_table = order(*[forward_product(hot, part) for part in halves(table)])
    if routed:
        pe_pair = pe_gather.total()
        vector_all = jnp.concatenate([part[:, PIX:] for part in pe_pair])
        vector_all = vector_all.reshape(device_count, shard_rows, SPAN)[:, :4].reshape(device_count, -1)
        vector_all = jnp.einsum("pb,pv->bv", owners, vector_all, preferred_element_type=F32)
        stats = vector_all[:, vec_length : vec_length + 6 * BANDS].reshape(-1, 2 * BANDS, 3)
        stats = jnp.sum(stats, axis=(0, 2))
        vector_all = vector_all[:, :vec_length].reshape(-1)
    else:
        early = jnp.concatenate([pe_rows, qkv_weight.astype(BF)], axis=1)
        early_full = lax.all_gather(early, AXES, axis=0, tiled=True)
        middle_full = lax.all_gather(middle_rows, AXES, axis=0, tiled=True)
        down_full = lax.all_gather(down_rows, AXES, axis=0, tiled=True)
        vector_all = lax.all_gather(vectors.astype(BF), AXES, axis=0, tiled=True).astype(F32)
        pe_pair = (early_full[:HALF, :PIX], early_full[HALF:, :PIX])
        qkv_pair = (early_full[:HALF, PIX:], early_full[HALF:, PIX:])
        middle_pair = (middle_full[:HALF], middle_full[HALF:])
        down_pair = (down_full[:HALF], down_full[HALF:])

    entry_count = row_count * device_count * PATCH * PATCH
    band_mean = stats[:BANDS] / entry_count
    band_scale = lax.rsqrt(stats[BANDS:] / entry_count - band_mean * band_mean + EPS_NORM)
    scale_row = jnp.repeat(band_scale, PATCH * PATCH)[None]
    pixel_norm = pixel_flat.astype(F32) - jnp.repeat(band_mean, PATCH * PATCH)[None]
    pixel_low = order((pixel_norm * scale_row).astype(BF))
    pieces, up_bias, dec_bias = split_vectors(vector_all)
    query_bias, value_bias = pieces[5], pieces[6]
    wide = jnp.stack(pieces[:5] + pieces[7:])
    if routed:
        wide = wide.astype(BF).reshape(8, 32, shard_rows)
        wide = jnp.einsum("pb,nbr->npr", owners, wide, preferred_element_type=F32).reshape(8, D)
    gain_one, shift_one, gain_two, shift_two, pe_bias, out_bias, down_bias, mask_token = [
        halves(wide[number]) for number in range(8)
    ]

    stream_in = outward(pixel_low, pe_pair, 0, PIX)
    stream_in = [part + bias + angle for part, bias, angle in zip(stream_in, pe_bias, enc_table)]
    norm_one, normed_one, inv_std_one = norm_forward(stream_in, gain_one, shift_one)
    norm_one = order(*norm_one)
    if routed:
        middle_gather.first_turn()
        down_gather.middle()
        qkv_gather.second_turn()
    if whole_images:
        dy_rows = order(dy_rows).reshape(row_count, DDEC)
    if routed:
        down_gather.grow()
        middle_gather.second_turn()
        qkv_gather.cores()
        qkv_pair = qkv_gather.total()
    norm_one = order(*norm_one)
    low_rows = jax.ShapeDtypeStruct((row_count, 3 * D), BF)
    qkv_bias = jnp.concatenate([query_bias, jnp.zeros_like(query_bias), value_bias])
    (projected,) = inward_call(
        shift_kernel, norm_one, qkv_pair, 0, 3 * D, qkv_bias.reshape(1, 3 * D), [low_rows]
    )
    projected = order(projected)
    mixture_low, peaks = order(*attend(projected))
    if routed:
        down_gather.near = [lax.ppermute(order(down_gather.held), AXES, turn_pairs(2, 1))]
        middle_gather.cores()
        middle_pair = middle_gather.total()
    mixture_low = order(mixture_low)
    UP, DEC = D, D + FF
    stream_mid = outward(mixture_low, middle_pair, 0, D)
    stream_mid = [part + more + bias for part, more, bias in zip(stream_in, stream_mid, out_bias)]
    norm_two, normed_two, inv_std_two = norm_forward(stream_mid, gain_two, shift_two)

    if whole_images:
        out_low = [part.astype(BF) for part in outward(dy_rows, middle_pair, DEC, DDEC)]
    else:
        placement = visible[:, :, None] == jnp.arange(GRID)[None, None, :]
        placement_low = placement.astype(BF)
        vacant = 1.0 - jnp.sum(placement.astype(F32), axis=1)
        grad_rows = cotangent_rows[0].reshape(-1, DDEC)
        dec_bias_grad = jnp.sum(grad_rows.astype(F32), axis=0)
        grid_grad = jnp.concatenate(outward(grad_rows, middle_pair, DEC, DDEC), axis=1)
        grid_grad = grid_grad.astype(BF).reshape(item_count, dp_count, QUART, D)
        returned = lax.all_to_all(
            grid_grad, "dp", split_axis=1, concat_axis=0, tiled=True
        ).reshape(image_count, GRID, D)
        out_low = jnp.einsum(
            "nvg,ngd->nvd", placement_low, returned, preferred_element_type=F32
        )
        out_low = halves(out_low.reshape(row_count, D).astype(BF))
        mask_grad = halves(
            jnp.einsum("ng,ngd->d", vacant.astype(BF), returned, preferred_element_type=F32)
        )
    out_grad_rows = [part.astype(F32) for part in out_low]

    out_low = order(*out_low)
    norm_two = order(*norm_two)
    if routed:
        down_gather.second_turn()
    activated, slope = order(*expand(norm_two, middle_pair, UP, up_bias))
    if routed:
        down_gather.cores()
        down_pair = down_gather.total()
    down_part = Reduction(product_of(order, (out_low, activated)), routed, order)
    down_part.cores()
    out_low = order(*out_low)
    hidden = jax.ShapeDtypeStruct((row_count, FF), BF)
    preact_low, up_bias_grad = order(
        *inward_call(
            slope_kernel,
            out_low,
            down_pair,
            0,
            FF,
            slope,
            [hidden, jax.ShapeDtypeStruct((1, FF), F32)],
        )
    )
    up_bias_grad = up_bias_grad[0]
    down_part.first_turn()
    activated = order(activated)
    stream_out = outward(activated, down_pair, 0, FF)
    stream_low = order(
        *[
            (part + more + bias).astype(BF)
            for part, more, bias in zip(stream_mid, stream_out, down_bias)
        ]
    )

    if not whole_images:
        full_grid = jnp.einsum(
            "nvg,nvd->ngd",
            placement_low,
            jnp.concatenate(stream_low, axis=1).reshape(image_count, VIS, D),
            preferred_element_type=F32,
        )
        full_grid = full_grid + vacant[:, :, None] * jnp.concatenate(mask_token)
        quarters = full_grid.astype(BF).reshape(4 * image_count, 1, QUART, D)
        ratio_image = jnp.power(2.0, scale_index.astype(F32) - 1.0)
        ratio_quarter = jnp.repeat(ratio_image, 4).reshape(4 * image_count, 1).astype(BF)
        received = lax.all_to_all(quarters, "dp", split_axis=0, concat_axis=1, tiled=True)
        received_ratio = lax.all_to_all(
            ratio_quarter, "dp", split_axis=0, concat_axis=1, tiled=True
        )
        quarter_id = dp_index * item_count + jnp.arange(item_count)
        position = (quarter_id % 4)[:, None] * QUART + jnp.arange(QUART)[None, :]
        scale_at = jnp.round(jnp.log2(received_ratio.astype(F32))).astype(jnp.int32) + 1
        full = (item_count, dp_count, QUART)
        dec_table = forward_product(
            angle_hot(
                jnp.broadcast_to(position[:, None, :], full).reshape(-1),
                jnp.broadcast_to(scale_at[:, :, None], full).reshape(-1),
                2,
            ),
            angle_pieces(DDEC, 2),
        )
        received = halves(received.reshape(-1, D))
        decoded = inward(received, middle_pair, DEC, DDEC) + dec_bias + dec_table
        decoded = decoded.astype(BF).reshape((1,) + full + (DDEC,))

    down_bias_grad = [jnp.sum(part, axis=0) for part in out_grad_rows]
    up_part = Reduction(product_of(order, (norm_two, preact_low)), routed, order)
    up_part.cores()
    down_part.second_turn()
    two_grad = outward(order(preact_low), middle_pair, UP, FF)
    mid_grad, gain_two_grad, shift_two_grad = norm_backward(
        two_grad, normed_two, inv_std_two, gain_two
    )
    mid_grad = [part + more for part, more in zip(mid_grad, out_grad_rows)]
    out_bias_grad = [jnp.sum(part, axis=0) for part in mid_grad]
    mid_low = order(*[part.astype(BF) for part in mid_grad])
    up_part.first_turn()
    down_part.along_z()
    mid_low = order(*mid_low)
    mixture_grad = order(inward(mid_low, middle_pair, 0, D).astype(BF))
    projected_low, attend_sums = order(*attend_back(projected, mixture_grad, peaks))
    query_bias_grad, value_bias_grad = attend_sums[0], attend_sums[1]
    down_shard = down_part.total()
    up_part.second_turn()
    qkv_part = Reduction(
        product_of(order, (mid_low, mixture_low), (norm_one, projected_low)), routed, order
    )
    qkv_part.cores()
    one_grad = outward(order(projected_low), qkv_pair, 0, 3 * D)
    in_grad, gain_one_grad, shift_one_grad = norm_backward(
        one_grad, normed_one, inv_std_one, gain_one
    )
    in_grad = [part + more for part, more in zip(in_grad, mid_grad)]
    pe_bias_grad = [jnp.sum(part, axis=0) for part in in_grad]
    in_low = order(*[part.astype(BF) for part in in_grad])
    qkv_part.first_turn()
    up_part.along_z()
    if whole_images:
        mask_grad = [
            jnp.sum(part, axis=0) for part in outward(order(vacant_low), middle_pair, DEC, DDEC)
        ]
    wide_grad = jnp.stack(
        [
            jnp.concatenate(pair)
            for pair in (
                gain_one_grad,
                shift_one_grad,
                gain_two_grad,
                shift_two_grad,
                pe_bias_grad,
                out_bias_grad,
                down_bias_grad,
                mask_grad,
            )
        ]
    )
    if routed:
        wide_grad = wide_grad.astype(BF).reshape(8, 32, shard_rows)
        wide_grad = jnp.einsum("pb,npr->nbr", owners, wide_grad, preferred_element_type=F32)
        wide_grad = wide_grad.reshape(8, D)
    vec_grad = jnp.concatenate(
        [
            wide_grad[:5].reshape(-1),
            query_bias_grad,
            value_bias_grad,
            wide_grad[5:].reshape(-1),
            up_bias_grad,
            dec_bias_grad,
        ]
    )
    if routed:
        vec_rows = jnp.pad(
            vec_grad.reshape(device_count, vec_length), ((0, 0), (0, 4 * SPAN - vec_length))
        )
        vec_rows = jnp.einsum("pb,bv->pv", owners, vec_rows.astype(BF), preferred_element_type=F32)
        vec_rows = vec_rows.reshape(device_count, 4, SPAN)
        vec_rows = jnp.pad(vec_rows, ((0, 0), (0, shard_rows - 4), (0, 0))).reshape(2, HALF, SPAN)

        def last_product(half, came):
            left, stream = order(in_low[half], stream_low[half])
            token = mask_token[half].reshape(HALF, 1)
            operands = (left, pixel_low, vec_rows[half], stream, dy_rows, token, dy_vacant[None])
            return last_call(operands, came)

    else:

        def last_product(half, came):
            return jnp.concatenate(
                [
                    weight_product(in_low[half], pixel_low),
                    weight_product(received[half], grad_rows),
                ],
                axis=1,
            ).astype(BF)

    pe_part = Reduction(last_product, routed, order)
    pe_part.cores()
    (norm_grad,) = inward_call(
        scale_kernel,
        order(*in_low),
        pe_pair,
        0,
        PIX,
        scale_row,
        [jax.ShapeDtypeStruct((row_count, PIX), F32)],
        256,
    )
    norm_grad = order(norm_grad)
    pe_part.first_turn()
    qkv_part.join(pe_part)
    qkv_part.second_turn()
    if whole_images:
        dec_pieces = angle_pieces(DDEC, 2)
        vis_table = forward_product(angle_hot(spots, scale_rows, 2), dec_pieces)
        vis_rows = inward(order(*stream_low), middle_pair, DEC, DDEC) + dec_bias + vis_table
        vis_rows = order(vis_rows.astype(BF).reshape(image_count, VIS, DDEC))
        vis_in = lax.all_to_all(vis_rows, "dp", split_axis=0, concat_axis=0, tiled=True)
        tokens = [jnp.broadcast_to(part.astype(BF), (8, HALF)) for part in mask_token]
        mask_rows = inward(tokens, middle_pair, DEC, DDEC)[:1] + dec_bias
    up_shard = up_part.total()
    qkv_part.along_z()
    pixel_grad = order(norm_grad).reshape(image_count, VIS, PIX)
    if whole_images:
        decoded = order(place_rows(visible_in, scale_in, order(vis_in), dec_pieces, mask_rows))
    last_total = qkv_part.total()
    out_shard, qkv_shard = last_total[:, :D], last_total[:, D : 4 * D]
    pe_shard, dec_shard = last_total[:, 4 * D : 4 * D + PIX], last_total[:, -DDEC:]
    if routed:
        vec_shard = last_total[:4, 4 * D + PIX : 4 * D + PIX + SPAN].reshape(-1)[:vec_length]
    else:
        vec_shard = lax.psum_scatter(vec_grad, AXES, scatter_dimension=0, tiled=True)
    shards = (pe_shard, qkv_shard, out_shard, up_shard, down_shard, dec_shard, vec_shard)
    parts = (last_total, up_shard, down_shard) if routed else shards
    local_squares = sum((jnp.sum(gradient * gradient) for gradient in parts))
    squares = tiny_sum(local_squares.reshape(1), routed)[0]
    grad_norm = jnp.sqrt(squares)
    vec_first = order.token
    clip_factor = jnp.minimum(1.0, CLIP_LEVEL / grad_norm)
    params = (pe_weight, qkv_weight, out_weight, up_weight, down_weight, dec_weight, vectors)
    firsts = (pe_first, qkv_first, out_first, up_first, down_first, dec_first, vec_first)
    seconds = (pe_second, qkv_second, out_second, up_second, down_second, dec_second, vec_second)
    results = []
    for number in range(7):
        step_rate = LR_VECTOR if number == 6 else LR_MATRIX
        decay_rate = 0.0 if number == 6 else DECAY_MATRIX
        gradient = shards[number].T if number in (0, 2, 4) else shards[number]
        results.extend(
            adamw_update(
                params[number],
                firsts[number],
                seconds[number],
                gradient * clip_factor,
                step_rate,
                decay_rate,
            )
        )
    return (decoded, pixel_grad, *results, grad_norm)


def solution(mesh):
    rows = P(AXES, None)
    cols = P(None, AXES)
    vecs = P(AXES)
    images = P(AXES, None, None)
    grids = P("grp", "dp", None, None, None)
    states = (cols,) * 3 + (rows,) * 3 + (cols,) * 3 + (rows,) * 3 + (cols,) * 3 + (rows,) * 3
    states = states + (vecs,) * 3
    return jax.shard_map(
        local,
        mesh=mesh,
        in_specs=(images, rows, vecs, grids) + states,
        out_specs=(grids, images) + states + (P(),),
        check_vma=False,
    )
```
